32 devices in a mesh: section: 2 (over y), dp: 16 (over z, x, core).
Axes of the slice: x: 2, y: 2, z: 4, core: 2. Of those that a mesh axis runs over, the one named last changes fastest.
Arguments:
- queries: bfloat16 [2, 2048, 2560], P('section', 'dp')
- key_cells: bfloat16 [2, 2048, 2560], P('section', 'dp')
- value_cells: bfloat16 [2, 2048, 2560], P('section', 'dp'), may hold values from -6 to 6
- grad_cells: bfloat16 [2, 2048, 2560], P('section', 'dp'), may hold values from -6 to 6
- packing: int32 [2, 16, 128], P('section', 'dp'), may hold values from 0 to 127, each once within a row
- segment_ids: int32 [2, 2048], P('section'), may hold values from 0 to 127, never falling along the last dimension, each value on 1 to 32 neighbouring positions
Outputs:
- input_grads: bfloat16 [2, 2048, 7680], P('section', 'dp')
The draws below stay inside these ranges and needn't reach their ends.
Inputs may be any that keep to these rules, and one draw needn't show every extreme that they name: `packing`: each row of a section and device is a permutation of 0 to 127. `segment_ids`: along a section's packed cells the ids never fall; each segment has 1 to 32 cells and one has exactly 32.
All inputs are finite; a program needn't handle non-finite values.
Results may differ from the reference program's by a relative error of at most 0.0086.
Values may be sent and summed in bfloat16 or wider, within the bound.
A program may use at most 64 MiB of HBM per device.

```python
import math
import jax
import jax.numpy as jnp
import numpy as np
from jax import lax

HEADS = 20
HEAD_DIM = 128
ROWS = 128
FEAT = 2560
SECTIONS = 2
TOKENS = 2048
PER_PEER = 8
REACH = 32
SEGS = 128
N_DP = 16


def draw_queries(key, part):
    noise = jax.random.normal(jax.random.fold_in(key, 1), (SECTIONS, TOKENS, FEAT), jnp.float32)
    values = jnp.clip(noise, -6.0, 6.0)
    return values.astype(jnp.bfloat16)


def draw_key_cells(key, part):
    noise = jax.random.normal(jax.random.fold_in(key, 2), (SECTIONS, TOKENS, FEAT), jnp.float32)
    values = jnp.clip(noise, -6.0, 6.0)
    return values.astype(jnp.bfloat16)


def level_of(stream_key, shape, cuts, low, high):
    loudness, own = 1.0, jax.random.fold_in(stream_key, 6)
    for dim, parts in cuts:
        draws = jnp.exp(jax.random.uniform(jax.random.fold_in(own, dim), (parts,), jnp.float32, low / len(cuts), high / len(cuts)))
        loudness = loudness * jnp.repeat(draws, shape[dim] // parts).reshape([-1 if axis == dim else 1 for axis in range(len(shape))])
    return loudness


def length_profile(amount, total, reach, slope):
    weights = [(1 << 20) // math.isqrt(grade ** slope) + 1 for grade in range(2, amount + 1)]
    surplus, given = total - reach - (amount - 1), [1] * (amount - 1)
    while surplus > 0:
        free = [i for i in range(amount - 1) if given[i] < reach]
        whole, remaining = sum([weights[i] for i in free]), surplus
        for i in free:
            extra = min(reach - given[i], max(1, remaining * weights[i] // whole), surplus)
            given[i] = given[i] + extra
            surplus = surplus - extra
    return np.array([reach] + given)


def uneven_parts(own_key, amount, total, limit, skew):
    if amount == 2:
        one = jax.random.randint(own_key, (), max(1, total - limit), min(limit, total - 1) + 1)
        return jnp.stack([one, total - one])
    lengths = jnp.asarray(length_profile(amount, total, limit, skew), jnp.int32)
    twos = (amount - 1) // 2
    giver, sink = lengths[1:1 + 2 * twos:2], lengths[2:2 + 2 * twos:2]
    slack = jnp.minimum(giver - 1, limit - sink)
    passed = jax.random.randint(jax.random.fold_in(own_key, 1), (twos,), 0, 1 << 20) % (slack + 1)
    lengths = lengths.at[1:1 + 2 * twos:2].set(giver - passed).at[2:2 + 2 * twos:2].set(sink + passed)
    return lengths[jax.random.permutation(jax.random.fold_in(own_key, 2), amount)]


def bell_draw(own_key, extent, scale, limit, cuts=(), kind=jnp.bfloat16):
    entries = jax.random.normal(own_key, extent, jnp.float32) * scale
    if len(cuts) > 0:
        entries = level_of(own_key, extent, cuts, -0.22, 0.18) * entries
    return jnp.clip(entries, min=-limit, max=limit).astype(kind)


def setup_inputs(seed: int = 0) -> dict:
    arg_keys = jax.random.split(jax.random.key(seed), 7)
    queries = draw_queries(jax.random.fold_in(arg_keys[6], 71), 0)
    key_cells = draw_key_cells(jax.random.fold_in(arg_keys[6], 71), 0)
    value_cells = bell_draw(arg_keys[2], (SECTIONS, TOKENS, FEAT), 1.0, 6.0, ((0, 2), (1, 16)))
    grad_cells = bell_draw(arg_keys[3], (SECTIONS, TOKENS, FEAT), 1.0, 6.0, ((0, 2), (1, 16)))
    packing = jax.vmap(lambda own: jax.random.permutation(own, ROWS))(jax.random.split(arg_keys[4], SECTIONS * N_DP)).reshape((SECTIONS, N_DP, ROWS)).astype(jnp.int32)
    segment_ids = jax.vmap(lambda own: jnp.searchsorted(jnp.cumsum(uneven_parts(own, SEGS, TOKENS, REACH, 2)), jnp.arange(TOKENS), side="right"))(jax.random.split(arg_keys[5], SECTIONS)).reshape((SECTIONS, TOKENS)).astype(jnp.int32)
    return dict(queries=queries, key_cells=key_cells, value_cells=value_cells, grad_cells=grad_cells, packing=packing, segment_ids=segment_ids)


def split_heads(matrix):
    return matrix.astype(jnp.float32).reshape(matrix.shape[0], HEADS, HEAD_DIM)


def block_grads(query_block, key_window, value_window, grad_block, query_ids, key_ids):
    scale = HEAD_DIM ** -0.5
    query_heads = split_heads(query_block)
    key_heads = split_heads(key_window)
    value_heads = split_heads(value_window)
    grad_heads = split_heads(grad_block)
    scores = jnp.einsum('ihd,jhd->hij', query_heads, key_heads) * scale
    allowed = (query_ids[:, None] == key_ids[None, :])[None]
    scores = jnp.where(allowed, scores, -jnp.inf)
    top = jnp.max(scores, axis=2)
    log_total = top + jnp.log(jnp.sum(jnp.exp(scores - top[:, :, None]), axis=2))
    probs = jnp.exp(scores - log_total[:, :, None])
    probs_low = lax.optimization_barrier(probs.astype(jnp.bfloat16)).astype(jnp.float32)
    attended = jnp.einsum('hij,jhd->ihd', probs_low, value_heads)
    delta = jnp.sum(grad_heads * attended, axis=2).T
    dprobs = jnp.einsum('ihd,jhd->hij', grad_heads, value_heads)
    dscores = (probs * (dprobs - delta[:, :, None]) * scale).astype(jnp.bfloat16)
    dscores = lax.optimization_barrier(dscores).astype(jnp.float32)
    grad_query = jnp.einsum('hij,jhd->ihd', dscores, key_heads).reshape(query_block.shape[0], FEAT)
    grad_key = jnp.einsum('hij,ihd->jhd', dscores, query_heads).reshape(key_window.shape[0], FEAT)
    grad_value = jnp.einsum('hij,ihd->jhd', probs_low, grad_heads).reshape(key_window.shape[0], FEAT)
    return grad_query.astype(jnp.bfloat16), jnp.concatenate([grad_key, grad_value], axis=1)


def section_grads(queries, key_cells, value_cells, grad_cells, packing, segment_ids):
    cells = jnp.arange(TOKENS, dtype=jnp.int32)
    block_of = cells // ROWS
    source = (cells % ROWS) // PER_PEER
    slot = cells % PER_PEER
    anchor = (source * ROWS + packing[source, block_of * PER_PEER + slot]).astype(jnp.int32)
    packed_q = queries[anchor]
    packed_g = grad_cells[anchor]
    edge = jnp.zeros((REACH, FEAT), jnp.bfloat16)
    padded_k = jnp.concatenate([edge, key_cells[anchor], edge], axis=0)
    padded_v = jnp.concatenate([edge, value_cells[anchor], edge], axis=0)
    rim_ids = jnp.full((REACH,), -1, jnp.int32)
    padded_ids = jnp.concatenate([rim_ids, segment_ids.astype(jnp.int32), rim_ids])
    window = ROWS + 2 * REACH

    def step(totals, block):
        start = (block * ROWS).astype(jnp.int32)
        query_block = lax.dynamic_slice_in_dim(packed_q, start, ROWS)
        grad_block = lax.dynamic_slice_in_dim(packed_g, start, ROWS)
        key_window = lax.dynamic_slice_in_dim(padded_k, start, window)
        value_window = lax.dynamic_slice_in_dim(padded_v, start, window)
        key_ids = lax.dynamic_slice_in_dim(padded_ids, start, window)
        query_ids = lax.dynamic_slice_in_dim(padded_ids, start + REACH, ROWS)
        grad_query, partial_value = block_grads(query_block, key_window, value_window, grad_block, query_ids, key_ids)
        before = lax.dynamic_slice_in_dim(totals, start, window)
        totals = lax.dynamic_update_slice_in_dim(totals, before + partial_value, start, 0)
        return totals, grad_query

    start_totals = jnp.zeros((TOKENS + 2 * REACH, 2 * FEAT), jnp.float32)
    totals, query_grads = lax.scan(step, start_totals, jnp.arange(N_DP, dtype=jnp.int32))
    key_value = totals[REACH:REACH + TOKENS].astype(jnp.bfloat16)
    packed_grads = jnp.concatenate([query_grads.reshape(TOKENS, FEAT), key_value], axis=1)
    return jnp.zeros_like(packed_grads).at[anchor].set(packed_grads)


def reference(queries, key_cells, value_cells, grad_cells, packing, segment_ids):
    grads = lax.map(lambda items: section_grads(*items), (queries, key_cells, value_cells, grad_cells, packing, segment_ids))
    return jnp.roll(grads, -1, axis=0)
```

```python
import functools
import jax
import jax.numpy as jnp
from jax import lax
from jax.sharding import PartitionSpec as P
from jax.experimental import pallas as pl
from jax.experimental.pallas import tpu as pltpu

HEADS = 20
HEAD_DIM = 128
CHUNK = 512
MESH = pl.DeviceIdType.MESH
NEG = -1e30
PIECES = ((0, 32, 0), (32, 16, 1), (48, 32, 2), (80, 16, 3))


def with_halo(value, sides, width):
    for axis, dim in sides:
        size, length = (lax.axis_size(axis), value.shape[dim])
        up = [(i, (i + 1) % size) for i in range(size - 1)]
        down = [(j, i) for i, j in up]
        last = lax.slice_in_dim(value, length - width, length, axis=dim)
        initial = lax.slice_in_dim(value, 0, width, axis=dim)
        before = lax.ppermute(last, axis, up)
        after = lax.ppermute(initial, axis, down)
        value = jnp.concatenate([before, value, after], axis=dim)
    return value


def passed_along(value, axis, steps):
    count = lax.axis_size(axis)
    initial, last = (max(0, -steps), min(count, count - steps))
    return lax.ppermute(value, axis, [(source, source + steps) for source in range(initial, last)])


def from_behind(block, axis, distance):
    devices = range(lax.axis_size(axis))
    route = [((i - distance) % len(devices), i) for i in devices]
    return lax.ppermute(block, axis, route)


def heads_of(matrix):
    return matrix.reshape(matrix.shape[0], HEADS, HEAD_DIM)


def masked_scores(query_rows, key_rows, query_ids, key_ids):
    scores = jnp.einsum(
        "ihd,jhd->hij", heads_of(query_rows), heads_of(key_rows), preferred_element_type=jnp.float32
    )
    scores = scores * HEAD_DIM ** (-0.5)
    allowed = (query_ids[:, None] == key_ids[None, :])[None]
    return jnp.where(allowed, scores, -jnp.inf)


def body(queries, key_cells, value_cells, grad_cells, packing, segment_ids):
    cell_count = queries.shape[1]
    width = queries.shape[2]
    groups = lax.axis_size("dp")
    per_peer = cell_count // groups
    reach = cell_count // 4
    place = lax.axis_index("dp")
    scale = HEAD_DIM ** (-0.5)
    order = packing[0, 0]

    def pack(matrix):
        return matrix[0][order].reshape(groups, per_peer, width)

    arrived = (
        lax.all_to_all(pack(queries), "dp", split_axis=0, concat_axis=0, tiled=True),
        lax.all_to_all(pack(key_cells), "dp", split_axis=0, concat_axis=0, tiled=True),
        lax.all_to_all(pack(value_cells), "dp", split_axis=0, concat_axis=0, tiled=True),
        lax.all_to_all(pack(grad_cells), "dp", split_axis=0, concat_axis=0, tiled=True),
    )
    own_q, own_k, own_v, own_g = [piece.reshape(cell_count, width) for piece in arrived]
    rim_ids = jnp.full((reach,), -1, jnp.int32)
    padded_ids = jnp.concatenate([rim_ids, segment_ids[0], rim_ids])
    window_ids = lax.dynamic_slice_in_dim(padded_ids, place * cell_count, cell_count + 2 * reach)
    own_ids = window_ids[reach : reach + cell_count]
    key_value = jnp.concatenate([own_k, own_v], axis=1)
    key_value_window = with_halo(key_value, (("dp", 0),), reach)
    key_window = key_value_window[:, :width]
    value_window = key_value_window[:, width:]
    scores = masked_scores(own_q, key_window, own_ids, window_ids)
    top = jnp.max(scores, axis=2)
    log_total = top + jnp.log(jnp.sum(jnp.exp(scores - top[:, :, None]), axis=2))
    probs = jnp.exp(scores - log_total[:, :, None])
    probs_low = probs.astype(jnp.bfloat16)
    grad_heads = heads_of(own_g)
    attended = jnp.einsum(
        "hij,jhd->ihd", probs_low, heads_of(value_window), preferred_element_type=jnp.float32
    )
    delta = jnp.sum(grad_heads.astype(jnp.float32) * attended, axis=2).T
    dprobs = jnp.einsum(
        "ihd,jhd->hij", grad_heads, heads_of(value_window), preferred_element_type=jnp.float32
    )
    dscores = (probs * (dprobs - delta[:, :, None]) * scale).astype(jnp.bfloat16)
    grad_query = jnp.einsum(
        "hij,jhd->ihd", dscores, heads_of(key_window), preferred_element_type=jnp.float32
    )
    grad_query = grad_query.reshape(cell_count, width).astype(jnp.bfloat16)
    window = cell_count + 2 * reach
    grad_key = jnp.einsum(
        "hij,ihd->jhd", dscores, heads_of(own_q), preferred_element_type=jnp.float32
    )
    grad_value = jnp.einsum(
        "hij,ihd->jhd", probs_low, grad_heads, preferred_element_type=jnp.float32
    )
    partial_value = jnp.concatenate(
        [grad_key.reshape(window, width), grad_value.reshape(window, width)], axis=1
    )
    from_after = passed_along(partial_value[:reach].astype(jnp.bfloat16), "dp", -1).astype(
        jnp.float32
    )
    from_before = passed_along(
        partial_value[reach + cell_count :].astype(jnp.bfloat16), "dp", 1
    ).astype(jnp.float32)
    summed = partial_value[reach : reach + cell_count]
    summed = summed.at[cell_count - reach :].add(from_after)
    summed = summed.at[:reach].add(from_before)
    packed_grads = jnp.concatenate([grad_query, summed.astype(jnp.bfloat16)], axis=1)
    returned = lax.all_to_all(
        packed_grads.reshape(groups, per_peer, 3 * width),
        "dp",
        split_axis=0,
        concat_axis=0,
        tiled=True,
    )
    returned = returned.reshape(cell_count, 3 * width)
    inverse = (
        jnp.zeros((cell_count,), jnp.int32).at[order].set(jnp.arange(cell_count, dtype=jnp.int32))
    )
    loaded_order = returned[inverse]
    handed = from_behind(loaded_order, "section", -1)
    return handed[None]


def dot_nt(a, b):
    return lax.dot_general(a, b, (((1,), (1,)), ((), ())), preferred_element_type=jnp.float32)


def dot_tn(a, b):
    return lax.dot_general(a, b, (((0,), (0,)), ((), ())), preferred_element_type=jnp.float32)


def dot_nn(a, b):
    return jnp.dot(a, b, preferred_element_type=jnp.float32)


def kernel(
    group, planes, sections, chunks, width,
    q_ref, k_ref, v_ref, g_ref, pack_ref, unpack_ref, pick_ref, place_ref, idc_ref, idr_ref,
    out_ref,
    packed, win, halo, back_out, back_in, fin_out, fin_in, unpack_in, bias,
    a2a_s, a2a_r, halo_s, halo_r, back_s, back_r, fin_s, fin_r, un_s, un_r,
):
    t = lax.axis_index("section")
    me = lax.axis_index("dp")
    z, j = lax.div(me, group), lax.rem(me, group)
    rows = 128 // group
    before = lax.rem(t + sections - 1, sections)
    after = lax.rem(t + 1, sections)
    zr, zl = lax.rem(z + 1, planes), lax.rem(z + planes - 1, planes)
    jr = lax.rem(j + jnp.where(z == planes - 1, 1, 0), group)
    jl = lax.rem(j + group - jnp.where(z == 0, 1, 0), group)
    sides = (zr * group + j, zr * group + jr, zl * group + j, zl * group + jl)
    mates = [lax.rem(j + o, group) for o in range(group)]
    sources = [lax.rem(j + group - o, group) for o in range(group)]

    barrier = pltpu.get_barrier_semaphore()
    for o in range(1, group):
        pl.semaphore_signal(barrier, inc=1, device_id=(t, z * group + mates[o]), device_id_type=MESH)
    for side in sides:
        pl.semaphore_signal(barrier, inc=1, device_id=(t, side), device_id_type=MESH)
    for o in range(group):
        pl.semaphore_signal(barrier, inc=1, device_id=(after, z * group + mates[o]), device_id_type=MESH)
    pl.semaphore_wait(barrier, 2 * group + 3)

    def at_rows(ref, c, start, count):
        if not isinstance(start, int):
            start = pl.multiple_of(start, 16)
        return ref.at[c, :, pl.ds(start, count), :]

    def a2a(c, o, landing):
        return pltpu.make_async_remote_copy(
            src_ref=at_rows(packed, c, mates[o] * rows, rows),
            dst_ref=at_rows(win, c, landing * rows, rows),
            send_sem=a2a_s.at[c, o - 1],
            recv_sem=a2a_r.at[c, o - 1],
            device_id=(t, z * group + mates[o]),
            device_id_type=MESH,
        )

    def outward(c, n):
        first, count, side = PIECES[n]
        return pltpu.make_async_remote_copy(
            src_ref=at_rows(halo, c, first, count),
            dst_ref=at_rows(win, c, 128 + first, count),
            send_sem=halo_s.at[c, n],
            recv_sem=halo_r.at[c, n],
            device_id=(t, sides[side]),
            device_id_type=MESH,
        )

    def homeward(c, n):
        first, count, side = PIECES[n]
        return pltpu.make_async_remote_copy(
            src_ref=at_rows(back_out, c, first, count),
            dst_ref=at_rows(back_in, c, first, count),
            send_sem=back_s.at[c, n],
            recv_sem=back_r.at[c, n],
            device_id=(t, sides[(side + 2) % 4]),
            device_id_type=MESH,
        )

    def final(c, o, landing):
        return pltpu.make_async_remote_copy(
            src_ref=at_rows(fin_out, c, mates[o] * rows, rows),
            dst_ref=at_rows(fin_in, c, landing * rows, rows),
            send_sem=fin_s.at[c, o],
            recv_sem=fin_r.at[c, o],
            device_id=(before, z * group + mates[o]),
            device_id_type=MESH,
        )

    unpack_copy = pltpu.make_async_remote_copy(
        src_ref=unpack_ref, dst_ref=unpack_in, send_sem=un_s, recv_sem=un_r,
        device_id=(before, me), device_id_type=MESH,
    )
    unpack_copy.start()

    def columns(start):
        return pl.ds(pl.multiple_of(start, 128), CHUNK)

    @pl.loop(0, chunks)
    def _(c):
        for a, ref in enumerate((q_ref, k_ref, v_ref, g_ref)):
            packed[c, a] = dot_nn(pack_ref[...], ref[0, :, columns(c * CHUNK)]).astype(jnp.bfloat16)
        for o in range(1, group):
            a2a(c, o, j).start()
        own = pl.ds(pl.multiple_of(j * rows, 16), rows)
        for a in range(4):
            win[c, a, own, :] = packed[c, a, own, :]
            win[c, a, 224:256, :] = jnp.zeros((32, CHUNK), jnp.bfloat16)

    allowed = (idc_ref[...] == idr_ref[...]) & (idr_ref[...] >= 0)
    bias[...] = jnp.where(allowed, 0.0, NEG)
    scale = HEAD_DIM ** (-0.5)

    def spread(c):
        for o in range(1, group):
            a2a(c, o, sources[o]).wait_recv()
        for a in range(4):
            halo[c, a] = dot_nn(pick_ref[...], win[c, a, 0:128, :]).astype(jnp.bfloat16)
        for n in range(4):
            outward(c, n).start()

    def attend(c):
        for n in range(4):
            outward(c, n).wait_recv()
        valid = jnp.where(idc_ref[...] >= 0, 1.0, 0.0)
        for h in range(CHUNK // HEAD_DIM):
            head = slice(h * HEAD_DIM, (h + 1) * HEAD_DIM)
            q, k, v, g = [win[c, a, :, head] for a in range(4)]
            s = dot_nt(q, k) * scale + bias[...]
            e = jnp.exp(s - jnp.max(s, axis=1, keepdims=True))
            p = e * (valid / jnp.sum(e, axis=1, keepdims=True))
            low = p.astype(jnp.bfloat16)
            dp = dot_nt(g, v)
            delta = jnp.sum(low.astype(jnp.float32) * dp, axis=1, keepdims=True)
            ds = (p * (dp - delta) * scale).astype(jnp.bfloat16)
            for a, grad in enumerate((dot_nn(ds, k), dot_tn(ds, q), dot_tn(low, g))):
                grad = grad.astype(jnp.bfloat16)
                fin_out[c, a, :, head] = grad[0:128]
                back_out[c, a, :, head] = grad[128:224]
        for n in range(4):
            homeward(c, n).start()

    def hand_on(c):
        for n in range(4):
            homeward(c, n).wait_recv()
        for a in range(3):
            returned = dot_nn(place_ref[...], back_in[c, a])
            fin_out[c, a] = (fin_out[c, a].astype(jnp.float32) + returned).astype(jnp.bfloat16)
        for o in range(group):
            final(c, o, j).start()

    def finish(c):
        for o in range(group):
            final(c, o, sources[o]).wait_recv()
        for a in range(3):
            out_ref[0, :, columns(a * width + c * CHUNK)] = dot_nn(
                unpack_in[...], fin_in[c, a]
            ).astype(jnp.bfloat16)

    lead = (0, 1, 2, 3)

    @pl.loop(0, chunks + lead[3])
    def _(step):
        @pl.when(step < chunks)
        def _():
            spread(step)

        @pl.when((step >= lead[1]) & (step < chunks + lead[1]))
        def _():
            attend(step - lead[1])

        @pl.when((step >= lead[2]) & (step < chunks + lead[2]))
        def _():
            hand_on(step - lead[2])

        @pl.when(step == lead[3])
        def _():
            unpack_copy.wait_recv()

        @pl.when(step >= lead[3])
        def _():
            finish(step - lead[3])

    unpack_copy.wait_send()

    @pl.loop(0, chunks)
    def _(c):
        for o in range(1, group):
            a2a(c, o, j).wait_send()
        for n in range(4):
            outward(c, n).wait_send()
            homeward(c, n).wait_send()
        for o in range(group):
            final(c, o, j).wait_send()


def boundary_plan(ids, reach, planes, group, z, j):
    blocks = ids.shape[0] // (reach * planes)
    quarters = ids.reshape(-1, reach)
    first, last = quarters[:, 0], quarters[:, -1]
    none = jnp.full((1,), -1, jnp.int32)
    straddles = last == jnp.concatenate([first[1:], none])
    tail = jnp.where(straddles, jnp.sum(quarters == last[:, None], axis=1, dtype=jnp.int32), 0)
    heads = jnp.sum(quarters == first[:, None], axis=1, dtype=jnp.int32)
    head = jnp.where(straddles, jnp.concatenate([heads[1:], none]), 0)
    right = (tail <= reach // 2).reshape(group, 4, planes)
    r0, r1 = right[:, 0], right[:, 1]
    r2 = jnp.where(r0 == r1, ~r0, right[:, 2])
    go = jnp.stack([r0, r1, r2, right[:, 3]], axis=1).astype(jnp.int32)
    zero = jnp.zeros_like(go[:, 0])
    off_right = jnp.stack([zero, go[:, 0], go[:, 0] + go[:, 1], zero + 2], axis=1) * 16
    off_left = jnp.stack([zero, 1 - go[:, 0], 2 - go[:, 0] - go[:, 1], zero + 2], axis=1) * 16
    go, off_right, off_left = [x.reshape(-1) for x in (go, off_right, off_left)]
    send_right = jnp.where(go == 1, tail, 0)
    send_left = jnp.where(go == 0, head, 0)
    table = jnp.stack([send_right, off_right, send_left, off_left])
    both = jnp.concatenate([table, jnp.pad(table, ((0, 0), (1, 0)))[:, :-1]])
    mine = lax.dynamic_slice(both.reshape(8, blocks, planes), (0, 4 * j, z), (8, 4, 1))
    own = lax.dynamic_slice(ids.reshape(blocks, planes, reach), (4 * j, z, 0), (4, 1, reach))[:, 0]
    sr, our, sl, oul = [mine[i] for i in (0, 1, 6, 7)]
    fr, ofr, fl, ofl = [mine[i] for i in (4, 5, 2, 3)]
    place = jnp.arange(reach, dtype=jnp.int32)[None]
    slot_right = jnp.where(place >= reach - sr, our + place - reach + sr, -1)
    slot_left = jnp.where(place < sl, oul + place, -1)
    slots = jnp.where(slot_right >= 0, slot_right, jnp.where(slot_left >= 0, slot_left + 48, -1))
    kept = jnp.where(slots >= 0, -1, own)

    def arrival(x):
        return x.reshape(4, group, reach // group).transpose(1, 0, 2).reshape(-1)

    slots, kept = arrival(slots), arrival(kept)
    slot = jnp.arange(48, dtype=jnp.int32)[None]
    from_left = jnp.max(jnp.where((slot >= ofr) & (slot < ofr + fr), own[:, :1], -1), axis=0)
    from_right = jnp.max(jnp.where((slot >= ofl) & (slot < ofl + fl), own[:, -1:], -1), axis=0)
    window = jnp.concatenate([kept, from_left, from_right, jnp.full((32,), -1, jnp.int32)])
    return slots, window


def fused_body(sections, queries, key_cells, value_cells, grad_cells, packing, segment_ids):
    cell_count, width = queries.shape[1:]
    devices = lax.axis_size("dp")
    reach = cell_count // 4
    group = reach * devices // cell_count
    planes = devices // group
    me = lax.axis_index("dp")
    slots, window = boundary_plan(
        segment_ids[0], reach, planes, group, me // group, me % group
    )
    cells = jnp.arange(cell_count, dtype=jnp.int32)
    order = packing[0, 0]
    pack = (order[:, None] == cells[None]).astype(jnp.bfloat16)
    unpack = (cells[:, None] == order[None]).astype(jnp.bfloat16)
    spots = jnp.arange(96, dtype=jnp.int32)
    pick = (spots[:, None] == slots[None]).astype(jnp.bfloat16)
    place = (slots[:, None] == spots[None]).astype(jnp.bfloat16)
    chunks = width // CHUNK
    vmem = pl.BlockSpec(memory_space=pltpu.VMEM)
    bf16 = jnp.bfloat16
    sem = pltpu.SemaphoreType.DMA
    return pl.pallas_call(
        functools.partial(kernel, group, planes, sections, chunks, width),
        out_shape=jax.ShapeDtypeStruct((1, cell_count, 3 * width), bf16),
        in_specs=[vmem] * 10,
        out_specs=vmem,
        scratch_shapes=[
            pltpu.VMEM((chunks, 4, 128, CHUNK), bf16),
            pltpu.VMEM((chunks, 4, 256, CHUNK), bf16),
            pltpu.VMEM((chunks, 4, 96, CHUNK), bf16),
            pltpu.VMEM((chunks, 3, 96, CHUNK), bf16),
            pltpu.VMEM((chunks, 3, 96, CHUNK), bf16),
            pltpu.VMEM((chunks, 3, 128, CHUNK), bf16),
            pltpu.VMEM((chunks, 3, 128, CHUNK), bf16),
            pltpu.VMEM((128, 128), bf16),
            pltpu.VMEM((256, 256), jnp.float32),
            sem((chunks, group - 1)), sem((chunks, group - 1)),
            sem((chunks, 4)), sem((chunks, 4)),
            sem((chunks, 4)), sem((chunks, 4)),
            sem((chunks, group)), sem((chunks, group)),
            sem, sem,
        ],
        compiler_params=pltpu.CompilerParams(
            collective_id=0, has_side_effects=True, vmem_limit_bytes=48 * 1024 * 1024
        ),
    )(
        queries, key_cells, value_cells, grad_cells,
        pack, unpack, pick, place, window[:, None], window[None],
    )


def solution(mesh):
    sections, devices = mesh.shape["section"], mesh.shape["dp"]

    def body_of(queries, *rest):
        fits = queries.shape[1] == 128 and queries.shape[2] % CHUNK == 0 and devices == 16
        if fits:
            return fused_body(sections, queries, *rest)
        return body(queries, *rest)

    return jax.shard_map(
        body_of,
        mesh=mesh,
        in_specs=(
            P("section", "dp", None),
            P("section", "dp", None),
            P("section", "dp", None),
            P("section", "dp", None),
            P("section", "dp", None),
            P("section", None),
        ),
        out_specs=P("section", "dp", None),
        check_vma=False,
    )
```

```python
import functools
import jax
import jax.numpy as jnp
from jax import lax
from jax.sharding import PartitionSpec as P
from jax.experimental import pallas as pl
from jax.experimental.pallas import tpu as pltpu

HEADS = 20
HEAD_DIM = 128
CHUNK = 256
MESH = pl.DeviceIdType.MESH
NEG = -1e30
PIECES = ((0, 32, 0), (32, 16, 1), (48, 32, 2), (80, 16, 3))


def with_halo(value, sides, width):
    for axis, dim in sides:
        size, length = (lax.axis_size(axis), value.shape[dim])
        up = [(i, (i + 1) % size) for i in range(size - 1)]
        down = [(j, i) for i, j in up]
        last = lax.slice_in_dim(value, length - width, length, axis=dim)
        initial = lax.slice_in_dim(value, 0, width, axis=dim)
        before = lax.ppermute(last, axis, up)
        after = lax.ppermute(initial, axis, down)
        value = jnp.concatenate([before, value, after], axis=dim)
    return value


def passed_along(value, axis, steps):
    count = lax.axis_size(axis)
    initial, last = (max(0, -steps), min(count, count - steps))
    return lax.ppermute(value, axis, [(source, source + steps) for source in range(initial, last)])


def from_behind(block, axis, distance):
    devices = range(lax.axis_size(axis))
    route = [((i - distance) % len(devices), i) for i in devices]
    return lax.ppermute(block, axis, route)


def heads_of(matrix):
    return matrix.reshape(matrix.shape[0], HEADS, HEAD_DIM)


def masked_scores(query_rows, key_rows, query_ids, key_ids):
    scores = jnp.einsum(
        "ihd,jhd->hij", heads_of(query_rows), heads_of(key_rows), preferred_element_type=jnp.float32
    )
    scores = scores * HEAD_DIM ** (-0.5)
    allowed = (query_ids[:, None] == key_ids[None, :])[None]
    return jnp.where(allowed, scores, -jnp.inf)


def body(queries, key_cells, value_cells, grad_cells, packing, segment_ids):
    cell_count = queries.shape[1]
    width = queries.shape[2]
    groups = lax.axis_size("dp")
    per_peer = cell_count // groups
    reach = cell_count // 4
    place = lax.axis_index("dp")
    scale = HEAD_DIM ** (-0.5)
    order = packing[0, 0]

    def pack(matrix):
        return matrix[0][order].reshape(groups, per_peer, width)

    arrived = (
        lax.all_to_all(pack(queries), "dp", split_axis=0, concat_axis=0, tiled=True),
        lax.all_to_all(pack(key_cells), "dp", split_axis=0, concat_axis=0, tiled=True),
        lax.all_to_all(pack(value_cells), "dp", split_axis=0, concat_axis=0, tiled=True),
        lax.all_to_all(pack(grad_cells), "dp", split_axis=0, concat_axis=0, tiled=True),
    )
    own_q, own_k, own_v, own_g = [piece.reshape(cell_count, width) for piece in arrived]
    rim_ids = jnp.full((reach,), -1, jnp.int32)
    padded_ids = jnp.concatenate([rim_ids, segment_ids[0], rim_ids])
    window_ids = lax.dynamic_slice_in_dim(padded_ids, place * cell_count, cell_count + 2 * reach)
    own_ids = window_ids[reach : reach + cell_count]
    key_value = jnp.concatenate([own_k, own_v], axis=1)
    key_value_window = with_halo(key_value, (("dp", 0),), reach)
    key_window = key_value_window[:, :width]
    value_window = key_value_window[:, width:]
    scores = masked_scores(own_q, key_window, own_ids, window_ids)
    top = jnp.max(scores, axis=2)
    log_total = top + jnp.log(jnp.sum(jnp.exp(scores - top[:, :, None]), axis=2))
    probs = jnp.exp(scores - log_total[:, :, None])
    probs_low = probs.astype(jnp.bfloat16)
    grad_heads = heads_of(own_g)
    attended = jnp.einsum(
        "hij,jhd->ihd", probs_low, heads_of(value_window), preferred_element_type=jnp.float32
    )
    delta = jnp.sum(grad_heads.astype(jnp.float32) * attended, axis=2).T
    dprobs = jnp.einsum(
        "ihd,jhd->hij", grad_heads, heads_of(value_window), preferred_element_type=jnp.float32
    )
    dscores = (probs * (dprobs - delta[:, :, None]) * scale).astype(jnp.bfloat16)
    grad_query = jnp.einsum(
        "hij,jhd->ihd", dscores, heads_of(key_window), preferred_element_type=jnp.float32
    )
    grad_query = grad_query.reshape(cell_count, width).astype(jnp.bfloat16)
    window = cell_count + 2 * reach
    grad_key = jnp.einsum(
        "hij,ihd->jhd", dscores, heads_of(own_q), preferred_element_type=jnp.float32
    )
    grad_value = jnp.einsum(
        "hij,ihd->jhd", probs_low, grad_heads, preferred_element_type=jnp.float32
    )
    partial_value = jnp.concatenate(
        [grad_key.reshape(window, width), grad_value.reshape(window, width)], axis=1
    )
    from_after = passed_along(partial_value[:reach].astype(jnp.bfloat16), "dp", -1).astype(
        jnp.float32
    )
    from_before = passed_along(
        partial_value[reach + cell_count :].astype(jnp.bfloat16), "dp", 1
    ).astype(jnp.float32)
    summed = partial_value[reach : reach + cell_count]
    summed = summed.at[cell_count - reach :].add(from_after)
    summed = summed.at[:reach].add(from_before)
    packed_grads = jnp.concatenate([grad_query, summed.astype(jnp.bfloat16)], axis=1)
    returned = lax.all_to_all(
        packed_grads.reshape(groups, per_peer, 3 * width),
        "dp",
        split_axis=0,
        concat_axis=0,
        tiled=True,
    )
    returned = returned.reshape(cell_count, 3 * width)
    inverse = (
        jnp.zeros((cell_count,), jnp.int32).at[order].set(jnp.arange(cell_count, dtype=jnp.int32))
    )
    loaded_order = returned[inverse]
    handed = from_behind(loaded_order, "section", -1)
    return handed[None]


def dot_nt(a, b):
    return lax.dot_general(a, b, (((1,), (1,)), ((), ())), preferred_element_type=jnp.float32)


def dot_tn(a, b):
    return lax.dot_general(a, b, (((0,), (0,)), ((), ())), preferred_element_type=jnp.float32)


def dot_nn(a, b):
    return jnp.dot(a, b, preferred_element_type=jnp.float32)


def one_hot(index, dim, shape):
    return jnp.where(lax.broadcasted_iota(jnp.int32, shape, dim) == index, 1.0, 0.0).astype(jnp.bfloat16)


def small(x):
    return x.astype(jnp.float32).astype(jnp.bfloat16)


def upright(row):
    eye = one_hot(lax.broadcasted_iota(jnp.int32, (1, 128), 1), 0, (128, 128))
    column = dot_nt(eye, small(jnp.broadcast_to(row, (16, 128))))
    return column[:, 0:1].astype(jnp.int32)


def directions(tails, shift):
    kept = [tails[i : i + 1] <= 16 for i in range(4)]
    order = [jnp.where(shift, kept[(i + 1) % 4].astype(jnp.int32), kept[i].astype(jnp.int32)) for i in range(4)]
    g0, g1 = order[0], order[1]
    go = [g0, g1, jnp.where(g0 == g1, 1 - g0, order[2]), order[3]]
    zero = jnp.zeros_like(g0)
    right = [zero, 16 * g0, 16 * (g0 + g1), zero + 32]
    left = [zero, 16 * (1 - g0), 16 * (2 - g0 - g1), zero + 32]
    return [
        jnp.concatenate([jnp.where(shift, x[(i + 3) % 4], x[i]) for i in range(4)], axis=0)
        for x in (go, right, left)
    ]


def boundary_plan(ids_ref, blocks, planes, z, j):
    reach = 128 // 4
    count = ids_ref.shape[1] // 128
    blocks[...] = jnp.full(blocks.shape, -1, jnp.int32)
    for b in range(count):
        blocks[b + 1 : b + 2, :] = ids_ref[:, b * 128 : (b + 1) * 128]
    here, ahead, behind = [
        jnp.concatenate([blocks[pl.ds(4 * j + k + d, 1), :] for k in range(4)], axis=0) for d in (1, 2, 0)
    ]
    span = 128 // planes
    first_plane, last_plane = z == 0, z == planes - 1
    place = lax.broadcasted_iota(jnp.int32, (4, 128), 1)
    inside = place < reach

    def turned(x, plane):
        return pltpu.roll(x, lax.rem(2 * 128 - plane * span, 128), 1)

    own = turned(here, z)
    prior = turned(jnp.where(first_plane, behind, here), z - 1)
    later = turned(jnp.where(last_plane, ahead, here), z + 1)

    def matching(x, value, straddles):
        hits = jnp.sum(jnp.where(inside & (x == value), 1.0, 0.0), axis=1, keepdims=True)
        return jnp.where(straddles, hits, 0.0).astype(jnp.int32)

    first, last = own[:, 0:1], own[:, reach - 1 : reach]
    before, after = prior[:, reach - 1 : reach], later[:, 0:1]
    tail_r, head_r = [matching(x, last, last == after) for x in (own, later)]
    tail_l, head_l = [matching(x, first, first == before) for x in (prior, own)]
    go_r, right_r, left_r = directions(tail_r, False)
    go_l, right_l, left_l = directions(tail_l, first_plane)
    sent_r, sent_l = jnp.where(go_r == 1, tail_r, 0), jnp.where(go_l == 0, head_l, 0)
    got_l, got_r = jnp.where(go_l == 1, tail_l, 0), jnp.where(go_r == 0, head_r, 0)
    begin = reach - sent_r
    slots = jnp.where(
        inside & (place >= begin),
        right_r + place - begin,
        jnp.where(place < sent_l, 48 + left_l + place, -1),
    )
    kept = jnp.where(slots >= 0, -1, own)
    lane = lax.broadcasted_iota(jnp.int32, (1, 128), 1)
    route = one_hot(lane // 32 * 8 + lane % 8, 0, (128, 128))
    block = lane // 8 % 4

    def arrival(x):
        moved = dot_nn(small(jnp.concatenate([x] * 4, axis=0)), route)
        total = jnp.zeros((1, 128), jnp.float32)
        for k in range(4):
            total = total + jnp.where(block == k, moved[k : k + 1], 0.0)
        return total.astype(jnp.int32)

    left_hit = (place >= right_l) & (place < right_l + got_l)
    right_hit = (place >= 48 + left_r) & (place < 48 + left_r + got_r)
    foreign = jnp.where(left_hit, first, jnp.where(right_hit, last, -1))
    foreign = jnp.max(foreign.astype(jnp.float32), axis=0, keepdims=True).astype(jnp.int32)
    return arrival(slots), arrival(kept), foreign


def kernel(
    group, planes, sections, chunks, width,
    q_ref, k_ref, v_ref, g_ref, packing_ref, ids_ref,
    out_ref,
    loaded, packed, win, halo, back_out, back_in, fin_out, fin_in, unpack_in, bias, valid,
    pack_ref, unpack_ref, pick_ref, place_ref, blocks, load_s,
    a2a_s, a2a_r, halo_s, halo_r, back_s, back_r, fin_s, fin_r, un_s, un_r,
):
    t = lax.axis_index("section")
    me = lax.axis_index("dp")
    z, j = lax.div(me, group), lax.rem(me, group)
    rows = 128 // group
    before = lax.rem(t + sections - 1, sections)
    after = lax.rem(t + 1, sections)
    zr, zl = lax.rem(z + 1, planes), lax.rem(z + planes - 1, planes)
    jr = lax.rem(j + jnp.where(z == planes - 1, 1, 0), group)
    jl = lax.rem(j + group - jnp.where(z == 0, 1, 0), group)
    sides = (zr * group + j, zr * group + jr, zl * group + j, zl * group + jl)
    mates = [lax.rem(j + o, group) for o in range(group)]
    sources = [lax.rem(j + group - o, group) for o in range(group)]

    def columns(start):
        return pl.ds(pl.multiple_of(start, 128), CHUNK)

    def load(c, a):
        ref = (q_ref, k_ref, v_ref, g_ref)[a]
        return pltpu.make_async_copy(ref.at[0, :, columns(c * CHUNK)], loaded.at[c, a], load_s.at[c, a])

    @pl.loop(0, chunks)
    def _(c):
        for a in range(4):
            load(c, a).start()

    barrier = pltpu.get_barrier_semaphore()
    for o in range(1, group):
        pl.semaphore_signal(barrier, inc=1, device_id=(t, z * group + mates[o]), device_id_type=MESH)
    for side in sides:
        pl.semaphore_signal(barrier, inc=1, device_id=(t, side), device_id_type=MESH)
    for o in range(group):
        pl.semaphore_signal(barrier, inc=1, device_id=(after, z * group + mates[o]), device_id_type=MESH)
    order = packing_ref[0]
    unpack_ref[...] = one_hot(order, 0, (128, 128))
    pack_ref[...] = one_hot(upright(order), 1, (128, 128))
    pl.semaphore_wait(barrier, 2 * group + 3)

    def at_rows(ref, c, start, count):
        if not isinstance(start, int):
            start = pl.multiple_of(start, 16)
        return ref.at[c, :, pl.ds(start, count), :]

    def a2a(c, o, landing):
        return pltpu.make_async_remote_copy(
            src_ref=at_rows(packed, c, mates[o] * rows, rows),
            dst_ref=at_rows(win, c, landing * rows, rows),
            send_sem=a2a_s.at[c, o - 1],
            recv_sem=a2a_r.at[c, o - 1],
            device_id=(t, z * group + mates[o]),
            device_id_type=MESH,
        )

    def outward(c, n):
        first, count, side = PIECES[n]
        return pltpu.make_async_remote_copy(
            src_ref=at_rows(halo, c, first, count),
            dst_ref=at_rows(win, c, 128 + first, count),
            send_sem=halo_s.at[c, n],
            recv_sem=halo_r.at[c, n],
            device_id=(t, sides[side]),
            device_id_type=MESH,
        )

    def homeward(c, n):
        first, count, side = PIECES[n]
        return pltpu.make_async_remote_copy(
            src_ref=at_rows(back_out, c, first, count),
            dst_ref=at_rows(back_in, c, first, count),
            send_sem=back_s.at[c, n],
            recv_sem=back_r.at[c, n],
            device_id=(t, sides[(side + 2) % 4]),
            device_id_type=MESH,
        )

    def final(c, o, landing):
        return pltpu.make_async_remote_copy(
            src_ref=at_rows(fin_out, c, mates[o] * rows, rows),
            dst_ref=at_rows(fin_in, c, landing * rows, rows),
            send_sem=fin_s.at[c, o],
            recv_sem=fin_r.at[c, o],
            device_id=(before, z * group + mates[o]),
            device_id_type=MESH,
        )

    unpack_copy = pltpu.make_async_remote_copy(
        src_ref=unpack_ref, dst_ref=unpack_in, send_sem=un_s, recv_sem=un_r,
        device_id=(before, me), device_id_type=MESH,
    )
    unpack_copy.start()

    @pl.loop(0, chunks)
    def _(c):
        for a in range(4):
            load(c, a).wait()
            packed[c, a] = dot_nn(pack_ref[...], loaded[c, a]).astype(jnp.bfloat16)
        for o in range(1, group):
            a2a(c, o, j).start()
        own = pl.ds(pl.multiple_of(j * rows, 16), rows)
        for a in range(4):
            win[c, a, own, :] = packed[c, a, own, :]
            win[c, a, 224:256, :] = jnp.zeros((32, CHUNK), jnp.bfloat16)

    slots, kept, foreign = boundary_plan(ids_ref, blocks, planes, z, j)
    pick_ref[...] = one_hot(slots, 0, (96, 128))
    place_ref[...] = one_hot(upright(slots), 1, (128, 96))
    id_row = jnp.concatenate([kept, foreign], axis=1)
    id_col = jnp.concatenate([upright(kept), upright(foreign)], axis=0)
    bias[...] = jnp.where((id_col == id_row) & (id_row >= 0), 0.0, NEG)
    valid[...] = jnp.where(id_col >= 0, 1.0, 0.0)
    scale = HEAD_DIM ** (-0.5)

    def spread(c):
        for o in range(1, group):
            a2a(c, o, sources[o]).wait_recv()
        for a in range(4):
            halo[c, a] = dot_nn(pick_ref[...], win[c, a, 0:128, :]).astype(jnp.bfloat16)
        for n in range(4):
            outward(c, n).start()

    def attend(c):
        for n in range(4):
            outward(c, n).wait_recv()
        for h in range(CHUNK // HEAD_DIM):
            head = slice(h * HEAD_DIM, (h + 1) * HEAD_DIM)
            q, k, v, g = [win[c, a, :, head] for a in range(4)]
            s = dot_nt(q, k) * scale + bias[...]
            e = jnp.exp(s - jnp.max(s, axis=1, keepdims=True))
            p = e * (valid[...] / jnp.sum(e, axis=1, keepdims=True))
            low = p.astype(jnp.bfloat16)
            dp = dot_nt(g, v)
            delta = jnp.sum(low.astype(jnp.float32) * dp, axis=1, keepdims=True)
            ds = (p * (dp - delta) * scale).astype(jnp.bfloat16)
            for a, grad in enumerate((dot_nn(ds, k), dot_tn(ds, q), dot_tn(low, g))):
                grad = grad.astype(jnp.bfloat16)
                fin_out[c, a, :, head] = grad[0:128]
                back_out[c, a, :, head] = grad[128:224]
        for n in range(4):
            homeward(c, n).start()

    def hand_on(c):
        for n in range(4):
            homeward(c, n).wait_recv()
        for a in range(3):
            returned = dot_nn(place_ref[...], back_in[c, a])
            fin_out[c, a] = (fin_out[c, a].astype(jnp.float32) + returned).astype(jnp.bfloat16)
        for o in range(group):
            final(c, o, j).start()

    def finish(c):
        for o in range(group):
            final(c, o, sources[o]).wait_recv()
        for a in range(3):
            out_ref[0, :, columns(a * width + c * CHUNK)] = dot_nn(
                unpack_in[...], fin_in[c, a]
            ).astype(jnp.bfloat16)

    lead = (0, 2, 4, 6)

    @pl.loop(0, chunks + lead[3])
    def _(step):
        @pl.when(step < chunks)
        def _():
            spread(step)

        @pl.when((step >= lead[1]) & (step < chunks + lead[1]))
        def _():
            attend(step - lead[1])

        @pl.when((step >= lead[2]) & (step < chunks + lead[2]))
        def _():
            hand_on(step - lead[2])

        @pl.when(step == lead[3])
        def _():
            unpack_copy.wait_recv()

        @pl.when(step >= lead[3])
        def _():
            finish(step - lead[3])

    unpack_copy.wait_send()

    @pl.loop(0, chunks)
    def _(c):
        for o in range(1, group):
            a2a(c, o, j).wait_send()
        for n in range(4):
            outward(c, n).wait_send()
            homeward(c, n).wait_send()
        for o in range(group):
            final(c, o, j).wait_send()


def fused_body(sections, queries, key_cells, value_cells, grad_cells, packing, segment_ids):
    cell_count, width = queries.shape[1:]
    devices = lax.axis_size("dp")
    group = devices // 4
    planes = devices // group
    chunks = width // CHUNK
    vmem = pl.BlockSpec(memory_space=pltpu.VMEM)
    far = pl.BlockSpec(memory_space=pl.ANY)
    bf16 = jnp.bfloat16
    sem = pltpu.SemaphoreType.DMA
    return pl.pallas_call(
        functools.partial(kernel, group, planes, sections, chunks, width),
        out_shape=jax.ShapeDtypeStruct((1, cell_count, 3 * width), bf16),
        in_specs=[far] * 4 + [vmem] * 2,
        out_specs=vmem,
        scratch_shapes=[
            pltpu.VMEM((chunks, 4, 128, CHUNK), bf16),
            pltpu.VMEM((chunks, 4, 128, CHUNK), bf16),
            pltpu.VMEM((chunks, 4, 256, CHUNK), bf16),
            pltpu.VMEM((chunks, 4, 96, CHUNK), bf16),
            pltpu.VMEM((chunks, 3, 96, CHUNK), bf16),
            pltpu.VMEM((chunks, 3, 96, CHUNK), bf16),
            pltpu.VMEM((chunks, 3, 128, CHUNK), bf16),
            pltpu.VMEM((chunks, 3, 128, CHUNK), bf16),
            pltpu.VMEM((128, 128), bf16),
            pltpu.VMEM((256, 256), jnp.float32),
            pltpu.VMEM((256, 1), jnp.float32),
            pltpu.VMEM((128, 128), bf16),
            pltpu.VMEM((128, 128), bf16),
            pltpu.VMEM((96, 128), bf16),
            pltpu.VMEM((128, 96), bf16),
            pltpu.VMEM((segment_ids.shape[1] // 128 + 8, 128), jnp.int32),
            sem((chunks, 4)),
            sem((chunks, group - 1)), sem((chunks, group - 1)),
            sem((chunks, 4)), sem((chunks, 4)),
            sem((chunks, 4)), sem((chunks, 4)),
            sem((chunks, group)), sem((chunks, group)),
            sem, sem,
        ],
        compiler_params=pltpu.CompilerParams(
            collective_id=0, has_side_effects=True, vmem_limit_bytes=48 * 1024 * 1024
        ),
    )(queries, key_cells, value_cells, grad_cells, packing, segment_ids)


def solution(mesh):
    sections, devices = mesh.shape["section"], mesh.shape["dp"]

    def body_of(queries, *rest):
        fits = queries.shape[1] == 128 and queries.shape[2] % CHUNK == 0 and devices == 16
        if fits:
            return fused_body(sections, queries, *rest)
        return body(queries, *rest)

    return jax.shard_map(
        body_of,
        mesh=mesh,
        in_specs=(
            P("section", "dp", None),
            P("section", "dp", None),
            P("section", "dp", None),
            P("section", "dp", None),
            P("section", "dp", None),
            P("section", None),
        ),
        out_specs=P("section", "dp", None),
        check_vma=False,
    )
```

```python
import functools
import jax
import jax.numpy as jnp
from jax import lax
from jax.sharding import PartitionSpec as P
from jax.experimental import pallas as pl
from jax.experimental.pallas import tpu as pltpu

HEADS = 20
HEAD_DIM = 128
CHUNK = 256
MESH = pl.DeviceIdType.MESH
NEG = -1e30
PIECES = ((0, 32, 0), (32, 16, 1), (48, 32, 2), (80, 16, 3))


def with_halo(value, sides, width):
    for axis, dim in sides:
        size, length = (lax.axis_size(axis), value.shape[dim])
        up = [(i, (i + 1) % size) for i in range(size - 1)]
        down = [(j, i) for i, j in up]
        last = lax.slice_in_dim(value, length - width, length, axis=dim)
        initial = lax.slice_in_dim(value, 0, width, axis=dim)
        before = lax.ppermute(last, axis, up)
        after = lax.ppermute(initial, axis, down)
        value = jnp.concatenate([before, value, after], axis=dim)
    return value


def passed_along(value, axis, steps):
    count = lax.axis_size(axis)
    initial, last = (max(0, -steps), min(count, count - steps))
    return lax.ppermute(value, axis, [(source, source + steps) for source in range(initial, last)])


def from_behind(block, axis, distance):
    devices = range(lax.axis_size(axis))
    route = [((i - distance) % len(devices), i) for i in devices]
    return lax.ppermute(block, axis, route)


def heads_of(matrix):
    return matrix.reshape(matrix.shape[0], HEADS, HEAD_DIM)


def masked_scores(query_rows, key_rows, query_ids, key_ids):
    scores = jnp.einsum(
        "ihd,jhd->hij", heads_of(query_rows), heads_of(key_rows), preferred_element_type=jnp.float32
    )
    scores = scores * HEAD_DIM ** (-0.5)
    allowed = (query_ids[:, None] == key_ids[None, :])[None]
    return jnp.where(allowed, scores, -jnp.inf)


def body(queries, key_cells, value_cells, grad_cells, packing, segment_ids):
    cell_count = queries.shape[1]
    width = queries.shape[2]
    groups = lax.axis_size("dp")
    per_peer = cell_count // groups
    reach = cell_count // 4
    place = lax.axis_index("dp")
    scale = HEAD_DIM ** (-0.5)
    order = packing[0, 0]

    def pack(matrix):
        return matrix[0][order].reshape(groups, per_peer, width)

    arrived = (
        lax.all_to_all(pack(queries), "dp", split_axis=0, concat_axis=0, tiled=True),
        lax.all_to_all(pack(key_cells), "dp", split_axis=0, concat_axis=0, tiled=True),
        lax.all_to_all(pack(value_cells), "dp", split_axis=0, concat_axis=0, tiled=True),
        lax.all_to_all(pack(grad_cells), "dp", split_axis=0, concat_axis=0, tiled=True),
    )
    own_q, own_k, own_v, own_g = [piece.reshape(cell_count, width) for piece in arrived]
    rim_ids = jnp.full((reach,), -1, jnp.int32)
    padded_ids = jnp.concatenate([rim_ids, segment_ids[0], rim_ids])
    window_ids = lax.dynamic_slice_in_dim(padded_ids, place * cell_count, cell_count + 2 * reach)
    own_ids = window_ids[reach : reach + cell_count]
    key_value = jnp.concatenate([own_k, own_v], axis=1)
    key_value_window = with_halo(key_value, (("dp", 0),), reach)
    key_window = key_value_window[:, :width]
    value_window = key_value_window[:, width:]
    scores = masked_scores(own_q, key_window, own_ids, window_ids)
    top = jnp.max(scores, axis=2)
    log_total = top + jnp.log(jnp.sum(jnp.exp(scores - top[:, :, None]), axis=2))
    probs = jnp.exp(scores - log_total[:, :, None])
    probs_low = probs.astype(jnp.bfloat16)
    grad_heads = heads_of(own_g)
    attended = jnp.einsum(
        "hij,jhd->ihd", probs_low, heads_of(value_window), preferred_element_type=jnp.float32
    )
    delta = jnp.sum(grad_heads.astype(jnp.float32) * attended, axis=2).T
    dprobs = jnp.einsum(
        "ihd,jhd->hij", grad_heads, heads_of(value_window), preferred_element_type=jnp.float32
    )
    dscores = (probs * (dprobs - delta[:, :, None]) * scale).astype(jnp.bfloat16)
    grad_query = jnp.einsum(
        "hij,jhd->ihd", dscores, heads_of(key_window), preferred_element_type=jnp.float32
    )
    grad_query = grad_query.reshape(cell_count, width).astype(jnp.bfloat16)
    window = cell_count + 2 * reach
    grad_key = jnp.einsum(
        "hij,ihd->jhd", dscores, heads_of(own_q), preferred_element_type=jnp.float32
    )
    grad_value = jnp.einsum(
        "hij,ihd->jhd", probs_low, grad_heads, preferred_element_type=jnp.float32
    )
    partial_value = jnp.concatenate(
        [grad_key.reshape(window, width), grad_value.reshape(window, width)], axis=1
    )
    from_after = passed_along(partial_value[:reach].astype(jnp.bfloat16), "dp", -1).astype(
        jnp.float32
    )
    from_before = passed_along(
        partial_value[reach + cell_count :].astype(jnp.bfloat16), "dp", 1
    ).astype(jnp.float32)
    summed = partial_value[reach : reach + cell_count]
    summed = summed.at[cell_count - reach :].add(from_after)
    summed = summed.at[:reach].add(from_before)
    packed_grads = jnp.concatenate([grad_query, summed.astype(jnp.bfloat16)], axis=1)
    returned = lax.all_to_all(
        packed_grads.reshape(groups, per_peer, 3 * width),
        "dp",
        split_axis=0,
        concat_axis=0,
        tiled=True,
    )
    returned = returned.reshape(cell_count, 3 * width)
    inverse = (
        jnp.zeros((cell_count,), jnp.int32).at[order].set(jnp.arange(cell_count, dtype=jnp.int32))
    )
    loaded_order = returned[inverse]
    handed = from_behind(loaded_order, "section", -1)
    return handed[None]


def dot_nt(a, b):
    return lax.dot_general(a, b, (((1,), (1,)), ((), ())), preferred_element_type=jnp.float32)


def dot_tn(a, b):
    return lax.dot_general(a, b, (((0,), (0,)), ((), ())), preferred_element_type=jnp.float32)


def dot_nn(a, b):
    return jnp.dot(a, b, preferred_element_type=jnp.float32)


def one_hot(index, dim, shape):
    return jnp.where(lax.broadcasted_iota(jnp.int32, shape, dim) == index, 1.0, 0.0).astype(jnp.bfloat16)


def small(x):
    return x.astype(jnp.float32).astype(jnp.bfloat16)


def upright(row):
    eye = one_hot(lax.broadcasted_iota(jnp.int32, (1, 128), 1), 0, (128, 128))
    column = dot_nt(eye, small(jnp.broadcast_to(row, (16, 128))))
    return column[:, 0:1].astype(jnp.int32)


def directions(tails, shift):
    kept = [tails[i : i + 1] <= 16 for i in range(4)]
    order = [jnp.where(shift, kept[(i + 1) % 4].astype(jnp.int32), kept[i].astype(jnp.int32)) for i in range(4)]
    g0, g1 = order[0], order[1]
    go = [g0, g1, jnp.where(g0 == g1, 1 - g0, order[2]), order[3]]
    zero = jnp.zeros_like(g0)
    right = [zero, 16 * g0, 16 * (g0 + g1), zero + 32]
    left = [zero, 16 * (1 - g0), 16 * (2 - g0 - g1), zero + 32]
    return [
        jnp.concatenate([jnp.where(shift, x[(i + 3) % 4], x[i]) for i in range(4)], axis=0)
        for x in (go, right, left)
    ]


def boundary_plan(ids_ref, blocks, planes, z, j):
    reach = 128 // 4
    count = ids_ref.shape[1] // 128
    blocks[...] = jnp.full(blocks.shape, -1, jnp.int32)
    for b in range(count):
        blocks[b + 1 : b + 2, :] = ids_ref[:, b * 128 : (b + 1) * 128]
    here, ahead, behind = [
        jnp.concatenate([blocks[pl.ds(4 * j + k + d, 1), :] for k in range(4)], axis=0) for d in (1, 2, 0)
    ]
    span = 128 // planes
    first_plane, last_plane = z == 0, z == planes - 1
    place = lax.broadcasted_iota(jnp.int32, (4, 128), 1)
    inside = place < reach

    def turned(x, plane):
        return pltpu.roll(x, lax.rem(2 * 128 - plane * span, 128), 1)

    own = turned(here, z)
    prior = turned(jnp.where(first_plane, behind, here), z - 1)
    later = turned(jnp.where(last_plane, ahead, here), z + 1)

    def matching(x, value, straddles):
        hits = jnp.sum(jnp.where(inside & (x == value), 1.0, 0.0), axis=1, keepdims=True)
        return jnp.where(straddles, hits, 0.0).astype(jnp.int32)

    first, last = own[:, 0:1], own[:, reach - 1 : reach]
    before, after = prior[:, reach - 1 : reach], later[:, 0:1]
    tail_r, head_r = [matching(x, last, last == after) for x in (own, later)]
    tail_l, head_l = [matching(x, first, first == before) for x in (prior, own)]
    go_r, right_r, left_r = directions(tail_r, False)
    go_l, right_l, left_l = directions(tail_l, first_plane)
    sent_r, sent_l = jnp.where(go_r == 1, tail_r, 0), jnp.where(go_l == 0, head_l, 0)
    got_l, got_r = jnp.where(go_l == 1, tail_l, 0), jnp.where(go_r == 0, head_r, 0)
    begin = reach - sent_r
    slots = jnp.where(
        inside & (place >= begin),
        right_r + place - begin,
        jnp.where(place < sent_l, 48 + left_l + place, -1),
    )
    kept = jnp.where(slots >= 0, -1, own)
    lane = lax.broadcasted_iota(jnp.int32, (1, 128), 1)
    route = one_hot(lane // 32 * 8 + lane % 8, 0, (128, 128))
    block = lane // 8 % 4

    def arrival(x):
        moved = dot_nn(small(jnp.concatenate([x] * 4, axis=0)), route)
        total = jnp.zeros((1, 128), jnp.float32)
        for k in range(4):
            total = total + jnp.where(block == k, moved[k : k + 1], 0.0)
        return total.astype(jnp.int32)

    left_hit = (place >= right_l) & (place < right_l + got_l)
    right_hit = (place >= 48 + left_r) & (place < 48 + left_r + got_r)
    foreign = jnp.where(left_hit, first, jnp.where(right_hit, last, -1))
    foreign = jnp.max(foreign.astype(jnp.float32), axis=0, keepdims=True).astype(jnp.int32)
    return arrival(slots), arrival(kept), foreign


def kernel(
    group, planes, sections, chunks, width,
    q_ref, k_ref, v_ref, g_ref, packing_ref, ids_ref,
    out_ref,
    loaded, packed, win, halo, back_out, back_in, fin_out, fin_in, unpack_in, bias, valid,
    pack_ref, unpack_ref, pick_ref, place_ref, blocks, load_s,
    a2a_s, a2a_r, halo_s, halo_r, back_s, back_r, fin_s, fin_r, un_s, un_r,
):
    t = lax.axis_index("section")
    me = lax.axis_index("dp")
    z, j = lax.div(me, group), lax.rem(me, group)
    rows = 128 // group
    before = lax.rem(t + sections - 1, sections)
    after = lax.rem(t + 1, sections)
    zr, zl = lax.rem(z + 1, planes), lax.rem(z + planes - 1, planes)
    jr = lax.rem(j + jnp.where(z == planes - 1, 1, 0), group)
    jl = lax.rem(j + group - jnp.where(z == 0, 1, 0), group)
    sides = (zr * group + j, zr * group + jr, zl * group + j, zl * group + jl)
    mates = [lax.rem(j + o, group) for o in range(group)]
    sources = [lax.rem(j + group - o, group) for o in range(group)]

    def columns(start):
        return pl.ds(pl.multiple_of(start, 128), CHUNK)

    def load(c, a):
        ref = (q_ref, k_ref, v_ref, g_ref)[a]
        return pltpu.make_async_copy(ref.at[0, :, columns(c * CHUNK)], loaded.at[c, a], load_s.at[c, a])

    barrier = pltpu.get_barrier_semaphore()
    for o in range(1, group):
        pl.semaphore_signal(barrier, inc=1, device_id=(t, z * group + mates[o]), device_id_type=MESH)
    for side in sides:
        pl.semaphore_signal(barrier, inc=1, device_id=(t, side), device_id_type=MESH)
    for o in range(group):
        pl.semaphore_signal(barrier, inc=1, device_id=(after, z * group + mates[o]), device_id_type=MESH)

    @pl.loop(0, chunks)
    def _(c):
        for a in range(4):
            load(c, a).start()

    order = packing_ref[0]
    unpack_ref[...] = one_hot(order, 0, (128, 128))
    pack_ref[...] = one_hot(upright(order), 1, (128, 128))
    pl.semaphore_wait(barrier, 2 * group + 3)

    def at_rows(ref, c, start, count):
        if not isinstance(start, int):
            start = pl.multiple_of(start, 16)
        return ref.at[c, :, pl.ds(start, count), :]

    def a2a(c, o, landing):
        return pltpu.make_async_remote_copy(
            src_ref=at_rows(packed, c, mates[o] * rows, rows),
            dst_ref=at_rows(win, c, landing * rows, rows),
            send_sem=a2a_s.at[c, o - 1],
            recv_sem=a2a_r.at[c, o - 1],
            device_id=(t, z * group + mates[o]),
            device_id_type=MESH,
        )

    def outward(c, n):
        first, count, side = PIECES[n]
        return pltpu.make_async_remote_copy(
            src_ref=at_rows(halo, c, first, count),
            dst_ref=at_rows(win, c, 128 + first, count),
            send_sem=halo_s.at[c, n],
            recv_sem=halo_r.at[c, n],
            device_id=(t, sides[side]),
            device_id_type=MESH,
        )

    def homeward(c, n):
        first, count, side = PIECES[n]
        return pltpu.make_async_remote_copy(
            src_ref=at_rows(back_out, c, first, count),
            dst_ref=at_rows(back_in, c, first, count),
            send_sem=back_s.at[c, n],
            recv_sem=back_r.at[c, n],
            device_id=(t, sides[(side + 2) % 4]),
            device_id_type=MESH,
        )

    def final(c, o, landing):
        return pltpu.make_async_remote_copy(
            src_ref=at_rows(fin_out, c, mates[o] * rows, rows),
            dst_ref=at_rows(fin_in, c, landing * rows, rows),
            send_sem=fin_s.at[c, o],
            recv_sem=fin_r.at[c, o],
            device_id=(before, z * group + mates[o]),
            device_id_type=MESH,
        )

    unpack_copy = pltpu.make_async_remote_copy(
        src_ref=unpack_ref, dst_ref=unpack_in, send_sem=un_s, recv_sem=un_r,
        device_id=(before, me), device_id_type=MESH,
    )
    unpack_copy.start()

    lead = (2, 2, 4, 6, 8)

    def hand_out(c):
        for a in range(4):
            load(c, a).wait()
            packed[c, a] = dot_nn(pack_ref[...], loaded[c, a]).astype(jnp.bfloat16)
        for o in range(1, group):
            a2a(c, o, j).start()
        own = pl.ds(pl.multiple_of(j * rows, 16), rows)
        for a in range(4):
            win[c, a, own, :] = packed[c, a, own, :]
            win[c, a, 224:256, :] = jnp.zeros((32, CHUNK), jnp.bfloat16)

    @pl.loop(0, lead[0])
    def _(c):
        hand_out(c)

    slots, kept, foreign = boundary_plan(ids_ref, blocks, planes, z, j)
    pick_ref[...] = one_hot(slots, 0, (96, 128))
    place_ref[...] = one_hot(upright(slots), 1, (128, 96))
    id_row = jnp.concatenate([kept, foreign], axis=1)
    id_col = jnp.concatenate([upright(kept), upright(foreign)], axis=0)
    id_col = id_col[0:224]
    bias[...] = jnp.where((id_col == id_row) & (id_row >= 0), 0.0, NEG)
    valid[...] = jnp.where(id_col >= 0, 1.0, 0.0)
    scale = HEAD_DIM ** (-0.5)

    def spread(c):
        for o in range(1, group):
            a2a(c, o, sources[o]).wait_recv()
        for a in range(4):
            halo[c, a] = dot_nn(pick_ref[...], win[c, a, 0:128, :]).astype(jnp.bfloat16)
        for n in range(4):
            outward(c, n).start()

    def attend(c):
        for n in range(4):
            outward(c, n).wait_recv()
        for h in range(CHUNK // HEAD_DIM):
            head = slice(h * HEAD_DIM, (h + 1) * HEAD_DIM)
            q, g = [win[c, a, 0:224, head] for a in (0, 3)]
            k, v = [win[c, a, :, head] for a in (1, 2)]
            s = dot_nt(q, k) * scale + bias[...]
            e = jnp.exp(s - jnp.max(s, axis=1, keepdims=True))
            p = e * (valid[...] / jnp.sum(e, axis=1, keepdims=True))
            low = p.astype(jnp.bfloat16)
            dp = dot_nt(g, v)
            delta = jnp.sum(low.astype(jnp.float32) * dp, axis=1, keepdims=True)
            ds = (p * (dp - delta) * scale).astype(jnp.bfloat16)
            for a, grad in enumerate((dot_nn(ds, k), dot_tn(ds, q), dot_tn(low, g))):
                grad = grad.astype(jnp.bfloat16)
                fin_out[c, a, :, head] = grad[0:128]
                back_out[c, a, :, head] = grad[128:224]
        for n in range(4):
            homeward(c, n).start()

    def hand_on(c):
        for n in range(4):
            homeward(c, n).wait_recv()
        for a in range(3):
            returned = dot_nn(place_ref[...], back_in[c, a])
            fin_out[c, a] = (fin_out[c, a].astype(jnp.float32) + returned).astype(jnp.bfloat16)
        for o in range(group):
            final(c, o, j).start()

    def finish(c):
        for o in range(group):
            final(c, o, sources[o]).wait_recv()
        for a in range(3):
            out_ref[0, :, columns(a * width + c * CHUNK)] = dot_nn(
                unpack_in[...], fin_in[c, a]
            ).astype(jnp.bfloat16)

    stages = (hand_out, spread, attend, hand_on, finish)

    @pl.loop(lead[0], chunks + lead[4])
    def _(step):
        @pl.when(step == lead[4])
        def _():
            unpack_copy.wait_recv()

        for n, stage in enumerate(stages):
            late = lead[n] if n > 0 else 0

            @pl.when((step >= late) & (step < chunks + late))
            def _():
                stage(step - late)

    unpack_copy.wait_send()

    @pl.loop(0, chunks)
    def _(c):
        for o in range(1, group):
            a2a(c, o, j).wait_send()
        for n in range(4):
            outward(c, n).wait_send()
            homeward(c, n).wait_send()
        for o in range(group):
            final(c, o, j).wait_send()


def fused_body(sections, queries, key_cells, value_cells, grad_cells, packing, segment_ids):
    cell_count, width = queries.shape[1:]
    devices = lax.axis_size("dp")
    group = devices // 4
    planes = devices // group
    chunks = width // CHUNK
    vmem = pl.BlockSpec(memory_space=pltpu.VMEM)
    far = pl.BlockSpec(memory_space=pl.ANY)
    bf16 = jnp.bfloat16
    sem = pltpu.SemaphoreType.DMA
    return pl.pallas_call(
        functools.partial(kernel, group, planes, sections, chunks, width),
        out_shape=jax.ShapeDtypeStruct((1, cell_count, 3 * width), bf16),
        in_specs=[far] * 4 + [vmem] * 2,
        out_specs=vmem,
        scratch_shapes=[
            pltpu.VMEM((chunks, 4, 128, CHUNK), bf16),
            pltpu.VMEM((chunks, 4, 128, CHUNK), bf16),
            pltpu.VMEM((chunks, 4, 256, CHUNK), bf16),
            pltpu.VMEM((chunks, 4, 96, CHUNK), bf16),
            pltpu.VMEM((chunks, 3, 96, CHUNK), bf16),
            pltpu.VMEM((chunks, 3, 96, CHUNK), bf16),
            pltpu.VMEM((chunks, 3, 128, CHUNK), bf16),
            pltpu.VMEM((chunks, 3, 128, CHUNK), bf16),
            pltpu.VMEM((128, 128), bf16),
            pltpu.VMEM((224, 256), jnp.float32),
            pltpu.VMEM((224, 1), jnp.float32),
            pltpu.VMEM((128, 128), bf16),
            pltpu.VMEM((128, 128), bf16),
            pltpu.VMEM((96, 128), bf16),
            pltpu.VMEM((128, 96), bf16),
            pltpu.VMEM((segment_ids.shape[1] // 128 + 8, 128), jnp.int32),
            sem((chunks, 4)),
            sem((chunks, group - 1)), sem((chunks, group - 1)),
            sem((chunks, 4)), sem((chunks, 4)),
            sem((chunks, 4)), sem((chunks, 4)),
            sem((chunks, group)), sem((chunks, group)),
            sem, sem,
        ],
        compiler_params=pltpu.CompilerParams(
            collective_id=0, has_side_effects=True, vmem_limit_bytes=60 * 1024 * 1024
        ),
    )(queries, key_cells, value_cells, grad_cells, packing, segment_ids)


def solution(mesh):
    sections, devices = mesh.shape["section"], mesh.shape["dp"]

    def body_of(queries, *rest):
        fits = queries.shape[1] == 128 and queries.shape[2] % CHUNK == 0 and devices == 16
        if fits:
            return fused_body(sections, queries, *rest)
        return body(queries, *rest)

    return jax.shard_map(
        body_of,
        mesh=mesh,
        in_specs=(
            P("section", "dp", None),
            P("section", "dp", None),
            P("section", "dp", None),
            P("section", "dp", None),
            P("section", "dp", None),
            P("section", None),
        ),
        out_specs=P("section", "dp", None),
        check_vma=False,
    )
```

```python
import functools
import jax
import jax.numpy as jnp
from jax import lax
from jax.sharding import PartitionSpec as P
from jax.experimental import pallas as pl
from jax.experimental.pallas import tpu as pltpu

HEADS = 20
HEAD_DIM = 128
CHUNK = 256
MESH = pl.DeviceIdType.MESH
NEG = -1e30
GROUPS = 12
INNER, TURN = 40, 32


def with_halo(value, sides, width):
    for axis, dim in sides:
        size, length = (lax.axis_size(axis), value.shape[dim])
        up = [(i, (i + 1) % size) for i in range(size - 1)]
        down = [(j, i) for i, j in up]
        last = lax.slice_in_dim(value, length - width, length, axis=dim)
        initial = lax.slice_in_dim(value, 0, width, axis=dim)
        before = lax.ppermute(last, axis, up)
        after = lax.ppermute(initial, axis, down)
        value = jnp.concatenate([before, value, after], axis=dim)
    return value


def passed_along(value, axis, steps):
    count = lax.axis_size(axis)
    initial, last = (max(0, -steps), min(count, count - steps))
    return lax.ppermute(value, axis, [(source, source + steps) for source in range(initial, last)])


def from_behind(block, axis, distance):
    devices = range(lax.axis_size(axis))
    route = [((i - distance) % len(devices), i) for i in devices]
    return lax.ppermute(block, axis, route)


def heads_of(matrix):
    return matrix.reshape(matrix.shape[0], HEADS, HEAD_DIM)


def masked_scores(query_rows, key_rows, query_ids, key_ids):
    scores = jnp.einsum(
        "ihd,jhd->hij", heads_of(query_rows), heads_of(key_rows), preferred_element_type=jnp.float32
    )
    scores = scores * HEAD_DIM ** (-0.5)
    allowed = (query_ids[:, None] == key_ids[None, :])[None]
    return jnp.where(allowed, scores, -jnp.inf)


def body(queries, key_cells, value_cells, grad_cells, packing, segment_ids):
    cell_count = queries.shape[1]
    width = queries.shape[2]
    groups = lax.axis_size("dp")
    per_peer = cell_count // groups
    reach = cell_count // 4
    place = lax.axis_index("dp")
    scale = HEAD_DIM ** (-0.5)
    order = packing[0, 0]

    def pack(matrix):
        return matrix[0][order].reshape(groups, per_peer, width)

    arrived = (
        lax.all_to_all(pack(queries), "dp", split_axis=0, concat_axis=0, tiled=True),
        lax.all_to_all(pack(key_cells), "dp", split_axis=0, concat_axis=0, tiled=True),
        lax.all_to_all(pack(value_cells), "dp", split_axis=0, concat_axis=0, tiled=True),
        lax.all_to_all(pack(grad_cells), "dp", split_axis=0, concat_axis=0, tiled=True),
    )
    own_q, own_k, own_v, own_g = [piece.reshape(cell_count, width) for piece in arrived]
    rim_ids = jnp.full((reach,), -1, jnp.int32)
    padded_ids = jnp.concatenate([rim_ids, segment_ids[0], rim_ids])
    window_ids = lax.dynamic_slice_in_dim(padded_ids, place * cell_count, cell_count + 2 * reach)
    own_ids = window_ids[reach : reach + cell_count]
    key_value = jnp.concatenate([own_k, own_v], axis=1)
    key_value_window = with_halo(key_value, (("dp", 0),), reach)
    key_window = key_value_window[:, :width]
    value_window = key_value_window[:, width:]
    scores = masked_scores(own_q, key_window, own_ids, window_ids)
    top = jnp.max(scores, axis=2)
    log_total = top + jnp.log(jnp.sum(jnp.exp(scores - top[:, :, None]), axis=2))
    probs = jnp.exp(scores - log_total[:, :, None])
    probs_low = probs.astype(jnp.bfloat16)
    grad_heads = heads_of(own_g)
    attended = jnp.einsum(
        "hij,jhd->ihd", probs_low, heads_of(value_window), preferred_element_type=jnp.float32
    )
    delta = jnp.sum(grad_heads.astype(jnp.float32) * attended, axis=2).T
    dprobs = jnp.einsum(
        "ihd,jhd->hij", grad_heads, heads_of(value_window), preferred_element_type=jnp.float32
    )
    dscores = (probs * (dprobs - delta[:, :, None]) * scale).astype(jnp.bfloat16)
    grad_query = jnp.einsum(
        "hij,jhd->ihd", dscores, heads_of(key_window), preferred_element_type=jnp.float32
    )
    grad_query = grad_query.reshape(cell_count, width).astype(jnp.bfloat16)
    window = cell_count + 2 * reach
    grad_key = jnp.einsum(
        "hij,ihd->jhd", dscores, heads_of(own_q), preferred_element_type=jnp.float32
    )
    grad_value = jnp.einsum(
        "hij,ihd->jhd", probs_low, grad_heads, preferred_element_type=jnp.float32
    )
    partial_value = jnp.concatenate(
        [grad_key.reshape(window, width), grad_value.reshape(window, width)], axis=1
    )
    from_after = passed_along(partial_value[:reach].astype(jnp.bfloat16), "dp", -1).astype(
        jnp.float32
    )
    from_before = passed_along(
        partial_value[reach + cell_count :].astype(jnp.bfloat16), "dp", 1
    ).astype(jnp.float32)
    summed = partial_value[reach : reach + cell_count]
    summed = summed.at[cell_count - reach :].add(from_after)
    summed = summed.at[:reach].add(from_before)
    packed_grads = jnp.concatenate([grad_query, summed.astype(jnp.bfloat16)], axis=1)
    returned = lax.all_to_all(
        packed_grads.reshape(groups, per_peer, 3 * width),
        "dp",
        split_axis=0,
        concat_axis=0,
        tiled=True,
    )
    returned = returned.reshape(cell_count, 3 * width)
    inverse = (
        jnp.zeros((cell_count,), jnp.int32).at[order].set(jnp.arange(cell_count, dtype=jnp.int32))
    )
    loaded_order = returned[inverse]
    handed = from_behind(loaded_order, "section", -1)
    return handed[None]


def dot_nt(a, b):
    return lax.dot_general(a, b, (((1,), (1,)), ((), ())), preferred_element_type=jnp.float32)


def dot_tn(a, b):
    return lax.dot_general(a, b, (((0,), (0,)), ((), ())), preferred_element_type=jnp.float32)


def dot_nn(a, b):
    return jnp.dot(a, b, preferred_element_type=jnp.float32)


def one_hot(index, dim, shape):
    return jnp.where(lax.broadcasted_iota(jnp.int32, shape, dim) == index, 1.0, 0.0).astype(jnp.bfloat16)


def small(x):
    return x.astype(jnp.float32).astype(jnp.bfloat16)


def upright(row):
    eye = one_hot(lax.broadcasted_iota(jnp.int32, (1, 128), 1), 0, (128, 128))
    column = dot_nt(eye, small(jnp.broadcast_to(row, (16, 128))))
    return column[:, 0:1].astype(jnp.int32)


def directions(tails, heads, turn):
    subset = lax.broadcasted_iota(jnp.int32, (4, 128), 1)
    number = lax.broadcasted_iota(jnp.int32, (4, 128), 0)
    chosen = jnp.where(number == 0, subset, jnp.where(number == 1, subset // 2, subset // 4))
    chosen = jnp.where(number == 3, subset // 8, chosen) % 2
    right, left = chosen * tails, (1 - chosen) * heads

    def total(x, rows):
        return sum(x[i : i + 1] for i in rows)

    inner = (total(right, range(4)) <= INNER) & (total(left, range(4)) <= INNER)
    turned = (total(right, range(3)) <= TURN) & (total(left, range(3)) <= TURN)
    turned = turned & (right[3:4] <= 16) & (left[3:4] <= 16)
    fits = jnp.where(turn, turned.astype(jnp.int32), inner.astype(jnp.int32))
    best = jnp.where((fits == 1) & (subset[0:1] < 16), subset[0:1], 16).astype(jnp.float32)
    best = jnp.min(best, axis=1, keepdims=True).astype(jnp.int32)
    picked = subset == best

    def at_best(x):
        return jnp.sum(jnp.where(picked, x, 0).astype(jnp.float32), axis=1, keepdims=True).astype(jnp.int32)

    go, right, left = at_best(chosen), at_best(right), at_best(left)

    def first_slots(x):
        starts = [jnp.zeros_like(x[0:1])]
        for i in range(3):
            starts.append(starts[i] + x[i : i + 1])
        starts[3] = jnp.where(turn, TURN, starts[3])
        return jnp.concatenate(starts, axis=0)

    return go, first_slots(right), first_slots(left)


def boundary_plan(ids_ref, blocks, planes, z, j):
    reach = 128 // 4
    count = ids_ref.shape[1] // 128
    blocks[...] = jnp.full(blocks.shape, -1, jnp.int32)
    for b in range(count):
        blocks[b + 1 : b + 2, :] = ids_ref[:, b * 128 : (b + 1) * 128]
    here, ahead, behind = [
        jnp.concatenate([blocks[pl.ds(4 * j + k + d, 1), :] for k in range(4)], axis=0) for d in (1, 2, 0)
    ]
    span = 128 // planes
    first_plane, last_plane = z == 0, z == planes - 1
    place = lax.broadcasted_iota(jnp.int32, (4, 128), 1)
    inside = place < reach

    def turned(x, plane):
        return pltpu.roll(x, lax.rem(2 * 128 - plane * span, 128), 1)

    own = turned(here, z)
    prior = turned(jnp.where(first_plane, behind, here), z - 1)
    later = turned(jnp.where(last_plane, ahead, here), z + 1)

    def matching(x, value, straddles):
        hits = jnp.sum(jnp.where(inside & (x == value), 1.0, 0.0), axis=1, keepdims=True)
        return jnp.where(straddles, hits, 0.0).astype(jnp.int32)

    first, last = own[:, 0:1], own[:, reach - 1 : reach]
    before, after = prior[:, reach - 1 : reach], later[:, 0:1]
    tail_r, head_r = [matching(x, last, last == after) for x in (own, later)]
    tail_l, head_l = [matching(x, first, first == before) for x in (prior, own)]
    go_r, right_r, left_r = directions(tail_r, head_r, last_plane)

    def shifted(x, by):
        rows = [x[(i + by) % 4 : (i + by) % 4 + 1] for i in range(4)]
        return jnp.where(first_plane, jnp.concatenate(rows, axis=0), x)

    go_l, right_l, left_l = [
        shifted(x, 3) for x in directions(shifted(tail_l, 1), shifted(head_l, 1), first_plane)
    ]
    sent_r, sent_l = jnp.where(go_r == 1, tail_r, 0), jnp.where(go_l == 0, head_l, 0)
    got_l, got_r = jnp.where(go_l == 1, tail_l, 0), jnp.where(go_r == 0, head_r, 0)
    begin = reach - sent_r
    slots = jnp.where(
        inside & (place >= begin),
        right_r + place - begin,
        jnp.where(place < sent_l, 48 + left_l + place, -1),
    )
    kept = jnp.where(slots >= 0, -1, own)
    lane = lax.broadcasted_iota(jnp.int32, (1, 128), 1)
    route = one_hot(lane // 32 * 8 + lane % 8, 0, (128, 128))
    block = lane // 8 % 4

    def arrival(x):
        moved = dot_nn(small(jnp.concatenate([x] * 4, axis=0)), route)
        total = jnp.zeros((1, 128), jnp.float32)
        for k in range(4):
            total = total + jnp.where(block == k, moved[k : k + 1], 0.0)
        return total.astype(jnp.int32)

    left_hit = (place >= right_l) & (place < right_l + got_l)
    right_hit = (place >= 48 + left_r) & (place < 48 + left_r + got_r)
    foreign = jnp.where(left_hit, first, jnp.where(right_hit, last, -1))
    foreign = jnp.max(foreign.astype(jnp.float32), axis=0, keepdims=True).astype(jnp.int32)
    return arrival(slots), arrival(kept), foreign


def kernel(
    group, planes, sections, chunks, width,
    q_ref, k_ref, v_ref, g_ref, packing_ref, ids_ref,
    out_ref,
    loaded, packed, win, halo, halo_in, back_out, back_in, fin_out, fin_in, unpack_in, bias, valid,
    pack_ref, unpack_ref, pick_ref, place_ref, blocks, load_s,
    a2a_s, a2a_r, halo_s, halo_r, back_s, back_r, fin_s, fin_r, un_s, un_r,
):
    t = lax.axis_index("section")
    me = lax.axis_index("dp")
    z, j = lax.div(me, group), lax.rem(me, group)
    rows = 128 // group
    before = lax.rem(t + sections - 1, sections)
    after = lax.rem(t + 1, sections)
    zr, zl = lax.rem(z + 1, planes), lax.rem(z + planes - 1, planes)
    jr = lax.rem(j + jnp.where(z == planes - 1, 1, 0), group)
    jl = lax.rem(j + group - jnp.where(z == 0, 1, 0), group)
    sides = (zr * group + j, zr * group + jr, zl * group + j, zl * group + jl)
    mates = [lax.rem(j + o, group) for o in range(group)]
    sources = [lax.rem(j + group - o, group) for o in range(group)]

    def columns(start):
        return pl.ds(pl.multiple_of(start, 128), CHUNK)

    def load(c, a):
        ref = (q_ref, k_ref, v_ref, g_ref)[a]
        return pltpu.make_async_copy(ref.at[0, :, columns(c * CHUNK)], loaded.at[c, a], load_s.at[c, a])

    @pl.loop(0, chunks)
    def _(c):
        for n in (5, 11):
            halo_in[c, n] = jnp.zeros(halo_in.shape[2:], jnp.bfloat16)
            back_in[c, n] = jnp.zeros(back_in.shape[2:], jnp.bfloat16)

    barrier = pltpu.get_barrier_semaphore()
    for o in range(1, group):
        pl.semaphore_signal(barrier, inc=1, device_id=(t, z * group + mates[o]), device_id_type=MESH)
    for side in sides:
        pl.semaphore_signal(barrier, inc=1, device_id=(t, side), device_id_type=MESH)
    for o in range(group):
        pl.semaphore_signal(barrier, inc=1, device_id=(after, z * group + mates[o]), device_id_type=MESH)

    @pl.loop(0, chunks)
    def _(c):
        for a in range(4):
            load(c, a).start()

    order = packing_ref[0]
    unpack_ref[...] = one_hot(order, 0, (128, 128))
    pack_ref[...] = one_hot(upright(order), 1, (128, 128))
    pl.semaphore_wait(barrier, 2 * group + 3)

    def at_rows(ref, c, start, count):
        if not isinstance(start, int):
            start = pl.multiple_of(start, 16)
        return ref.at[c, :, pl.ds(start, count), :]

    def a2a(c, o, landing):
        return pltpu.make_async_remote_copy(
            src_ref=at_rows(packed, c, mates[o] * rows, rows),
            dst_ref=at_rows(win, c, landing * rows, rows),
            send_sem=a2a_s.at[c, o - 1],
            recv_sem=a2a_r.at[c, o - 1],
            device_id=(t, z * group + mates[o]),
            device_id_type=MESH,
        )

    last_plane, first_plane = z == planes - 1, z == 0
    right_a, right_b, left_a, left_b = sides
    rightward = (((0, 5, 0, right_a),), ((0, 4, 0, right_a), (4, 2, 1, right_b)))
    leftward = (((6, 5, 2, left_a),), ((6, 4, 2, left_a), (10, 2, 3, left_b)))
    returned_left = (((0, 5, 0, left_a),), ((0, 4, 0, left_a), (4, 2, 1, left_b)))
    returned_right = (((6, 5, 2, right_a),), ((6, 4, 2, right_a), (10, 2, 3, right_b)))

    def each(copies, turn, act):
        for n in range(2):
            @pl.when(turn if n == 1 else jnp.logical_not(turn))
            def _():
                for copy in copies[n]:
                    act(*copy)

    def outward(c, act):
        def one(first, count, n, target):
            act(pltpu.make_async_remote_copy(
                src_ref=halo.at[c, pl.ds(first, count)],
                dst_ref=halo_in.at[c, pl.ds(first, count)],
                send_sem=halo_s.at[c, n],
                recv_sem=halo_r.at[c, n],
                device_id=(t, target),
                device_id_type=MESH,
            ))
        return one

    def homeward(c, act):
        def one(first, count, n, target):
            act(pltpu.make_async_remote_copy(
                src_ref=back_out.at[c, pl.ds(first, count)],
                dst_ref=back_in.at[c, pl.ds(first, count)],
                send_sem=back_s.at[c, n],
                recv_sem=back_r.at[c, n],
                device_id=(t, target),
                device_id_type=MESH,
            ))
        return one

    def start(copy):
        copy.start()

    def landed(copy):
        copy.wait_recv()

    def gone(copy):
        copy.wait_send()

    def outward_sends(c, act):
        each(rightward, last_plane, outward(c, act))
        each(leftward, first_plane, outward(c, act))

    def outward_arrivals(c):
        each(returned_left, first_plane, outward(c, landed))
        each(returned_right, last_plane, outward(c, landed))

    def homeward_sends(c, act):
        each(returned_left, first_plane, homeward(c, act))
        each(returned_right, last_plane, homeward(c, act))

    def homeward_arrivals(c):
        each(rightward, last_plane, homeward(c, landed))
        each(leftward, first_plane, homeward(c, landed))

    def final(c, o, landing):
        return pltpu.make_async_remote_copy(
            src_ref=at_rows(fin_out, c, mates[o] * rows, rows),
            dst_ref=at_rows(fin_in, c, landing * rows, rows),
            send_sem=fin_s.at[c, o],
            recv_sem=fin_r.at[c, o],
            device_id=(before, z * group + mates[o]),
            device_id_type=MESH,
        )

    unpack_copy = pltpu.make_async_remote_copy(
        src_ref=unpack_ref, dst_ref=unpack_in, send_sem=un_s, recv_sem=un_r,
        device_id=(before, me), device_id_type=MESH,
    )
    unpack_copy.start()

    lead = (2, 2, 4, 6, 8)

    def hand_out(c):
        for a in range(4):
            load(c, a).wait()
            packed[c, a] = dot_nn(pack_ref[...], loaded[c, a]).astype(jnp.bfloat16)
        for o in range(1, group):
            a2a(c, o, j).start()
        own = pl.ds(pl.multiple_of(j * rows, 16), rows)
        for a in range(4):
            win[c, a, own, :] = packed[c, a, own, :]
            win[c, a, 224:256, :] = jnp.zeros((32, CHUNK), jnp.bfloat16)

    @pl.loop(0, lead[0])
    def _(c):
        hand_out(c)

    slots, kept, foreign = boundary_plan(ids_ref, blocks, planes, z, j)
    pick_ref[...] = one_hot(slots, 0, (96, 128))
    place_ref[...] = one_hot(upright(slots), 1, (128, 96))
    id_row = jnp.concatenate([kept, foreign], axis=1)
    id_col = jnp.concatenate([upright(kept), upright(foreign)], axis=0)
    id_col = id_col[0:224]
    bias[...] = jnp.where((id_col == id_row) & (id_row >= 0), 0.0, NEG)
    valid[...] = jnp.where(id_col >= 0, 1.0, 0.0)
    scale = HEAD_DIM ** (-0.5)

    def spread(c):
        for o in range(1, group):
            a2a(c, o, sources[o]).wait_recv()
        picked = [
            dot_nn(pick_ref[...], win[c, a, 0:128, :]).reshape(GROUPS, 8, CHUNK) for a in range(4)
        ]
        for a in (0, 2):
            pair = jnp.concatenate(picked[a : a + 2], axis=1)
            halo[c, :, a * 8 : a * 8 + 16, :] = pair.astype(jnp.bfloat16)
        outward_sends(c, start)

    def attend(c):
        outward_arrivals(c)
        for a in (0, 2):
            pair = halo_in[c, :, a * 8 : a * 8 + 16, :].astype(jnp.float32)
            for n in range(2):
                cells = pair[:, n * 8 : n * 8 + 8].reshape(GROUPS * 8, CHUNK)
                win[c, a + n, 128:224, :] = cells.astype(jnp.bfloat16)
        foreign = []
        for h in range(CHUNK // HEAD_DIM):
            head = slice(h * HEAD_DIM, (h + 1) * HEAD_DIM)
            q, g = [win[c, a, 0:224, head] for a in (0, 3)]
            k, v = [win[c, a, :, head] for a in (1, 2)]
            s = dot_nt(q, k) * scale + bias[...]
            e = jnp.exp(s - jnp.max(s, axis=1, keepdims=True))
            p = e * (valid[...] / jnp.sum(e, axis=1, keepdims=True))
            low = p.astype(jnp.bfloat16)
            dp = dot_nt(g, v)
            delta = jnp.sum(low.astype(jnp.float32) * dp, axis=1, keepdims=True)
            ds = (p * (dp - delta) * scale).astype(jnp.bfloat16)
            for a, grad in enumerate((dot_nn(ds, k), dot_tn(ds, q), dot_tn(low, g))):
                fin_out[c, a, :, head] = grad[0:128].astype(jnp.bfloat16)
                foreign.append(grad[128:224].reshape(GROUPS, 8, HEAD_DIM))
                if len(foreign) % 2 == 0:
                    pair = jnp.concatenate(foreign[-2:], axis=1)
                    last = len(foreign) * 8
                    back_out[c, :, last - 16 : last, :] = pair.astype(jnp.bfloat16)
        homeward_sends(c, start)

    def hand_on(c):
        homeward_arrivals(c)
        foreign = []
        for n in range(0, 3 * CHUNK // HEAD_DIM, 2):
            pair = back_in[c, :, n * 8 : n * 8 + 16, :].astype(jnp.float32)
            for i in range(2):
                foreign.append(pair[:, i * 8 : i * 8 + 8].reshape(GROUPS * 8, HEAD_DIM))
        for a in range(3):
            returned = dot_nn(place_ref[...], jnp.concatenate(foreign[a::3], axis=1).astype(jnp.bfloat16))
            fin_out[c, a] = (fin_out[c, a].astype(jnp.float32) + returned).astype(jnp.bfloat16)
        for o in range(group):
            final(c, o, j).start()

    def finish(c):
        for o in range(group):
            final(c, o, sources[o]).wait_recv()
        for a in range(3):
            out_ref[0, :, columns(a * width + c * CHUNK)] = dot_nn(
                unpack_in[...], fin_in[c, a]
            ).astype(jnp.bfloat16)

    stages = (hand_out, spread, attend, hand_on, finish)

    @pl.loop(lead[0], chunks + lead[4])
    def _(step):
        @pl.when(step == lead[4])
        def _():
            unpack_copy.wait_recv()

        for n, stage in enumerate(stages):
            late = lead[n] if n > 0 else 0

            @pl.when((step >= late) & (step < chunks + late))
            def _():
                stage(step - late)

    unpack_copy.wait_send()

    @pl.loop(0, chunks)
    def _(c):
        for o in range(1, group):
            a2a(c, o, j).wait_send()
        outward_sends(c, gone)
        homeward_sends(c, gone)
        for o in range(group):
            final(c, o, j).wait_send()


def fused_body(sections, queries, key_cells, value_cells, grad_cells, packing, segment_ids):
    cell_count, width = queries.shape[1:]
    devices = lax.axis_size("dp")
    group = devices // 4
    planes = devices // group
    chunks = width // CHUNK
    vmem = pl.BlockSpec(memory_space=pltpu.VMEM)
    far = pl.BlockSpec(memory_space=pl.ANY)
    bf16 = jnp.bfloat16
    sem = pltpu.SemaphoreType.DMA
    return pl.pallas_call(
        functools.partial(kernel, group, planes, sections, chunks, width),
        out_shape=jax.ShapeDtypeStruct((1, cell_count, 3 * width), bf16),
        in_specs=[far] * 4 + [vmem] * 2,
        out_specs=vmem,
        scratch_shapes=[
            pltpu.VMEM((chunks, 4, 128, CHUNK), bf16),
            pltpu.VMEM((chunks, 4, 128, CHUNK), bf16),
            pltpu.VMEM((chunks, 4, 256, CHUNK), bf16),
            pltpu.VMEM((chunks, GROUPS, 32, CHUNK), bf16),
            pltpu.VMEM((chunks, GROUPS, 32, CHUNK), bf16),
            pltpu.VMEM((chunks, GROUPS, 24 * CHUNK // HEAD_DIM, HEAD_DIM), bf16),
            pltpu.VMEM((chunks, GROUPS, 24 * CHUNK // HEAD_DIM, HEAD_DIM), bf16),
            pltpu.VMEM((chunks, 3, 128, CHUNK), bf16),
            pltpu.VMEM((chunks, 3, 128, CHUNK), bf16),
            pltpu.VMEM((128, 128), bf16),
            pltpu.VMEM((224, 256), jnp.float32),
            pltpu.VMEM((224, 1), jnp.float32),
            pltpu.VMEM((128, 128), bf16),
            pltpu.VMEM((128, 128), bf16),
            pltpu.VMEM((96, 128), bf16),
            pltpu.VMEM((128, 96), bf16),
            pltpu.VMEM((segment_ids.shape[1] // 128 + 8, 128), jnp.int32),
            sem((chunks, 4)),
            sem((chunks, group - 1)), sem((chunks, group - 1)),
            sem((chunks, 4)), sem((chunks, 4)),
            sem((chunks, 4)), sem((chunks, 4)),
            sem((chunks, group)), sem((chunks, group)),
            sem, sem,
        ],
        compiler_params=pltpu.CompilerParams(
            collective_id=0, has_side_effects=True, vmem_limit_bytes=60 * 1024 * 1024
        ),
    )(queries, key_cells, value_cells, grad_cells, packing, segment_ids)


def solution(mesh):
    sections, devices = mesh.shape["section"], mesh.shape["dp"]

    def body_of(queries, *rest):
        fits = queries.shape[1] == 128 and queries.shape[2] % CHUNK == 0 and devices == 16
        if fits:
            return fused_body(sections, queries, *rest)
        return body(queries, *rest)

    return jax.shard_map(
        body_of,
        mesh=mesh,
        in_specs=(
            P("section", "dp", None),
            P("section", "dp", None),
            P("section", "dp", None),
            P("section", "dp", None),
            P("section", "dp", None),
            P("section", None),
        ),
        out_specs=P("section", "dp", None),
        check_vma=False,
    )
```

```python
import functools
import jax
import jax.numpy as jnp
from jax import lax
from jax.sharding import PartitionSpec as P
from jax.experimental import pallas as pl
from jax.experimental.pallas import tpu as pltpu

HEADS = 20
HEAD_DIM = 128
CHUNK = 256
MESH = pl.DeviceIdType.MESH
NEG = -1e30
GROUPS = 12
INNER, TURN = 40, 32


def with_halo(value, sides, width):
    for axis, dim in sides:
        size, length = (lax.axis_size(axis), value.shape[dim])
        up = [(i, (i + 1) % size) for i in range(size - 1)]
        down = [(j, i) for i, j in up]
        last = lax.slice_in_dim(value, length - width, length, axis=dim)
        initial = lax.slice_in_dim(value, 0, width, axis=dim)
        before = lax.ppermute(last, axis, up)
        after = lax.ppermute(initial, axis, down)
        value = jnp.concatenate([before, value, after], axis=dim)
    return value


def passed_along(value, axis, steps):
    count = lax.axis_size(axis)
    initial, last = (max(0, -steps), min(count, count - steps))
    return lax.ppermute(value, axis, [(source, source + steps) for source in range(initial, last)])


def from_behind(block, axis, distance):
    devices = range(lax.axis_size(axis))
    route = [((i - distance) % len(devices), i) for i in devices]
    return lax.ppermute(block, axis, route)


def heads_of(matrix):
    return matrix.reshape(matrix.shape[0], HEADS, HEAD_DIM)


def masked_scores(query_rows, key_rows, query_ids, key_ids):
    scores = jnp.einsum(
        "ihd,jhd->hij", heads_of(query_rows), heads_of(key_rows), preferred_element_type=jnp.float32
    )
    scores = scores * HEAD_DIM ** (-0.5)
    allowed = (query_ids[:, None] == key_ids[None, :])[None]
    return jnp.where(allowed, scores, -jnp.inf)


def body(queries, key_cells, value_cells, grad_cells, packing, segment_ids):
    cell_count = queries.shape[1]
    width = queries.shape[2]
    groups = lax.axis_size("dp")
    per_peer = cell_count // groups
    reach = cell_count // 4
    place = lax.axis_index("dp")
    scale = HEAD_DIM ** (-0.5)
    order = packing[0, 0]

    def pack(matrix):
        return matrix[0][order].reshape(groups, per_peer, width)

    arrived = (
        lax.all_to_all(pack(queries), "dp", split_axis=0, concat_axis=0, tiled=True),
        lax.all_to_all(pack(key_cells), "dp", split_axis=0, concat_axis=0, tiled=True),
        lax.all_to_all(pack(value_cells), "dp", split_axis=0, concat_axis=0, tiled=True),
        lax.all_to_all(pack(grad_cells), "dp", split_axis=0, concat_axis=0, tiled=True),
    )
    own_q, own_k, own_v, own_g = [piece.reshape(cell_count, width) for piece in arrived]
    rim_ids = jnp.full((reach,), -1, jnp.int32)
    padded_ids = jnp.concatenate([rim_ids, segment_ids[0], rim_ids])
    window_ids = lax.dynamic_slice_in_dim(padded_ids, place * cell_count, cell_count + 2 * reach)
    own_ids = window_ids[reach : reach + cell_count]
    key_value = jnp.concatenate([own_k, own_v], axis=1)
    key_value_window = with_halo(key_value, (("dp", 0),), reach)
    key_window = key_value_window[:, :width]
    value_window = key_value_window[:, width:]
    scores = masked_scores(own_q, key_window, own_ids, window_ids)
    top = jnp.max(scores, axis=2)
    log_total = top + jnp.log(jnp.sum(jnp.exp(scores - top[:, :, None]), axis=2))
    probs = jnp.exp(scores - log_total[:, :, None])
    probs_low = probs.astype(jnp.bfloat16)
    grad_heads = heads_of(own_g)
    attended = jnp.einsum(
        "hij,jhd->ihd", probs_low, heads_of(value_window), preferred_element_type=jnp.float32
    )
    delta = jnp.sum(grad_heads.astype(jnp.float32) * attended, axis=2).T
    dprobs = jnp.einsum(
        "ihd,jhd->hij", grad_heads, heads_of(value_window), preferred_element_type=jnp.float32
    )
    dscores = (probs * (dprobs - delta[:, :, None]) * scale).astype(jnp.bfloat16)
    grad_query = jnp.einsum(
        "hij,jhd->ihd", dscores, heads_of(key_window), preferred_element_type=jnp.float32
    )
    grad_query = grad_query.reshape(cell_count, width).astype(jnp.bfloat16)
    window = cell_count + 2 * reach
    grad_key = jnp.einsum(
        "hij,ihd->jhd", dscores, heads_of(own_q), preferred_element_type=jnp.float32
    )
    grad_value = jnp.einsum(
        "hij,ihd->jhd", probs_low, grad_heads, preferred_element_type=jnp.float32
    )
    partial_value = jnp.concatenate(
        [grad_key.reshape(window, width), grad_value.reshape(window, width)], axis=1
    )
    from_after = passed_along(partial_value[:reach].astype(jnp.bfloat16), "dp", -1).astype(
        jnp.float32
    )
    from_before = passed_along(
        partial_value[reach + cell_count :].astype(jnp.bfloat16), "dp", 1
    ).astype(jnp.float32)
    summed = partial_value[reach : reach + cell_count]
    summed = summed.at[cell_count - reach :].add(from_after)
    summed = summed.at[:reach].add(from_before)
    packed_grads = jnp.concatenate([grad_query, summed.astype(jnp.bfloat16)], axis=1)
    returned = lax.all_to_all(
        packed_grads.reshape(groups, per_peer, 3 * width),
        "dp",
        split_axis=0,
        concat_axis=0,
        tiled=True,
    )
    returned = returned.reshape(cell_count, 3 * width)
    inverse = (
        jnp.zeros((cell_count,), jnp.int32).at[order].set(jnp.arange(cell_count, dtype=jnp.int32))
    )
    loaded_order = returned[inverse]
    handed = from_behind(loaded_order, "section", -1)
    return handed[None]


def dot_nt(a, b):
    return lax.dot_general(a, b, (((1,), (1,)), ((), ())), preferred_element_type=jnp.float32)


def dot_tn(a, b):
    return lax.dot_general(a, b, (((0,), (0,)), ((), ())), preferred_element_type=jnp.float32)


def dot_nn(a, b):
    return jnp.dot(a, b, preferred_element_type=jnp.float32)


def one_hot(index, dim, shape):
    return jnp.where(lax.broadcasted_iota(jnp.int32, shape, dim) == index, 1.0, 0.0).astype(jnp.bfloat16)


def small(x):
    return x.astype(jnp.float32).astype(jnp.bfloat16)


def upright(row):
    eye = one_hot(lax.broadcasted_iota(jnp.int32, (1, 128), 1), 0, (128, 128))
    column = dot_nt(eye, small(jnp.broadcast_to(row, (16, 128))))
    return column[:, 0:1].astype(jnp.int32)


def directions(tails, heads, turn):
    subset = lax.broadcasted_iota(jnp.int32, (4, 128), 1)
    number = lax.broadcasted_iota(jnp.int32, (4, 128), 0)
    chosen = jnp.where(number == 0, subset, jnp.where(number == 1, subset // 2, subset // 4))
    chosen = jnp.where(number == 3, subset // 8, chosen) % 2
    right, left = chosen * tails, (1 - chosen) * heads

    def total(x, rows):
        return sum(x[i : i + 1] for i in rows)

    inner = (total(right, range(4)) <= INNER) & (total(left, range(4)) <= INNER)
    turned = (total(right, range(3)) <= TURN) & (total(left, range(3)) <= TURN)
    turned = turned & (right[3:4] <= 16) & (left[3:4] <= 16)
    fits = jnp.where(turn, turned.astype(jnp.int32), inner.astype(jnp.int32))
    best = jnp.where((fits == 1) & (subset[0:1] < 16), subset[0:1], 16).astype(jnp.float32)
    best = jnp.min(best, axis=1, keepdims=True).astype(jnp.int32)
    picked = subset == best

    def at_best(x):
        return jnp.sum(jnp.where(picked, x, 0).astype(jnp.float32), axis=1, keepdims=True).astype(jnp.int32)

    go, right, left = at_best(chosen), at_best(right), at_best(left)

    def first_slots(x):
        starts = [jnp.zeros_like(x[0:1])]
        for i in range(3):
            starts.append(starts[i] + x[i : i + 1])
        starts[3] = jnp.where(turn, TURN, starts[3])
        return jnp.concatenate(starts, axis=0)

    return go, first_slots(right), first_slots(left)


def boundary_plan(ids_ref, blocks, planes, z, j):
    reach = 128 // 4
    count = ids_ref.shape[1] // 128
    blocks[...] = jnp.full(blocks.shape, -1, jnp.int32)
    for b in range(count):
        blocks[b + 1 : b + 2, :] = ids_ref[:, b * 128 : (b + 1) * 128]
    here, ahead, behind = [
        jnp.concatenate([blocks[pl.ds(4 * j + k + d, 1), :] for k in range(4)], axis=0) for d in (1, 2, 0)
    ]
    span = 128 // planes
    first_plane, last_plane = z == 0, z == planes - 1
    place = lax.broadcasted_iota(jnp.int32, (4, 128), 1)
    inside = place < reach

    def turned(x, plane):
        return pltpu.roll(x, lax.rem(2 * 128 - plane * span, 128), 1)

    own = turned(here, z)
    prior = turned(jnp.where(first_plane, behind, here), z - 1)
    later = turned(jnp.where(last_plane, ahead, here), z + 1)

    def matching(x, value, straddles):
        hits = jnp.sum(jnp.where(inside & (x == value), 1.0, 0.0), axis=1, keepdims=True)
        return jnp.where(straddles, hits, 0.0).astype(jnp.int32)

    first, last = own[:, 0:1], own[:, reach - 1 : reach]
    before, after = prior[:, reach - 1 : reach], later[:, 0:1]
    tail_r, head_r = [matching(x, last, last == after) for x in (own, later)]
    tail_l, head_l = [matching(x, first, first == before) for x in (prior, own)]
    go_r, right_r, left_r = directions(tail_r, head_r, last_plane)

    def shifted(x, by):
        rows = [x[(i + by) % 4 : (i + by) % 4 + 1] for i in range(4)]
        return jnp.where(first_plane, jnp.concatenate(rows, axis=0), x)

    go_l, right_l, left_l = [
        shifted(x, 3) for x in directions(shifted(tail_l, 1), shifted(head_l, 1), first_plane)
    ]
    sent_r, sent_l = jnp.where(go_r == 1, tail_r, 0), jnp.where(go_l == 0, head_l, 0)
    got_l, got_r = jnp.where(go_l == 1, tail_l, 0), jnp.where(go_r == 0, head_r, 0)
    begin = reach - sent_r
    slots = jnp.where(
        inside & (place >= begin),
        right_r + place - begin,
        jnp.where(place < sent_l, 48 + left_l + place, -1),
    )
    kept = jnp.where(slots >= 0, -1, own)
    lane = lax.broadcasted_iota(jnp.int32, (1, 128), 1)
    route = one_hot(lane // 32 * 8 + lane % 8, 0, (128, 128))
    block = lane // 8 % 4

    def arrival(x):
        moved = dot_nn(small(jnp.concatenate([x] * 4, axis=0)), route)
        total = jnp.zeros((1, 128), jnp.float32)
        for k in range(4):
            total = total + jnp.where(block == k, moved[k : k + 1], 0.0)
        return total.astype(jnp.int32)

    left_hit = (place >= right_l) & (place < right_l + got_l)
    right_hit = (place >= 48 + left_r) & (place < 48 + left_r + got_r)
    foreign = jnp.where(left_hit, first, jnp.where(right_hit, last, -1))
    foreign = jnp.max(foreign.astype(jnp.float32), axis=0, keepdims=True).astype(jnp.int32)
    return arrival(slots), arrival(kept), foreign


def kernel(
    group, planes, sections, chunks, width,
    q_ref, k_ref, v_ref, g_ref, packing_ref, ids_ref,
    fin_in, unpack_in,
    loaded, packed, win, halo, halo_in, back_out, back_in, fin_out, bias, valid,
    pack_ref, unpack_ref, pick_ref, place_ref, blocks, load_s,
    a2a_s, a2a_r, halo_s, halo_r, back_s, back_r, fin_s, fin_r, un_s, un_r,
):
    t = lax.axis_index("section")
    me = lax.axis_index("dp")
    z, j = lax.div(me, group), lax.rem(me, group)
    rows = 128 // group
    before = lax.rem(t + sections - 1, sections)
    after = lax.rem(t + 1, sections)
    zr, zl = lax.rem(z + 1, planes), lax.rem(z + planes - 1, planes)
    jr = lax.rem(j + jnp.where(z == planes - 1, 1, 0), group)
    jl = lax.rem(j + group - jnp.where(z == 0, 1, 0), group)
    sides = (zr * group + j, zr * group + jr, zl * group + j, zl * group + jl)
    mates = [lax.rem(j + o, group) for o in range(group)]
    sources = [lax.rem(j + group - o, group) for o in range(group)]

    def columns(start):
        return pl.ds(pl.multiple_of(start, 128), CHUNK)

    def load(c, a):
        ref = (q_ref, k_ref, v_ref, g_ref)[a]
        return pltpu.make_async_copy(ref.at[0, :, columns(c * CHUNK)], loaded.at[c, a], load_s.at[c, a])

    @pl.loop(0, chunks)
    def _(c):
        for n in (5, 11):
            halo_in[c, n] = jnp.zeros(halo_in.shape[2:], jnp.bfloat16)
            back_in[c, n] = jnp.zeros(back_in.shape[2:], jnp.bfloat16)

    for a in range(4):
        load(0, a).start()

    barrier = pltpu.get_barrier_semaphore()
    for o in range(1, group):
        pl.semaphore_signal(barrier, inc=1, device_id=(t, z * group + mates[o]), device_id_type=MESH)
    for side in sides:
        pl.semaphore_signal(barrier, inc=1, device_id=(t, side), device_id_type=MESH)
    for o in range(group):
        pl.semaphore_signal(barrier, inc=1, device_id=(after, z * group + mates[o]), device_id_type=MESH)

    @pl.loop(1, chunks)
    def _(c):
        for a in range(4):
            load(c, a).start()

    order = packing_ref[0]
    unpack_ref[...] = one_hot(order, 0, (128, 128))
    pack_ref[...] = one_hot(upright(order), 1, (128, 128))
    pl.semaphore_wait(barrier, 2 * group + 3)

    def at_rows(ref, c, start, count):
        if not isinstance(start, int):
            start = pl.multiple_of(start, 16)
        return ref.at[c, :, pl.ds(start, count), :]

    def a2a(c, o, landing):
        return pltpu.make_async_remote_copy(
            src_ref=at_rows(packed, c, mates[o] * rows, rows),
            dst_ref=at_rows(win, c, landing * rows, rows),
            send_sem=a2a_s.at[c, o - 1],
            recv_sem=a2a_r.at[c, o - 1],
            device_id=(t, z * group + mates[o]),
            device_id_type=MESH,
        )

    last_plane, first_plane = z == planes - 1, z == 0
    right_a, right_b, left_a, left_b = sides
    rightward = (((0, 5, 0, right_a),), ((0, 4, 0, right_a), (4, 2, 1, right_b)))
    leftward = (((6, 5, 2, left_a),), ((6, 4, 2, left_a), (10, 2, 3, left_b)))
    returned_left = (((0, 5, 0, left_a),), ((0, 4, 0, left_a), (4, 2, 1, left_b)))
    returned_right = (((6, 5, 2, right_a),), ((6, 4, 2, right_a), (10, 2, 3, right_b)))

    def each(copies, turn, act):
        for n in range(2):
            @pl.when(turn if n == 1 else jnp.logical_not(turn))
            def _():
                for copy in copies[n]:
                    act(*copy)

    def outward(c, act):
        def one(first, count, n, target):
            act(pltpu.make_async_remote_copy(
                src_ref=halo.at[c, pl.ds(first, count)],
                dst_ref=halo_in.at[c, pl.ds(first, count)],
                send_sem=halo_s.at[c, n],
                recv_sem=halo_r.at[c, n],
                device_id=(t, target),
                device_id_type=MESH,
            ))
        return one

    def homeward(c, act):
        def one(first, count, n, target):
            act(pltpu.make_async_remote_copy(
                src_ref=back_out.at[c, pl.ds(first, count)],
                dst_ref=back_in.at[c, pl.ds(first, count)],
                send_sem=back_s.at[c, n],
                recv_sem=back_r.at[c, n],
                device_id=(t, target),
                device_id_type=MESH,
            ))
        return one

    def start(copy):
        copy.start()

    def landed(copy):
        copy.wait_recv()

    def gone(copy):
        copy.wait_send()

    def outward_sends(c, act):
        each(rightward, last_plane, outward(c, act))
        each(leftward, first_plane, outward(c, act))

    def outward_arrivals(c):
        each(returned_left, first_plane, outward(c, landed))
        each(returned_right, last_plane, outward(c, landed))

    def homeward_sends(c, act):
        each(returned_left, first_plane, homeward(c, act))
        each(returned_right, last_plane, homeward(c, act))

    def homeward_arrivals(c):
        each(rightward, last_plane, homeward(c, landed))
        each(leftward, first_plane, homeward(c, landed))

    def final(c, o, landing):
        return pltpu.make_async_remote_copy(
            src_ref=at_rows(fin_out, c, mates[o] * rows, rows),
            dst_ref=at_rows(fin_in, c, landing * rows, rows),
            send_sem=fin_s.at[c, o],
            recv_sem=fin_r.at[c, o],
            device_id=(before, z * group + mates[o]),
            device_id_type=MESH,
        )

    unpack_copy = pltpu.make_async_remote_copy(
        src_ref=unpack_ref, dst_ref=unpack_in, send_sem=un_s, recv_sem=un_r,
        device_id=(before, me), device_id_type=MESH,
    )
    unpack_copy.start()

    def hand_out(c):
        for a in range(4):
            load(c, a).wait()
            packed[c, a] = dot_nn(pack_ref[...], loaded[c, a]).astype(jnp.bfloat16)
        for o in range(1, group):
            a2a(c, o, j).start()
        own = pl.ds(pl.multiple_of(j * rows, 16), rows)
        for a in range(4):
            win[c, a, own, :] = packed[c, a, own, :]
            win[c, a, 224:256, :] = jnp.zeros((32, CHUNK), jnp.bfloat16)

    @pl.loop(0, 2)
    def _(c):
        hand_out(c)

    slots, kept, foreign = boundary_plan(ids_ref, blocks, planes, z, j)
    pick_ref[...] = one_hot(slots, 0, (96, 128))
    place_ref[...] = one_hot(upright(slots), 1, (128, 96))
    id_row = jnp.concatenate([kept, foreign], axis=1)
    id_col = jnp.concatenate([upright(kept), upright(foreign)], axis=0)
    id_col = id_col[0:224]
    bias[...] = jnp.where((id_col == id_row) & (id_row >= 0), 0.0, NEG)
    valid[...] = jnp.where(id_col >= 0, 1.0, 0.0)
    scale = HEAD_DIM ** (-0.5)

    def spread(c):
        for o in range(1, group):
            a2a(c, o, sources[o]).wait_recv()
        picked = [
            dot_nn(pick_ref[...], win[c, a, 0:128, :]).reshape(GROUPS, 8, CHUNK) for a in range(4)
        ]
        for a in (0, 2):
            pair = jnp.concatenate(picked[a : a + 2], axis=1)
            halo[c, :, a * 8 : a * 8 + 16, :] = pair.astype(jnp.bfloat16)
        outward_sends(c, start)

    def attend(c):
        outward_arrivals(c)
        for a in (0, 2):
            pair = halo_in[c, :, a * 8 : a * 8 + 16, :].astype(jnp.float32)
            for n in range(2):
                cells = pair[:, n * 8 : n * 8 + 8].reshape(GROUPS * 8, CHUNK)
                win[c, a + n, 128:224, :] = cells.astype(jnp.bfloat16)
        foreign = []
        for h in range(CHUNK // HEAD_DIM):
            head = slice(h * HEAD_DIM, (h + 1) * HEAD_DIM)
            q, g = [win[c, a, 0:224, head] for a in (0, 3)]
            k, v = [win[c, a, :, head] for a in (1, 2)]
            s = dot_nt(q, k) * scale + bias[...]
            e = jnp.exp(s - jnp.max(s, axis=1, keepdims=True))
            p = e * (valid[...] / jnp.sum(e, axis=1, keepdims=True))
            low = p.astype(jnp.bfloat16)
            dp = dot_nt(g, v)
            delta = jnp.sum(low.astype(jnp.float32) * dp, axis=1, keepdims=True)
            ds = (p * (dp - delta) * scale).astype(jnp.bfloat16)
            for a, grad in enumerate((dot_nn(ds, k), dot_tn(ds, q), dot_tn(low, g))):
                fin_out[c, a, :, head] = grad[0:128].astype(jnp.bfloat16)
                foreign.append(grad[128:224].reshape(GROUPS, 8, HEAD_DIM))
                if len(foreign) % 2 == 0:
                    pair = jnp.concatenate(foreign[-2:], axis=1)
                    last = len(foreign) * 8
                    back_out[c, :, last - 16 : last, :] = pair.astype(jnp.bfloat16)
        homeward_sends(c, start)

    def hand_on(c):
        homeward_arrivals(c)
        foreign = []
        for n in range(0, 3 * CHUNK // HEAD_DIM, 2):
            pair = back_in[c, :, n * 8 : n * 8 + 16, :].astype(jnp.float32)
            for i in range(2):
                foreign.append(pair[:, i * 8 : i * 8 + 8].reshape(GROUPS * 8, HEAD_DIM))
        for a in range(3):
            returned = dot_nn(place_ref[...], jnp.concatenate(foreign[a::3], axis=1).astype(jnp.bfloat16))
            fin_out[c, a] = (fin_out[c, a].astype(jnp.float32) + returned).astype(jnp.bfloat16)
        for o in range(group):
            final(c, o, j).start()

    stages = (spread, attend, hand_on, hand_out)
    lead = (2, 4, 6, 0)

    @pl.loop(2, chunks + max(lead))
    def _(step):
        for late, stage in zip(lead, stages):

            @pl.when((step >= late) & (step < chunks + late))
            def _():
                stage(step - late)

    unpack_copy.wait()

    @pl.loop(0, chunks)
    def _(c):
        for o in range(1, group):
            a2a(c, o, j).wait_send()
        outward_sends(c, gone)
        homeward_sends(c, gone)
        for o in range(group):
            final(c, o, j).wait_send()
            final(c, o, sources[o]).wait_recv()


def put_in_place(unpack_ref, arrived_ref, out_ref):
    chunks = arrived_ref.shape[0]
    for c in range(chunks):
        rows = dot_nn(unpack_ref[...], arrived_ref[c, 0])
        out_ref[0, :, c * CHUNK : (c + 1) * CHUNK] = rows.astype(jnp.bfloat16)


def fused_body(sections, queries, key_cells, value_cells, grad_cells, packing, segment_ids):
    cell_count, width = queries.shape[1:]
    devices = lax.axis_size("dp")
    group = devices // 4
    planes = devices // group
    chunks = width // CHUNK
    vmem = pl.BlockSpec(memory_space=pltpu.VMEM)
    far = pl.BlockSpec(memory_space=pl.ANY)
    bf16 = jnp.bfloat16
    sem = pltpu.SemaphoreType.DMA
    arrived, unpack = pl.pallas_call(
        functools.partial(kernel, group, planes, sections, chunks, width),
        out_shape=(
            jax.ShapeDtypeStruct((chunks, 3, cell_count, CHUNK), bf16),
            jax.ShapeDtypeStruct((cell_count, cell_count), bf16),
        ),
        in_specs=[far] * 4 + [vmem] * 2,
        out_specs=(far, far),
        scratch_shapes=[
            pltpu.VMEM((chunks, 4, 128, CHUNK), bf16),
            pltpu.VMEM((chunks, 4, 128, CHUNK), bf16),
            pltpu.VMEM((chunks, 4, 256, CHUNK), bf16),
            pltpu.VMEM((chunks, GROUPS, 32, CHUNK), bf16),
            pltpu.VMEM((chunks, GROUPS, 32, CHUNK), bf16),
            pltpu.VMEM((chunks, GROUPS, 24 * CHUNK // HEAD_DIM, HEAD_DIM), bf16),
            pltpu.VMEM((chunks, GROUPS, 24 * CHUNK // HEAD_DIM, HEAD_DIM), bf16),
            pltpu.VMEM((chunks, 3, 128, CHUNK), bf16),
            pltpu.VMEM((224, 256), jnp.float32),
            pltpu.VMEM((224, 1), jnp.float32),
            pltpu.VMEM((128, 128), bf16),
            pltpu.VMEM((128, 128), bf16),
            pltpu.VMEM((96, 128), bf16),
            pltpu.VMEM((128, 96), bf16),
            pltpu.VMEM((segment_ids.shape[1] // 128 + 8, 128), jnp.int32),
            sem((chunks, 4)),
            sem((chunks, group - 1)), sem((chunks, group - 1)),
            sem((chunks, 4)), sem((chunks, 4)),
            sem((chunks, 4)), sem((chunks, 4)),
            sem((chunks, group)), sem((chunks, group)),
            sem, sem,
        ],
        compiler_params=pltpu.CompilerParams(
            collective_id=0, has_side_effects=True, vmem_limit_bytes=60 * 1024 * 1024
        ),
    )(queries, key_cells, value_cells, grad_cells, packing, segment_ids)
    return pl.pallas_call(
        put_in_place,
        grid=(3,),
        out_shape=jax.ShapeDtypeStruct((1, cell_count, 3 * width), bf16),
        in_specs=[
            pl.BlockSpec((cell_count, cell_count), lambda a: (0, 0)),
            pl.BlockSpec((chunks, 1, cell_count, CHUNK), lambda a: (0, a, 0, 0)),
        ],
        out_specs=pl.BlockSpec((1, cell_count, width), lambda a: (0, 0, a)),
        compiler_params=pltpu.CompilerParams(vmem_limit_bytes=60 * 1024 * 1024),
    )(unpack, arrived)


def solution(mesh):
    sections, devices = mesh.shape["section"], mesh.shape["dp"]

    def body_of(queries, *rest):
        fits = queries.shape[1] == 128 and queries.shape[2] % CHUNK == 0 and devices == 16
        if fits:
            return fused_body(sections, queries, *rest)
        return body(queries, *rest)

    return jax.shard_map(
        body_of,
        mesh=mesh,
        in_specs=(
            P("section", "dp", None),
            P("section", "dp", None),
            P("section", "dp", None),
            P("section", "dp", None),
            P("section", "dp", None),
            P("section", None),
        ),
        out_specs=P("section", "dp", None),
        check_vma=False,
    )
```

```python
import functools
import jax
import jax.numpy as jnp
from jax import lax
from jax.sharding import PartitionSpec as P
from jax.experimental import pallas as pl
from jax.experimental.pallas import tpu as pltpu

HEADS = 20
HEAD_DIM = 128
CHUNK = 256
MESH = pl.DeviceIdType.MESH
NEG = -1e30
GROUPS = 12
INNER, TURN = 40, 32


def with_halo(value, sides, width):
    for axis, dim in sides:
        size, length = (lax.axis_size(axis), value.shape[dim])
        up = [(i, (i + 1) % size) for i in range(size - 1)]
        down = [(j, i) for i, j in up]
        last = lax.slice_in_dim(value, length - width, length, axis=dim)
        initial = lax.slice_in_dim(value, 0, width, axis=dim)
        before = lax.ppermute(last, axis, up)
        after = lax.ppermute(initial, axis, down)
        value = jnp.concatenate([before, value, after], axis=dim)
    return value


def passed_along(value, axis, steps):
    count = lax.axis_size(axis)
    initial, last = (max(0, -steps), min(count, count - steps))
    return lax.ppermute(value, axis, [(source, source + steps) for source in range(initial, last)])


def from_behind(block, axis, distance):
    devices = range(lax.axis_size(axis))
    route = [((i - distance) % len(devices), i) for i in devices]
    return lax.ppermute(block, axis, route)


def heads_of(matrix):
    return matrix.reshape(matrix.shape[0], HEADS, HEAD_DIM)


def masked_scores(query_rows, key_rows, query_ids, key_ids):
    scores = jnp.einsum(
        "ihd,jhd->hij", heads_of(query_rows), heads_of(key_rows), preferred_element_type=jnp.float32
    )
    scores = scores * HEAD_DIM ** (-0.5)
    allowed = (query_ids[:, None] == key_ids[None, :])[None]
    return jnp.where(allowed, scores, -jnp.inf)


def body(queries, key_cells, value_cells, grad_cells, packing, segment_ids):
    cell_count = queries.shape[1]
    width = queries.shape[2]
    groups = lax.axis_size("dp")
    per_peer = cell_count // groups
    reach = cell_count // 4
    place = lax.axis_index("dp")
    scale = HEAD_DIM ** (-0.5)
    order = packing[0, 0]

    def pack(matrix):
        return matrix[0][order].reshape(groups, per_peer, width)

    arrived = (
        lax.all_to_all(pack(queries), "dp", split_axis=0, concat_axis=0, tiled=True),
        lax.all_to_all(pack(key_cells), "dp", split_axis=0, concat_axis=0, tiled=True),
        lax.all_to_all(pack(value_cells), "dp", split_axis=0, concat_axis=0, tiled=True),
        lax.all_to_all(pack(grad_cells), "dp", split_axis=0, concat_axis=0, tiled=True),
    )
    own_q, own_k, own_v, own_g = [piece.reshape(cell_count, width) for piece in arrived]
    rim_ids = jnp.full((reach,), -1, jnp.int32)
    padded_ids = jnp.concatenate([rim_ids, segment_ids[0], rim_ids])
    window_ids = lax.dynamic_slice_in_dim(padded_ids, place * cell_count, cell_count + 2 * reach)
    own_ids = window_ids[reach : reach + cell_count]
    key_value = jnp.concatenate([own_k, own_v], axis=1)
    key_value_window = with_halo(key_value, (("dp", 0),), reach)
    key_window = key_value_window[:, :width]
    value_window = key_value_window[:, width:]
    scores = masked_scores(own_q, key_window, own_ids, window_ids)
    top = jnp.max(scores, axis=2)
    log_total = top + jnp.log(jnp.sum(jnp.exp(scores - top[:, :, None]), axis=2))
    probs = jnp.exp(scores - log_total[:, :, None])
    probs_low = probs.astype(jnp.bfloat16)
    grad_heads = heads_of(own_g)
    attended = jnp.einsum(
        "hij,jhd->ihd", probs_low, heads_of(value_window), preferred_element_type=jnp.float32
    )
    delta = jnp.sum(grad_heads.astype(jnp.float32) * attended, axis=2).T
    dprobs = jnp.einsum(
        "ihd,jhd->hij", grad_heads, heads_of(value_window), preferred_element_type=jnp.float32
    )
    dscores = (probs * (dprobs - delta[:, :, None]) * scale).astype(jnp.bfloat16)
    grad_query = jnp.einsum(
        "hij,jhd->ihd", dscores, heads_of(key_window), preferred_element_type=jnp.float32
    )
    grad_query = grad_query.reshape(cell_count, width).astype(jnp.bfloat16)
    window = cell_count + 2 * reach
    grad_key = jnp.einsum(
        "hij,ihd->jhd", dscores, heads_of(own_q), preferred_element_type=jnp.float32
    )
    grad_value = jnp.einsum(
        "hij,ihd->jhd", probs_low, grad_heads, preferred_element_type=jnp.float32
    )
    partial_value = jnp.concatenate(
        [grad_key.reshape(window, width), grad_value.reshape(window, width)], axis=1
    )
    from_after = passed_along(partial_value[:reach].astype(jnp.bfloat16), "dp", -1).astype(
        jnp.float32
    )
    from_before = passed_along(
        partial_value[reach + cell_count :].astype(jnp.bfloat16), "dp", 1
    ).astype(jnp.float32)
    summed = partial_value[reach : reach + cell_count]
    summed = summed.at[cell_count - reach :].add(from_after)
    summed = summed.at[:reach].add(from_before)
    packed_grads = jnp.concatenate([grad_query, summed.astype(jnp.bfloat16)], axis=1)
    returned = lax.all_to_all(
        packed_grads.reshape(groups, per_peer, 3 * width),
        "dp",
        split_axis=0,
        concat_axis=0,
        tiled=True,
    )
    returned = returned.reshape(cell_count, 3 * width)
    inverse = (
        jnp.zeros((cell_count,), jnp.int32).at[order].set(jnp.arange(cell_count, dtype=jnp.int32))
    )
    loaded_order = returned[inverse]
    handed = from_behind(loaded_order, "section", -1)
    return handed[None]


def dot_nt(a, b):
    return lax.dot_general(a, b, (((1,), (1,)), ((), ())), preferred_element_type=jnp.float32)


def dot_tn(a, b):
    return lax.dot_general(a, b, (((0,), (0,)), ((), ())), preferred_element_type=jnp.float32)


def dot_nn(a, b):
    return jnp.dot(a, b, preferred_element_type=jnp.float32)


def one_hot(index, dim, shape):
    return jnp.where(lax.broadcasted_iota(jnp.int32, shape, dim) == index, 1.0, 0.0).astype(jnp.bfloat16)


def small(x):
    return x.astype(jnp.float32).astype(jnp.bfloat16)


def upright(row):
    eye = one_hot(lax.broadcasted_iota(jnp.int32, (1, 128), 1), 0, (128, 128))
    column = dot_nt(eye, small(jnp.broadcast_to(row, (16, 128))))
    return column[:, 0:1].astype(jnp.int32)


def directions(tails, heads, turn):
    subset = lax.broadcasted_iota(jnp.int32, (4, 128), 1)
    number = lax.broadcasted_iota(jnp.int32, (4, 128), 0)
    chosen = jnp.where(number == 0, subset, jnp.where(number == 1, subset // 2, subset // 4))
    chosen = jnp.where(number == 3, subset // 8, chosen) % 2
    right, left = chosen * tails, (1 - chosen) * heads

    def total(x, rows):
        return sum(x[i : i + 1] for i in rows)

    inner = (total(right, range(4)) <= INNER) & (total(left, range(4)) <= INNER)
    turned = (total(right, range(3)) <= TURN) & (total(left, range(3)) <= TURN)
    turned = turned & (right[3:4] <= 16) & (left[3:4] <= 16)
    fits = jnp.where(turn, turned.astype(jnp.int32), inner.astype(jnp.int32))
    best = jnp.where((fits == 1) & (subset[0:1] < 16), subset[0:1], 16).astype(jnp.float32)
    best = jnp.min(best, axis=1, keepdims=True).astype(jnp.int32)
    picked = subset == best

    def at_best(x):
        return jnp.sum(jnp.where(picked, x, 0).astype(jnp.float32), axis=1, keepdims=True).astype(jnp.int32)

    go, right, left = at_best(chosen), at_best(right), at_best(left)

    def first_slots(x):
        starts = [jnp.zeros_like(x[0:1])]
        for i in range(3):
            starts.append(starts[i] + x[i : i + 1])
        starts[3] = jnp.where(turn, TURN, starts[3])
        return jnp.concatenate(starts, axis=0)

    return go, first_slots(right), first_slots(left)


def boundary_plan(ids_ref, blocks, planes, z, j):
    reach = 128 // 4
    count = ids_ref.shape[1] // 128
    blocks[...] = jnp.full(blocks.shape, -1, jnp.int32)
    for b in range(count):
        blocks[b + 1 : b + 2, :] = ids_ref[:, b * 128 : (b + 1) * 128]
    here, ahead, behind = [
        jnp.concatenate([blocks[pl.ds(4 * j + k + d, 1), :] for k in range(4)], axis=0) for d in (1, 2, 0)
    ]
    span = 128 // planes
    first_plane, last_plane = z == 0, z == planes - 1
    place = lax.broadcasted_iota(jnp.int32, (4, 128), 1)
    inside = place < reach

    def turned(x, plane):
        return pltpu.roll(x, lax.rem(2 * 128 - plane * span, 128), 1)

    own = turned(here, z)
    prior = turned(jnp.where(first_plane, behind, here), z - 1)
    later = turned(jnp.where(last_plane, ahead, here), z + 1)

    def matching(x, value, straddles):
        hits = jnp.sum(jnp.where(inside & (x == value), 1.0, 0.0), axis=1, keepdims=True)
        return jnp.where(straddles, hits, 0.0).astype(jnp.int32)

    first, last = own[:, 0:1], own[:, reach - 1 : reach]
    before, after = prior[:, reach - 1 : reach], later[:, 0:1]
    tail_r, head_r = [matching(x, last, last == after) for x in (own, later)]
    tail_l, head_l = [matching(x, first, first == before) for x in (prior, own)]
    go_r, right_r, left_r = directions(tail_r, head_r, last_plane)

    def shifted(x, by):
        rows = [x[(i + by) % 4 : (i + by) % 4 + 1] for i in range(4)]
        return jnp.where(first_plane, jnp.concatenate(rows, axis=0), x)

    go_l, right_l, left_l = [
        shifted(x, 3) for x in directions(shifted(tail_l, 1), shifted(head_l, 1), first_plane)
    ]
    sent_r, sent_l = jnp.where(go_r == 1, tail_r, 0), jnp.where(go_l == 0, head_l, 0)
    got_l, got_r = jnp.where(go_l == 1, tail_l, 0), jnp.where(go_r == 0, head_r, 0)
    begin = reach - sent_r
    slots = jnp.where(
        inside & (place >= begin),
        right_r + place - begin,
        jnp.where(place < sent_l, 48 + left_l + place, -1),
    )
    kept = jnp.where(slots >= 0, -1, own)
    lane = lax.broadcasted_iota(jnp.int32, (1, 128), 1)
    route = one_hot(lane // 32 * 8 + lane % 8, 0, (128, 128))
    block = lane // 8 % 4

    def arrival(x):
        moved = dot_nn(small(jnp.concatenate([x] * 4, axis=0)), route)
        total = jnp.zeros((1, 128), jnp.float32)
        for k in range(4):
            total = total + jnp.where(block == k, moved[k : k + 1], 0.0)
        return total.astype(jnp.int32)

    left_hit = (place >= right_l) & (place < right_l + got_l)
    right_hit = (place >= 48 + left_r) & (place < 48 + left_r + got_r)
    foreign = jnp.where(left_hit, first, jnp.where(right_hit, last, -1))
    foreign = jnp.max(foreign.astype(jnp.float32), axis=0, keepdims=True).astype(jnp.int32)
    return arrival(slots), arrival(kept), foreign


def kernel(
    group, planes, sections, chunks, width,
    q_ref, k_ref, v_ref, g_ref, packing_ref, ids_ref,
    out_ref,
    loaded, packed, win, halo, halo_in, back_out, back_in, fin_out, fin_in, unpack_in, placed, bias, valid,
    pack_ref, unpack_ref, pick_ref, place_ref, blocks, load_s,
    a2a_s, a2a_r, halo_s, halo_r, back_s, back_r, fin_s, fin_r, un_s, un_r, put_s,
):
    t = lax.axis_index("section")
    me = lax.axis_index("dp")
    z, j = lax.div(me, group), lax.rem(me, group)
    rows = 128 // group
    before = lax.rem(t + sections - 1, sections)
    after = lax.rem(t + 1, sections)
    zr, zl = lax.rem(z + 1, planes), lax.rem(z + planes - 1, planes)
    jr = lax.rem(j + jnp.where(z == planes - 1, 1, 0), group)
    jl = lax.rem(j + group - jnp.where(z == 0, 1, 0), group)
    sides = (zr * group + j, zr * group + jr, zl * group + j, zl * group + jl)
    mates = [lax.rem(j + o, group) for o in range(group)]
    sources = [lax.rem(j + group - o, group) for o in range(group)]

    def columns(start):
        return pl.ds(pl.multiple_of(start, 128), CHUNK)

    def load(c, a):
        ref = (q_ref, k_ref, v_ref, g_ref)[a]
        return pltpu.make_async_copy(ref.at[0, :, columns(c * CHUNK)], loaded.at[c, a], load_s.at[c, a])

    @pl.loop(0, chunks)
    def _(c):
        for n in (5, 11):
            halo_in[c, n] = jnp.zeros(halo_in.shape[2:], jnp.bfloat16)
            back_in[c, n] = jnp.zeros(back_in.shape[2:], jnp.bfloat16)

    for a in range(4):
        load(0, a).start()

    barrier = pltpu.get_barrier_semaphore()
    for o in range(1, group):
        pl.semaphore_signal(barrier, inc=1, device_id=(t, z * group + mates[o]), device_id_type=MESH)
    for side in sides:
        pl.semaphore_signal(barrier, inc=1, device_id=(t, side), device_id_type=MESH)
    for o in range(group):
        pl.semaphore_signal(barrier, inc=1, device_id=(after, z * group + mates[o]), device_id_type=MESH)

    @pl.loop(1, chunks)
    def _(c):
        for a in range(4):
            load(c, a).start()

    order = packing_ref[0]
    unpack_ref[...] = one_hot(order, 0, (128, 128))
    pack_ref[...] = one_hot(upright(order), 1, (128, 128))
    pl.semaphore_wait(barrier, 2 * group + 3)

    def at_rows(ref, c, start, count):
        if not isinstance(start, int):
            start = pl.multiple_of(start, 16)
        return ref.at[c, :, pl.ds(start, count), :]

    def a2a(c, o, landing):
        return pltpu.make_async_remote_copy(
            src_ref=at_rows(packed, c, mates[o] * rows, rows),
            dst_ref=at_rows(win, c, landing * rows, rows),
            send_sem=a2a_s.at[c, o - 1],
            recv_sem=a2a_r.at[c, o - 1],
            device_id=(t, z * group + mates[o]),
            device_id_type=MESH,
        )

    last_plane, first_plane = z == planes - 1, z == 0
    right_a, right_b, left_a, left_b = sides
    rightward = (((0, 5, 0, right_a),), ((0, 4, 0, right_a), (4, 2, 1, right_b)))
    leftward = (((6, 5, 2, left_a),), ((6, 4, 2, left_a), (10, 2, 3, left_b)))
    returned_left = (((0, 5, 0, left_a),), ((0, 4, 0, left_a), (4, 2, 1, left_b)))
    returned_right = (((6, 5, 2, right_a),), ((6, 4, 2, right_a), (10, 2, 3, right_b)))

    def each(copies, turn, act):
        for n in range(2):
            @pl.when(turn if n == 1 else jnp.logical_not(turn))
            def _():
                for copy in copies[n]:
                    act(*copy)

    def outward(c, act):
        def one(first, count, n, target):
            act(pltpu.make_async_remote_copy(
                src_ref=halo.at[c, pl.ds(first, count)],
                dst_ref=halo_in.at[c, pl.ds(first, count)],
                send_sem=halo_s.at[c, n],
                recv_sem=halo_r.at[c, n],
                device_id=(t, target),
                device_id_type=MESH,
            ))
        return one

    def homeward(c, act):
        def one(first, count, n, target):
            act(pltpu.make_async_remote_copy(
                src_ref=back_out.at[c, pl.ds(first, count)],
                dst_ref=back_in.at[c, pl.ds(first, count)],
                send_sem=back_s.at[c, n],
                recv_sem=back_r.at[c, n],
                device_id=(t, target),
                device_id_type=MESH,
            ))
        return one

    def start(copy):
        copy.start()

    def landed(copy):
        copy.wait_recv()

    def gone(copy):
        copy.wait_send()

    def outward_sends(c, act):
        each(rightward, last_plane, outward(c, act))
        each(leftward, first_plane, outward(c, act))

    def outward_arrivals(c):
        each(returned_left, first_plane, outward(c, landed))
        each(returned_right, last_plane, outward(c, landed))

    def homeward_sends(c, act):
        each(returned_left, first_plane, homeward(c, act))
        each(returned_right, last_plane, homeward(c, act))

    def homeward_arrivals(c):
        each(rightward, last_plane, homeward(c, landed))
        each(leftward, first_plane, homeward(c, landed))

    def final(c, o, landing):
        return pltpu.make_async_remote_copy(
            src_ref=at_rows(fin_out, c, mates[o] * rows, rows),
            dst_ref=at_rows(fin_in, c, landing * rows, rows),
            send_sem=fin_s.at[c, o],
            recv_sem=fin_r.at[c, o],
            device_id=(before, z * group + mates[o]),
            device_id_type=MESH,
        )

    unpack_copy = pltpu.make_async_remote_copy(
        src_ref=unpack_ref, dst_ref=unpack_in, send_sem=un_s, recv_sem=un_r,
        device_id=(before, me), device_id_type=MESH,
    )
    unpack_copy.start()

    def hand_out(c):
        for a in range(4):
            load(c, a).wait()
            packed[c, a] = dot_nn(pack_ref[...], loaded[c, a]).astype(jnp.bfloat16)
        for o in range(1, group):
            a2a(c, o, j).start()
        own = pl.ds(pl.multiple_of(j * rows, 16), rows)
        for a in range(4):
            win[c, a, own, :] = packed[c, a, own, :]
            win[c, a, 224:256, :] = jnp.zeros((32, CHUNK), jnp.bfloat16)

    @pl.loop(0, 2)
    def _(c):
        hand_out(c)

    slots, kept, foreign = boundary_plan(ids_ref, blocks, planes, z, j)
    pick_ref[...] = one_hot(slots, 0, (96, 128))
    place_ref[...] = one_hot(upright(slots), 1, (128, 96))
    id_row = jnp.concatenate([kept, foreign], axis=1)
    id_col = jnp.concatenate([upright(kept), upright(foreign)], axis=0)
    id_col = id_col[0:224]
    bias[...] = jnp.where((id_col == id_row) & (id_row >= 0), 0.0, NEG)
    valid[...] = jnp.where(id_col >= 0, 1.0, 0.0)
    scale = HEAD_DIM ** (-0.5)

    def spread(c):
        for o in range(1, group):
            a2a(c, o, sources[o]).wait_recv()
        picked = [
            dot_nn(pick_ref[...], win[c, a, 0:128, :]).reshape(GROUPS, 8, CHUNK) for a in range(4)
        ]
        for a in (0, 2):
            pair = jnp.concatenate(picked[a : a + 2], axis=1)
            halo[c, :, a * 8 : a * 8 + 16, :] = pair.astype(jnp.bfloat16)
        outward_sends(c, start)

    def attend(c):
        outward_arrivals(c)
        for a in (0, 2):
            pair = halo_in[c, :, a * 8 : a * 8 + 16, :].astype(jnp.float32)
            for n in range(2):
                cells = pair[:, n * 8 : n * 8 + 8].reshape(GROUPS * 8, CHUNK)
                win[c, a + n, 128:224, :] = cells.astype(jnp.bfloat16)
        foreign = []
        for h in range(CHUNK // HEAD_DIM):
            head = slice(h * HEAD_DIM, (h + 1) * HEAD_DIM)
            q, g = [win[c, a, 0:224, head] for a in (0, 3)]
            k, v = [win[c, a, :, head] for a in (1, 2)]
            s = dot_nt(q, k) * scale + bias[...]
            e = jnp.exp(s - jnp.max(s, axis=1, keepdims=True))
            p = e * (valid[...] / jnp.sum(e, axis=1, keepdims=True))
            low = p.astype(jnp.bfloat16)
            dp = dot_nt(g, v)
            delta = jnp.sum(low.astype(jnp.float32) * dp, axis=1, keepdims=True)
            ds = (p * (dp - delta) * scale).astype(jnp.bfloat16)
            for a, grad in enumerate((dot_nn(ds, k), dot_tn(ds, q), dot_tn(low, g))):
                fin_out[c, a, :, head] = grad[0:128].astype(jnp.bfloat16)
                foreign.append(grad[128:224].reshape(GROUPS, 8, HEAD_DIM))
                if len(foreign) % 2 == 0:
                    pair = jnp.concatenate(foreign[-2:], axis=1)
                    last = len(foreign) * 8
                    back_out[c, :, last - 16 : last, :] = pair.astype(jnp.bfloat16)
        homeward_sends(c, start)

    def hand_on(c):
        homeward_arrivals(c)
        foreign = []
        for n in range(0, 3 * CHUNK // HEAD_DIM, 2):
            pair = back_in[c, :, n * 8 : n * 8 + 16, :].astype(jnp.float32)
            for i in range(2):
                foreign.append(pair[:, i * 8 : i * 8 + 8].reshape(GROUPS * 8, HEAD_DIM))
        for a in range(3):
            returned = dot_nn(place_ref[...], jnp.concatenate(foreign[a::3], axis=1).astype(jnp.bfloat16))
            fin_out[c, a] = (fin_out[c, a].astype(jnp.float32) + returned).astype(jnp.bfloat16)
        for o in range(group):
            final(c, o, j).start()

    def written(c, a):
        return pltpu.make_async_copy(
            placed.at[c, a], out_ref.at[0, :, columns(a * width + c * CHUNK)], put_s.at[c, a]
        )

    def finish(c):
        @pl.when(c == 0)
        def _():
            unpack_copy.wait_recv()

        for o in range(group):
            final(c, o, sources[o]).wait_recv()
        for a in range(3):
            placed[c, a] = dot_nn(unpack_in[...], fin_in[c, a]).astype(jnp.bfloat16)
            written(c, a).start()

    stages = (spread, attend, hand_on, finish, hand_out)
    lead = (2, 4, 6, 8, 0)

    @pl.loop(2, chunks + max(lead))
    def _(step):
        for late, stage in zip(lead, stages):

            @pl.when((step >= late) & (step < chunks + late))
            def _():
                stage(step - late)

    unpack_copy.wait_send()

    @pl.loop(0, chunks)
    def _(c):
        for o in range(1, group):
            a2a(c, o, j).wait_send()
        outward_sends(c, gone)
        homeward_sends(c, gone)
        for o in range(group):
            final(c, o, j).wait_send()
        for a in range(3):
            written(c, a).wait()


def hand_over(from_ref, to_ref, sems):
    def part(n):
        rows = pl.ds(n * 16, 16)
        return pltpu.make_async_copy(from_ref.at[:, rows], to_ref.at[:, rows], sems.at[n])

    for n in range(8):
        part(n).start()
    for n in range(8):
        part(n).wait()


def fused_body(sections, queries, key_cells, value_cells, grad_cells, packing, segment_ids):
    cell_count, width = queries.shape[1:]
    devices = lax.axis_size("dp")
    group = devices // 4
    planes = devices // group
    chunks = width // CHUNK
    vmem = pl.BlockSpec(memory_space=pltpu.VMEM)
    far = pl.BlockSpec(memory_space=pl.ANY)
    bf16 = jnp.bfloat16
    sem = pltpu.SemaphoreType.DMA
    result = pl.pallas_call(
        functools.partial(kernel, group, planes, sections, chunks, width),
        out_shape=jax.ShapeDtypeStruct((1, cell_count, 3 * width), bf16),
        in_specs=[far] * 4 + [vmem] * 2,
        out_specs=far,
        scratch_shapes=[
            pltpu.VMEM((chunks, 4, 128, CHUNK), bf16),
            pltpu.VMEM((chunks, 4, 128, CHUNK), bf16),
            pltpu.VMEM((chunks, 4, 256, CHUNK), bf16),
            pltpu.VMEM((chunks, GROUPS, 32, CHUNK), bf16),
            pltpu.VMEM((chunks, GROUPS, 32, CHUNK), bf16),
            pltpu.VMEM((chunks, GROUPS, 24 * CHUNK // HEAD_DIM, HEAD_DIM), bf16),
            pltpu.VMEM((chunks, GROUPS, 24 * CHUNK // HEAD_DIM, HEAD_DIM), bf16),
            pltpu.VMEM((chunks, 3, 128, CHUNK), bf16),
            pltpu.VMEM((chunks, 3, 128, CHUNK), bf16),
            pltpu.VMEM((128, 128), bf16),
            pltpu.VMEM((chunks, 3, 128, CHUNK), bf16),
            pltpu.VMEM((224, 256), jnp.float32),
            pltpu.VMEM((224, 1), jnp.float32),
            pltpu.VMEM((128, 128), bf16),
            pltpu.VMEM((128, 128), bf16),
            pltpu.VMEM((96, 128), bf16),
            pltpu.VMEM((128, 96), bf16),
            pltpu.VMEM((segment_ids.shape[1] // 128 + 8, 128), jnp.int32),
            sem((chunks, 4)),
            sem((chunks, group - 1)), sem((chunks, group - 1)),
            sem((chunks, 4)), sem((chunks, 4)),
            sem((chunks, 4)), sem((chunks, 4)),
            sem((chunks, group)), sem((chunks, group)),
            sem, sem, sem((chunks, 3)),
        ],
        compiler_params=pltpu.CompilerParams(
            collective_id=0, has_side_effects=True, vmem_limit_bytes=60 * 1024 * 1024
        ),
    )(queries, key_cells, value_cells, grad_cells, packing, segment_ids)
    return pl.pallas_call(
        hand_over,
        out_shape=jax.ShapeDtypeStruct(result.shape, bf16),
        in_specs=[far],
        out_specs=far,
        scratch_shapes=[sem((8,))],
        compiler_params=pltpu.CompilerParams(vmem_limit_bytes=60 * 1024 * 1024),
    )(result)


def solution(mesh):
    sections, devices = mesh.shape["section"], mesh.shape["dp"]

    def body_of(queries, *rest):
        fits = queries.shape[1] == 128 and queries.shape[2] % CHUNK == 0 and devices == 16
        if fits:
            return fused_body(sections, queries, *rest)
        return body(queries, *rest)

    return jax.shard_map(
        body_of,
        mesh=mesh,
        in_specs=(
            P("section", "dp", None),
            P("section", "dp", None),
            P("section", "dp", None),
            P("section", "dp", None),
            P("section", "dp", None),
            P("section", None),
        ),
        out_specs=P("section", "dp", None),
        check_vma=False,
    )
```

```python
import functools
import jax
import jax.numpy as jnp
from jax import lax
from jax.sharding import PartitionSpec as P
from jax.experimental import pallas as pl
from jax.experimental.pallas import tpu as pltpu

HEADS = 20
HEAD_DIM = 128
CHUNK = 256
MESH = pl.DeviceIdType.MESH
NEG = -1e30
GROUPS = 12
INNER, TURN = 40, 32


def with_halo(value, sides, width):
    for axis, dim in sides:
        size, length = (lax.axis_size(axis), value.shape[dim])
        up = [(i, (i + 1) % size) for i in range(size - 1)]
        down = [(j, i) for i, j in up]
        last = lax.slice_in_dim(value, length - width, length, axis=dim)
        initial = lax.slice_in_dim(value, 0, width, axis=dim)
        before = lax.ppermute(last, axis, up)
        after = lax.ppermute(initial, axis, down)
        value = jnp.concatenate([before, value, after], axis=dim)
    return value


def passed_along(value, axis, steps):
    count = lax.axis_size(axis)
    initial, last = (max(0, -steps), min(count, count - steps))
    return lax.ppermute(value, axis, [(source, source + steps) for source in range(initial, last)])


def from_behind(block, axis, distance):
    devices = range(lax.axis_size(axis))
    route = [((i - distance) % len(devices), i) for i in devices]
    return lax.ppermute(block, axis, route)


def heads_of(matrix):
    return matrix.reshape(matrix.shape[0], HEADS, HEAD_DIM)


def masked_scores(query_rows, key_rows, query_ids, key_ids):
    scores = jnp.einsum(
        "ihd,jhd->hij", heads_of(query_rows), heads_of(key_rows), preferred_element_type=jnp.float32
    )
    scores = scores * HEAD_DIM ** (-0.5)
    allowed = (query_ids[:, None] == key_ids[None, :])[None]
    return jnp.where(allowed, scores, -jnp.inf)


def body(queries, key_cells, value_cells, grad_cells, packing, segment_ids):
    cell_count = queries.shape[1]
    width = queries.shape[2]
    groups = lax.axis_size("dp")
    per_peer = cell_count // groups
    reach = cell_count // 4
    place = lax.axis_index("dp")
    scale = HEAD_DIM ** (-0.5)
    order = packing[0, 0]

    def pack(matrix):
        return matrix[0][order].reshape(groups, per_peer, width)

    arrived = (
        lax.all_to_all(pack(queries), "dp", split_axis=0, concat_axis=0, tiled=True),
        lax.all_to_all(pack(key_cells), "dp", split_axis=0, concat_axis=0, tiled=True),
        lax.all_to_all(pack(value_cells), "dp", split_axis=0, concat_axis=0, tiled=True),
        lax.all_to_all(pack(grad_cells), "dp", split_axis=0, concat_axis=0, tiled=True),
    )
    own_q, own_k, own_v, own_g = [piece.reshape(cell_count, width) for piece in arrived]
    rim_ids = jnp.full((reach,), -1, jnp.int32)
    padded_ids = jnp.concatenate([rim_ids, segment_ids[0], rim_ids])
    window_ids = lax.dynamic_slice_in_dim(padded_ids, place * cell_count, cell_count + 2 * reach)
    own_ids = window_ids[reach : reach + cell_count]
    key_value = jnp.concatenate([own_k, own_v], axis=1)
    key_value_window = with_halo(key_value, (("dp", 0),), reach)
    key_window = key_value_window[:, :width]
    value_window = key_value_window[:, width:]
    scores = masked_scores(own_q, key_window, own_ids, window_ids)
    top = jnp.max(scores, axis=2)
    log_total = top + jnp.log(jnp.sum(jnp.exp(scores - top[:, :, None]), axis=2))
    probs = jnp.exp(scores - log_total[:, :, None])
    probs_low = probs.astype(jnp.bfloat16)
    grad_heads = heads_of(own_g)
    attended = jnp.einsum(
        "hij,jhd->ihd", probs_low, heads_of(value_window), preferred_element_type=jnp.float32
    )
    delta = jnp.sum(grad_heads.astype(jnp.float32) * attended, axis=2).T
    dprobs = jnp.einsum(
        "ihd,jhd->hij", grad_heads, heads_of(value_window), preferred_element_type=jnp.float32
    )
    dscores = (probs * (dprobs - delta[:, :, None]) * scale).astype(jnp.bfloat16)
    grad_query = jnp.einsum(
        "hij,jhd->ihd", dscores, heads_of(key_window), preferred_element_type=jnp.float32
    )
    grad_query = grad_query.reshape(cell_count, width).astype(jnp.bfloat16)
    window = cell_count + 2 * reach
    grad_key = jnp.einsum(
        "hij,ihd->jhd", dscores, heads_of(own_q), preferred_element_type=jnp.float32
    )
    grad_value = jnp.einsum(
        "hij,ihd->jhd", probs_low, grad_heads, preferred_element_type=jnp.float32
    )
    partial_value = jnp.concatenate(
        [grad_key.reshape(window, width), grad_value.reshape(window, width)], axis=1
    )
    from_after = passed_along(partial_value[:reach].astype(jnp.bfloat16), "dp", -1).astype(
        jnp.float32
    )
    from_before = passed_along(
        partial_value[reach + cell_count :].astype(jnp.bfloat16), "dp", 1
    ).astype(jnp.float32)
    summed = partial_value[reach : reach + cell_count]
    summed = summed.at[cell_count - reach :].add(from_after)
    summed = summed.at[:reach].add(from_before)
    packed_grads = jnp.concatenate([grad_query, summed.astype(jnp.bfloat16)], axis=1)
    returned = lax.all_to_all(
        packed_grads.reshape(groups, per_peer, 3 * width),
        "dp",
        split_axis=0,
        concat_axis=0,
        tiled=True,
    )
    returned = returned.reshape(cell_count, 3 * width)
    inverse = (
        jnp.zeros((cell_count,), jnp.int32).at[order].set(jnp.arange(cell_count, dtype=jnp.int32))
    )
    loaded_order = returned[inverse]
    handed = from_behind(loaded_order, "section", -1)
    return handed[None]


def dot_nt(a, b):
    return lax.dot_general(a, b, (((1,), (1,)), ((), ())), preferred_element_type=jnp.float32)


def dot_tn(a, b):
    return lax.dot_general(a, b, (((0,), (0,)), ((), ())), preferred_element_type=jnp.float32)


def dot_nn(a, b):
    return jnp.dot(a, b, preferred_element_type=jnp.float32)


def one_hot(index, dim, shape):
    return jnp.where(lax.broadcasted_iota(jnp.int32, shape, dim) == index, 1.0, 0.0).astype(jnp.bfloat16)


def small(x):
    return x.astype(jnp.float32).astype(jnp.bfloat16)


def upright(row):
    eye = one_hot(lax.broadcasted_iota(jnp.int32, (1, 128), 1), 0, (128, 128))
    column = dot_nt(eye, small(jnp.broadcast_to(row, (16, 128))))
    return column[:, 0:1].astype(jnp.int32)


def directions(tails, heads, turn):
    subset = lax.broadcasted_iota(jnp.int32, (4, 128), 1)
    number = lax.broadcasted_iota(jnp.int32, (4, 128), 0)
    chosen = jnp.where(number == 0, subset, jnp.where(number == 1, subset // 2, subset // 4))
    chosen = jnp.where(number == 3, subset // 8, chosen) % 2
    right, left = chosen * tails, (1 - chosen) * heads

    def total(x, rows):
        return sum(x[i : i + 1] for i in rows)

    inner = (total(right, range(4)) <= INNER) & (total(left, range(4)) <= INNER)
    turned = (total(right, range(3)) <= TURN) & (total(left, range(3)) <= TURN)
    turned = turned & (right[3:4] <= 16) & (left[3:4] <= 16)
    fits = jnp.where(turn, turned.astype(jnp.int32), inner.astype(jnp.int32))
    best = jnp.where((fits == 1) & (subset[0:1] < 16), subset[0:1], 16).astype(jnp.float32)
    best = jnp.min(best, axis=1, keepdims=True).astype(jnp.int32)
    picked = subset == best

    def at_best(x):
        return jnp.sum(jnp.where(picked, x, 0).astype(jnp.float32), axis=1, keepdims=True).astype(jnp.int32)

    go, right, left = at_best(chosen), at_best(right), at_best(left)

    def first_slots(x):
        starts = [jnp.zeros_like(x[0:1])]
        for i in range(3):
            starts.append(starts[i] + x[i : i + 1])
        starts[3] = jnp.where(turn, TURN, starts[3])
        return jnp.concatenate(starts, axis=0)

    return go, first_slots(right), first_slots(left)


def boundary_plan(ids_ref, blocks, planes, z, j):
    reach = 128 // 4
    count = ids_ref.shape[1] // 128
    blocks[...] = jnp.full(blocks.shape, -1, jnp.int32)
    for b in range(count):
        blocks[b + 1 : b + 2, :] = ids_ref[:, b * 128 : (b + 1) * 128]
    here, ahead, behind = [
        jnp.concatenate([blocks[pl.ds(4 * j + k + d, 1), :] for k in range(4)], axis=0) for d in (1, 2, 0)
    ]
    span = 128 // planes
    first_plane, last_plane = z == 0, z == planes - 1
    place = lax.broadcasted_iota(jnp.int32, (4, 128), 1)
    inside = place < reach

    def turned(x, plane):
        return pltpu.roll(x, lax.rem(2 * 128 - plane * span, 128), 1)

    own = turned(here, z)
    prior = turned(jnp.where(first_plane, behind, here), z - 1)
    later = turned(jnp.where(last_plane, ahead, here), z + 1)

    def matching(x, value, straddles):
        hits = jnp.sum(jnp.where(inside & (x == value), 1.0, 0.0), axis=1, keepdims=True)
        return jnp.where(straddles, hits, 0.0).astype(jnp.int32)

    first, last = own[:, 0:1], own[:, reach - 1 : reach]
    before, after = prior[:, reach - 1 : reach], later[:, 0:1]
    tail_r, head_r = [matching(x, last, last == after) for x in (own, later)]
    tail_l, head_l = [matching(x, first, first == before) for x in (prior, own)]
    go_r, right_r, left_r = directions(tail_r, head_r, last_plane)

    def shifted(x, by):
        rows = [x[(i + by) % 4 : (i + by) % 4 + 1] for i in range(4)]
        return jnp.where(first_plane, jnp.concatenate(rows, axis=0), x)

    go_l, right_l, left_l = [
        shifted(x, 3) for x in directions(shifted(tail_l, 1), shifted(head_l, 1), first_plane)
    ]
    sent_r, sent_l = jnp.where(go_r == 1, tail_r, 0), jnp.where(go_l == 0, head_l, 0)
    got_l, got_r = jnp.where(go_l == 1, tail_l, 0), jnp.where(go_r == 0, head_r, 0)
    begin = reach - sent_r
    slots = jnp.where(
        inside & (place >= begin),
        right_r + place - begin,
        jnp.where(place < sent_l, 48 + left_l + place, -1),
    )
    kept = jnp.where(slots >= 0, -1, own)
    lane = lax.broadcasted_iota(jnp.int32, (1, 128), 1)
    route = one_hot(lane // 32 * 8 + lane % 8, 0, (128, 128))
    block = lane // 8 % 4

    def arrival(x):
        moved = dot_nn(small(jnp.concatenate([x] * 4, axis=0)), route)
        total = jnp.zeros((1, 128), jnp.float32)
        for k in range(4):
            total = total + jnp.where(block == k, moved[k : k + 1], 0.0)
        return total.astype(jnp.int32)

    left_hit = (place >= right_l) & (place < right_l + got_l)
    right_hit = (place >= 48 + left_r) & (place < 48 + left_r + got_r)
    foreign = jnp.where(left_hit, first, jnp.where(right_hit, last, -1))
    foreign = jnp.max(foreign.astype(jnp.float32), axis=0, keepdims=True).astype(jnp.int32)
    return arrival(slots), arrival(kept), foreign


def kernel(
    group, planes, sections, chunks, width,
    q_ref, k_ref, v_ref, g_ref, packing_ref, ids_ref,
    out_ref,
    loaded, packed, win, halo, halo_in, back_out, back_in, fin_out, fin_in, unpack_in, placed, bias, valid,
    pack_ref, unpack_ref, pick_ref, place_ref, blocks, load_s,
    a2a_s, a2a_r, halo_s, halo_r, back_s, back_r, fin_s, fin_r, un_s, un_r, put_s,
):
    t = lax.axis_index("section")
    me = lax.axis_index("dp")
    z, j = lax.div(me, group), lax.rem(me, group)
    rows = 128 // group
    before = lax.rem(t + sections - 1, sections)
    after = lax.rem(t + 1, sections)
    zr, zl = lax.rem(z + 1, planes), lax.rem(z + planes - 1, planes)
    jr = lax.rem(j + jnp.where(z == planes - 1, 1, 0), group)
    jl = lax.rem(j + group - jnp.where(z == 0, 1, 0), group)
    sides = (zr * group + j, zr * group + jr, zl * group + j, zl * group + jl)
    mates = [lax.rem(j + o, group) for o in range(group)]
    sources = [lax.rem(j + group - o, group) for o in range(group)]

    def columns(start):
        return pl.ds(pl.multiple_of(start, 128), CHUNK)

    def load(c, a):
        ref = (q_ref, k_ref, v_ref, g_ref)[a]
        return pltpu.make_async_copy(ref.at[0, :, columns(c * CHUNK)], loaded.at[c, a], load_s.at[c, a])

    @pl.loop(0, chunks)
    def _(c):
        for n in (5, 11):
            halo_in[c, n] = jnp.zeros(halo_in.shape[2:], jnp.bfloat16)
            back_in[c, n] = jnp.zeros(back_in.shape[2:], jnp.bfloat16)

    for a in range(4):
        load(0, a).start()

    barrier = pltpu.get_barrier_semaphore()
    for o in range(1, group):
        pl.semaphore_signal(barrier, inc=1, device_id=(t, z * group + mates[o]), device_id_type=MESH)
    for side in sides:
        pl.semaphore_signal(barrier, inc=1, device_id=(t, side), device_id_type=MESH)
    for o in range(group):
        pl.semaphore_signal(barrier, inc=1, device_id=(after, z * group + mates[o]), device_id_type=MESH)

    @pl.loop(1, chunks)
    def _(c):
        for a in range(4):
            load(c, a).start()

    order = packing_ref[0]
    unpack_ref[...] = one_hot(order, 0, (128, 128))
    pack_ref[...] = one_hot(upright(order), 1, (128, 128))
    pl.semaphore_wait(barrier, 2 * group + 3)

    def at_rows(ref, c, start, count):
        if not isinstance(start, int):
            start = pl.multiple_of(start, 16)
        return ref.at[c, :, pl.ds(start, count), :]

    def a2a(c, o, landing):
        return pltpu.make_async_remote_copy(
            src_ref=at_rows(packed, c, mates[o] * rows, rows),
            dst_ref=at_rows(win, c, landing * rows, rows),
            send_sem=a2a_s.at[c, o - 1],
            recv_sem=a2a_r.at[c, o - 1],
            device_id=(t, z * group + mates[o]),
            device_id_type=MESH,
        )

    last_plane, first_plane = z == planes - 1, z == 0
    right_a, right_b, left_a, left_b = sides
    rightward = (((0, 5, 0, right_a),), ((0, 4, 0, right_a), (4, 2, 1, right_b)))
    leftward = (((6, 5, 2, left_a),), ((6, 4, 2, left_a), (10, 2, 3, left_b)))
    returned_left = (((0, 5, 0, left_a),), ((0, 4, 0, left_a), (4, 2, 1, left_b)))
    returned_right = (((6, 5, 2, right_a),), ((6, 4, 2, right_a), (10, 2, 3, right_b)))

    def each(copies, turn, act):
        for n in range(2):
            @pl.when(turn if n == 1 else jnp.logical_not(turn))
            def _():
                for copy in copies[n]:
                    act(*copy)

    def outward(c, act):
        def one(first, count, n, target):
            act(pltpu.make_async_remote_copy(
                src_ref=halo.at[c, pl.ds(first, count)],
                dst_ref=halo_in.at[c, pl.ds(first, count)],
                send_sem=halo_s.at[c, n],
                recv_sem=halo_r.at[c, n],
                device_id=(t, target),
                device_id_type=MESH,
            ))
        return one

    def homeward(c, act):
        def one(first, count, n, target):
            act(pltpu.make_async_remote_copy(
                src_ref=back_out.at[c, pl.ds(first, count)],
                dst_ref=back_in.at[c, pl.ds(first, count)],
                send_sem=back_s.at[c, n],
                recv_sem=back_r.at[c, n],
                device_id=(t, target),
                device_id_type=MESH,
            ))
        return one

    def start(copy):
        copy.start()

    def landed(copy):
        copy.wait_recv()

    def gone(copy):
        copy.wait_send()

    def outward_sends(c, act):
        each(rightward, last_plane, outward(c, act))
        each(leftward, first_plane, outward(c, act))

    def outward_arrivals(c):
        each(returned_left, first_plane, outward(c, landed))
        each(returned_right, last_plane, outward(c, landed))

    def homeward_sends(c, act):
        each(returned_left, first_plane, homeward(c, act))
        each(returned_right, last_plane, homeward(c, act))

    def homeward_arrivals(c):
        each(rightward, last_plane, homeward(c, landed))
        each(leftward, first_plane, homeward(c, landed))

    def final(c, o, landing):
        return pltpu.make_async_remote_copy(
            src_ref=at_rows(fin_out, c, mates[o] * rows, rows),
            dst_ref=at_rows(fin_in, c, landing * rows, rows),
            send_sem=fin_s.at[c, o],
            recv_sem=fin_r.at[c, o],
            device_id=(before, z * group + mates[o]),
            device_id_type=MESH,
        )

    unpack_copy = pltpu.make_async_remote_copy(
        src_ref=unpack_ref, dst_ref=unpack_in, send_sem=un_s, recv_sem=un_r,
        device_id=(before, me), device_id_type=MESH,
    )
    unpack_copy.start()

    def hand_out(c):
        for a in range(4):
            load(c, a).wait()
            packed[c, a] = dot_nn(pack_ref[...], loaded[c, a]).astype(jnp.bfloat16)
        for o in range(1, group):
            a2a(c, o, j).start()
        own = pl.ds(pl.multiple_of(j * rows, 16), rows)
        for a in range(4):
            win[c, a, own, :] = packed[c, a, own, :]
            win[c, a, 224:256, :] = jnp.zeros((32, CHUNK), jnp.bfloat16)

    @pl.loop(0, 2)
    def _(c):
        hand_out(c)

    slots, kept, foreign = boundary_plan(ids_ref, blocks, planes, z, j)
    pick_ref[...] = one_hot(slots, 0, (96, 128))
    place_ref[...] = one_hot(upright(slots), 1, (128, 96))
    id_row = jnp.concatenate([kept, foreign], axis=1)
    id_col = jnp.concatenate([upright(kept), upright(foreign)], axis=0)
    id_col = id_col[0:224]
    bias[...] = jnp.where((id_col == id_row) & (id_row >= 0), 0.0, NEG)
    valid[...] = jnp.where(id_col >= 0, 1.0, 0.0)
    scale = HEAD_DIM ** (-0.5)

    def spread(c):
        for o in range(1, group):
            a2a(c, o, sources[o]).wait_recv()
        picked = [
            dot_nn(pick_ref[...], win[c, a, 0:128, :]).reshape(GROUPS, 8, CHUNK) for a in range(4)
        ]
        for a in (0, 2):
            pair = jnp.concatenate(picked[a : a + 2], axis=1)
            halo[c, :, a * 8 : a * 8 + 16, :] = pair.astype(jnp.bfloat16)
        outward_sends(c, start)

    def attend(c):
        outward_arrivals(c)
        for a in (0, 2):
            pair = halo_in[c, :, a * 8 : a * 8 + 16, :].astype(jnp.float32)
            for n in range(2):
                cells = pair[:, n * 8 : n * 8 + 8].reshape(GROUPS * 8, CHUNK)
                win[c, a + n, 128:224, :] = cells.astype(jnp.bfloat16)
        foreign = []
        for h in range(CHUNK // HEAD_DIM):
            head = slice(h * HEAD_DIM, (h + 1) * HEAD_DIM)
            q, g = [win[c, a, 0:224, head] for a in (0, 3)]
            k, v = [win[c, a, :, head] for a in (1, 2)]
            s = dot_nt(q, k) * scale + bias[...]
            e = jnp.exp(s - jnp.max(s, axis=1, keepdims=True))
            p = e * (valid[...] / jnp.sum(e, axis=1, keepdims=True))
            low = p.astype(jnp.bfloat16)
            dp = dot_nt(g, v)
            delta = jnp.sum(low.astype(jnp.float32) * dp, axis=1, keepdims=True)
            ds = (p * (dp - delta) * scale).astype(jnp.bfloat16)
            for a, grad in enumerate((dot_nn(ds, k), dot_tn(ds, q), dot_tn(low, g))):
                fin_out[c, a, :, head] = grad[0:128].astype(jnp.bfloat16)
                foreign.append(grad[128:224].reshape(GROUPS, 8, HEAD_DIM))
                if len(foreign) % 2 == 0:
                    pair = jnp.concatenate(foreign[-2:], axis=1)
                    last = len(foreign) * 8
                    back_out[c, :, last - 16 : last, :] = pair.astype(jnp.bfloat16)
        homeward_sends(c, start)

    def hand_on(c):
        homeward_arrivals(c)
        foreign = []
        for n in range(0, 3 * CHUNK // HEAD_DIM, 2):
            pair = back_in[c, :, n * 8 : n * 8 + 16, :].astype(jnp.float32)
            for i in range(2):
                foreign.append(pair[:, i * 8 : i * 8 + 8].reshape(GROUPS * 8, HEAD_DIM))
        for a in range(3):
            returned = dot_nn(place_ref[...], jnp.concatenate(foreign[a::3], axis=1).astype(jnp.bfloat16))
            fin_out[c, a] = (fin_out[c, a].astype(jnp.float32) + returned).astype(jnp.bfloat16)
        for o in range(group):
            final(c, o, j).start()

    def written(c, a):
        return pltpu.make_async_copy(
            placed.at[c, a], out_ref.at[0, :, columns(a * width + c * CHUNK)], put_s.at[c, a]
        )

    def finish(c):
        @pl.when(c == 0)
        def _():
            unpack_copy.wait_recv()

        for o in range(group):
            final(c, o, sources[o]).wait_recv()
        for a in range(3):
            placed[c, a] = dot_nn(unpack_in[...], fin_in[c, a]).astype(jnp.bfloat16)
            written(c, a).start()

    stages = (spread, attend, hand_on, finish, hand_out)
    lead = (2, 4, 6, 8, 0)

    @pl.loop(2, chunks + max(lead))
    def _(step):
        for late, stage in zip(lead, stages):

            @pl.when((step >= late) & (step < chunks + late))
            def _():
                stage(step - late)

    unpack_copy.wait_send()

    @pl.loop(0, chunks)
    def _(c):
        for o in range(1, group):
            a2a(c, o, j).wait_send()
        outward_sends(c, gone)
        homeward_sends(c, gone)
        for o in range(group):
            final(c, o, j).wait_send()
        for a in range(3):
            written(c, a).wait()


def hand_over(from_ref, to_ref, held, in_s, out_s):
    def part(n, inward):
        rows = pl.ds(n * 16, 16)
        if inward:
            return pltpu.make_async_copy(from_ref.at[:, rows], held.at[:, rows], in_s.at[n])
        return pltpu.make_async_copy(held.at[:, rows], to_ref.at[:, rows], out_s.at[n])

    for n in range(8):
        part(n, True).start()
    for n in range(8):
        part(n, True).wait()
        part(n, False).start()
    for n in range(8):
        part(n, False).wait()


def fused_body(sections, queries, key_cells, value_cells, grad_cells, packing, segment_ids):
    cell_count, width = queries.shape[1:]
    devices = lax.axis_size("dp")
    group = devices // 4
    planes = devices // group
    chunks = width // CHUNK
    vmem = pl.BlockSpec(memory_space=pltpu.VMEM)
    far = pl.BlockSpec(memory_space=pl.ANY)
    bf16 = jnp.bfloat16
    sem = pltpu.SemaphoreType.DMA
    result = pl.pallas_call(
        functools.partial(kernel, group, planes, sections, chunks, width),
        out_shape=jax.ShapeDtypeStruct((1, cell_count, 3 * width), bf16),
        in_specs=[far] * 4 + [vmem] * 2,
        out_specs=far,
        scratch_shapes=[
            pltpu.VMEM((chunks, 4, 128, CHUNK), bf16),
            pltpu.VMEM((chunks, 4, 128, CHUNK), bf16),
            pltpu.VMEM((chunks, 4, 256, CHUNK), bf16),
            pltpu.VMEM((chunks, GROUPS, 32, CHUNK), bf16),
            pltpu.VMEM((chunks, GROUPS, 32, CHUNK), bf16),
            pltpu.VMEM((chunks, GROUPS, 24 * CHUNK // HEAD_DIM, HEAD_DIM), bf16),
            pltpu.VMEM((chunks, GROUPS, 24 * CHUNK // HEAD_DIM, HEAD_DIM), bf16),
            pltpu.VMEM((chunks, 3, 128, CHUNK), bf16),
            pltpu.VMEM((chunks, 3, 128, CHUNK), bf16),
            pltpu.VMEM((128, 128), bf16),
            pltpu.VMEM((chunks, 3, 128, CHUNK), bf16),
            pltpu.VMEM((224, 256), jnp.float32),
            pltpu.VMEM((224, 1), jnp.float32),
            pltpu.VMEM((128, 128), bf16),
            pltpu.VMEM((128, 128), bf16),
            pltpu.VMEM((96, 128), bf16),
            pltpu.VMEM((128, 96), bf16),
            pltpu.VMEM((segment_ids.shape[1] // 128 + 8, 128), jnp.int32),
            sem((chunks, 4)),
            sem((chunks, group - 1)), sem((chunks, group - 1)),
            sem((chunks, 4)), sem((chunks, 4)),
            sem((chunks, 4)), sem((chunks, 4)),
            sem((chunks, group)), sem((chunks, group)),
            sem, sem, sem((chunks, 3)),
        ],
        compiler_params=pltpu.CompilerParams(
            collective_id=0, has_side_effects=True, vmem_limit_bytes=60 * 1024 * 1024
        ),
    )(queries, key_cells, value_cells, grad_cells, packing, segment_ids)
    return pl.pallas_call(
        hand_over,
        out_shape=jax.ShapeDtypeStruct(result.shape, bf16),
        in_specs=[far],
        out_specs=far,
        scratch_shapes=[pltpu.VMEM(result.shape, bf16), sem((8,)), sem((8,))],
        compiler_params=pltpu.CompilerParams(vmem_limit_bytes=60 * 1024 * 1024),
    )(result)


def solution(mesh):
    sections, devices = mesh.shape["section"], mesh.shape["dp"]

    def body_of(queries, *rest):
        fits = queries.shape[1] == 128 and queries.shape[2] % CHUNK == 0 and devices == 16
        if fits:
            return fused_body(sections, queries, *rest)
        return body(queries, *rest)

    return jax.shard_map(
        body_of,
        mesh=mesh,
        in_specs=(
            P("section", "dp", None),
            P("section", "dp", None),
            P("section", "dp", None),
            P("section", "dp", None),
            P("section", "dp", None),
            P("section", None),
        ),
        out_specs=P("section", "dp", None),
        check_vma=False,
    )
```

```python
import functools
import jax
import jax.numpy as jnp
from jax import lax
from jax.sharding import PartitionSpec as P
from jax.experimental import pallas as pl
from jax.experimental.pallas import tpu as pltpu

HEADS = 20
HEAD_DIM = 128
CHUNK = 256
MESH = pl.DeviceIdType.MESH
NEG = -1e30
LOG2_E = 1.4426950408889634
GROUPS = 12
INNER, TURN = 40, 32


def with_halo(value, sides, width):
    for axis, dim in sides:
        size, length = (lax.axis_size(axis), value.shape[dim])
        up = [(i, (i + 1) % size) for i in range(size - 1)]
        down = [(j, i) for i, j in up]
        last = lax.slice_in_dim(value, length - width, length, axis=dim)
        initial = lax.slice_in_dim(value, 0, width, axis=dim)
        before = lax.ppermute(last, axis, up)
        after = lax.ppermute(initial, axis, down)
        value = jnp.concatenate([before, value, after], axis=dim)
    return value


def passed_along(value, axis, steps):
    count = lax.axis_size(axis)
    initial, last = (max(0, -steps), min(count, count - steps))
    return lax.ppermute(value, axis, [(source, source + steps) for source in range(initial, last)])


def from_behind(block, axis, distance):
    devices = range(lax.axis_size(axis))
    route = [((i - distance) % len(devices), i) for i in devices]
    return lax.ppermute(block, axis, route)


def heads_of(matrix):
    return matrix.reshape(matrix.shape[0], HEADS, HEAD_DIM)


def masked_scores(query_rows, key_rows, query_ids, key_ids):
    scores = jnp.einsum(
        "ihd,jhd->hij", heads_of(query_rows), heads_of(key_rows), preferred_element_type=jnp.float32
    )
    scores = scores * HEAD_DIM ** (-0.5)
    allowed = (query_ids[:, None] == key_ids[None, :])[None]
    return jnp.where(allowed, scores, -jnp.inf)


def body(queries, key_cells, value_cells, grad_cells, packing, segment_ids):
    cell_count = queries.shape[1]
    width = queries.shape[2]
    groups = lax.axis_size("dp")
    per_peer = cell_count // groups
    reach = cell_count // 4
    place = lax.axis_index("dp")
    scale = HEAD_DIM ** (-0.5)
    order = packing[0, 0]

    def pack(matrix):
        return matrix[0][order].reshape(groups, per_peer, width)

    arrived = (
        lax.all_to_all(pack(queries), "dp", split_axis=0, concat_axis=0, tiled=True),
        lax.all_to_all(pack(key_cells), "dp", split_axis=0, concat_axis=0, tiled=True),
        lax.all_to_all(pack(value_cells), "dp", split_axis=0, concat_axis=0, tiled=True),
        lax.all_to_all(pack(grad_cells), "dp", split_axis=0, concat_axis=0, tiled=True),
    )
    own_q, own_k, own_v, own_g = [piece.reshape(cell_count, width) for piece in arrived]
    rim_ids = jnp.full((reach,), -1, jnp.int32)
    padded_ids = jnp.concatenate([rim_ids, segment_ids[0], rim_ids])
    window_ids = lax.dynamic_slice_in_dim(padded_ids, place * cell_count, cell_count + 2 * reach)
    own_ids = window_ids[reach : reach + cell_count]
    key_value = jnp.concatenate([own_k, own_v], axis=1)
    key_value_window = with_halo(key_value, (("dp", 0),), reach)
    key_window = key_value_window[:, :width]
    value_window = key_value_window[:, width:]
    scores = masked_scores(own_q, key_window, own_ids, window_ids)
    top = jnp.max(scores, axis=2)
    log_total = top + jnp.log(jnp.sum(jnp.exp(scores - top[:, :, None]), axis=2))
    probs = jnp.exp(scores - log_total[:, :, None])
    probs_low = probs.astype(jnp.bfloat16)
    grad_heads = heads_of(own_g)
    attended = jnp.einsum(
        "hij,jhd->ihd", probs_low, heads_of(value_window), preferred_element_type=jnp.float32
    )
    delta = jnp.sum(grad_heads.astype(jnp.float32) * attended, axis=2).T
    dprobs = jnp.einsum(
        "ihd,jhd->hij", grad_heads, heads_of(value_window), preferred_element_type=jnp.float32
    )
    dscores = (probs * (dprobs - delta[:, :, None]) * scale).astype(jnp.bfloat16)
    grad_query = jnp.einsum(
        "hij,jhd->ihd", dscores, heads_of(key_window), preferred_element_type=jnp.float32
    )
    grad_query = grad_query.reshape(cell_count, width).astype(jnp.bfloat16)
    window = cell_count + 2 * reach
    grad_key = jnp.einsum(
        "hij,ihd->jhd", dscores, heads_of(own_q), preferred_element_type=jnp.float32
    )
    grad_value = jnp.einsum(
        "hij,ihd->jhd", probs_low, grad_heads, preferred_element_type=jnp.float32
    )
    partial_value = jnp.concatenate(
        [grad_key.reshape(window, width), grad_value.reshape(window, width)], axis=1
    )
    from_after = passed_along(partial_value[:reach].astype(jnp.bfloat16), "dp", -1).astype(
        jnp.float32
    )
    from_before = passed_along(
        partial_value[reach + cell_count :].astype(jnp.bfloat16), "dp", 1
    ).astype(jnp.float32)
    summed = partial_value[reach : reach + cell_count]
    summed = summed.at[cell_count - reach :].add(from_after)
    summed = summed.at[:reach].add(from_before)
    packed_grads = jnp.concatenate([grad_query, summed.astype(jnp.bfloat16)], axis=1)
    returned = lax.all_to_all(
        packed_grads.reshape(groups, per_peer, 3 * width),
        "dp",
        split_axis=0,
        concat_axis=0,
        tiled=True,
    )
    returned = returned.reshape(cell_count, 3 * width)
    inverse = (
        jnp.zeros((cell_count,), jnp.int32).at[order].set(jnp.arange(cell_count, dtype=jnp.int32))
    )
    loaded_order = returned[inverse]
    handed = from_behind(loaded_order, "section", -1)
    return handed[None]


def dot_nt(a, b):
    return lax.dot_general(a, b, (((1,), (1,)), ((), ())), preferred_element_type=jnp.float32)


def dot_tn(a, b):
    return lax.dot_general(a, b, (((0,), (0,)), ((), ())), preferred_element_type=jnp.float32)


def dot_nn(a, b):
    return jnp.dot(a, b, preferred_element_type=jnp.float32)


def one_hot(index, dim, shape):
    return jnp.where(lax.broadcasted_iota(jnp.int32, shape, dim) == index, 1.0, 0.0).astype(jnp.bfloat16)


def small(x):
    return x.astype(jnp.float32).astype(jnp.bfloat16)


def upright(row):
    eye = one_hot(lax.broadcasted_iota(jnp.int32, (1, 128), 1), 0, (128, 128))
    column = dot_nt(eye, small(jnp.broadcast_to(row, (16, 128))))
    return column[:, 0:1].astype(jnp.int32)


def directions(tails, heads, turn):
    subset = lax.broadcasted_iota(jnp.int32, (4, 128), 1)
    number = lax.broadcasted_iota(jnp.int32, (4, 128), 0)
    chosen = jnp.where(number == 0, subset, jnp.where(number == 1, subset // 2, subset // 4))
    chosen = jnp.where(number == 3, subset // 8, chosen) % 2
    right, left = chosen * tails, (1 - chosen) * heads

    def total(x, rows):
        return sum(x[i : i + 1] for i in rows)

    inner = (total(right, range(4)) <= INNER) & (total(left, range(4)) <= INNER)
    turned = (total(right, range(3)) <= TURN) & (total(left, range(3)) <= TURN)
    turned = turned & (right[3:4] <= 16) & (left[3:4] <= 16)
    fits = jnp.where(turn, turned.astype(jnp.int32), inner.astype(jnp.int32))
    best = jnp.where((fits == 1) & (subset[0:1] < 16), subset[0:1], 16).astype(jnp.float32)
    best = jnp.min(best, axis=1, keepdims=True).astype(jnp.int32)
    picked = subset == best

    def at_best(x):
        return jnp.sum(jnp.where(picked, x, 0).astype(jnp.float32), axis=1, keepdims=True).astype(jnp.int32)

    go, right, left = at_best(chosen), at_best(right), at_best(left)

    def first_slots(x):
        starts = [jnp.zeros_like(x[0:1])]
        for i in range(3):
            starts.append(starts[i] + x[i : i + 1])
        starts[3] = jnp.where(turn, TURN, starts[3])
        return jnp.concatenate(starts, axis=0)

    return go, first_slots(right), first_slots(left)


def boundary_plan(ids_ref, blocks, planes, z, j):
    reach = 128 // 4
    count = ids_ref.shape[1] // 128
    blocks[...] = jnp.full(blocks.shape, -1, jnp.int32)
    for b in range(count):
        blocks[b + 1 : b + 2, :] = ids_ref[:, b * 128 : (b + 1) * 128]
    here, ahead, behind = [
        jnp.concatenate([blocks[pl.ds(4 * j + k + d, 1), :] for k in range(4)], axis=0) for d in (1, 2, 0)
    ]
    span = 128 // planes
    first_plane, last_plane = z == 0, z == planes - 1
    place = lax.broadcasted_iota(jnp.int32, (4, 128), 1)
    inside = place < reach

    def turned(x, plane):
        return pltpu.roll(x, lax.rem(2 * 128 - plane * span, 128), 1)

    own = turned(here, z)
    prior = turned(jnp.where(first_plane, behind, here), z - 1)
    later = turned(jnp.where(last_plane, ahead, here), z + 1)

    def matching(x, value, straddles):
        hits = jnp.sum(jnp.where(inside & (x == value), 1.0, 0.0), axis=1, keepdims=True)
        return jnp.where(straddles, hits, 0.0).astype(jnp.int32)

    first, last = own[:, 0:1], own[:, reach - 1 : reach]
    before, after = prior[:, reach - 1 : reach], later[:, 0:1]
    tail_r, head_r = [matching(x, last, last == after) for x in (own, later)]
    tail_l, head_l = [matching(x, first, first == before) for x in (prior, own)]
    go_r, right_r, left_r = directions(tail_r, head_r, last_plane)

    def shifted(x, by):
        rows = [x[(i + by) % 4 : (i + by) % 4 + 1] for i in range(4)]
        return jnp.where(first_plane, jnp.concatenate(rows, axis=0), x)

    go_l, right_l, left_l = [
        shifted(x, 3) for x in directions(shifted(tail_l, 1), shifted(head_l, 1), first_plane)
    ]
    sent_r, sent_l = jnp.where(go_r == 1, tail_r, 0), jnp.where(go_l == 0, head_l, 0)
    got_l, got_r = jnp.where(go_l == 1, tail_l, 0), jnp.where(go_r == 0, head_r, 0)
    begin = reach - sent_r
    slots = jnp.where(
        inside & (place >= begin),
        right_r + place - begin,
        jnp.where(place < sent_l, 48 + left_l + place, -1),
    )
    kept = jnp.where(slots >= 0, -1, own)
    lane = lax.broadcasted_iota(jnp.int32, (1, 128), 1)
    route = one_hot(lane // 32 * 8 + lane % 8, 0, (128, 128))
    block = lane // 8 % 4

    def arrival(x):
        moved = dot_nn(small(jnp.concatenate([x] * 4, axis=0)), route)
        total = jnp.zeros((1, 128), jnp.float32)
        for k in range(4):
            total = total + jnp.where(block == k, moved[k : k + 1], 0.0)
        return total.astype(jnp.int32)

    left_hit = (place >= right_l) & (place < right_l + got_l)
    right_hit = (place >= 48 + left_r) & (place < 48 + left_r + got_r)
    foreign = jnp.where(left_hit, first, jnp.where(right_hit, last, -1))
    foreign = jnp.max(foreign.astype(jnp.float32), axis=0, keepdims=True).astype(jnp.int32)
    return arrival(slots), arrival(kept), foreign


def kernel(
    group, planes, sections, chunks, width,
    q_ref, k_ref, v_ref, g_ref, packing_ref, ids_ref,
    out_ref,
    loaded, packed, win, halo, halo_in, back_out, back_in, fin_out, fin_in, unpack_in, placed, bias, valid,
    pack_ref, unpack_ref, pick_ref, place_ref, blocks, load_s,
    a2a_s, a2a_r, halo_s, halo_r, back_s, back_r, fin_s, fin_r, un_s, un_r, put_s,
):
    t = lax.axis_index("section")
    me = lax.axis_index("dp")
    z, j = lax.div(me, group), lax.rem(me, group)
    rows = 128 // group
    before = lax.rem(t + sections - 1, sections)
    after = lax.rem(t + 1, sections)
    zr, zl = lax.rem(z + 1, planes), lax.rem(z + planes - 1, planes)
    jr = lax.rem(j + jnp.where(z == planes - 1, 1, 0), group)
    jl = lax.rem(j + group - jnp.where(z == 0, 1, 0), group)
    sides = (zr * group + j, zr * group + jr, zl * group + j, zl * group + jl)
    mates = [lax.rem(j + o, group) for o in range(group)]
    sources = [lax.rem(j + group - o, group) for o in range(group)]

    def columns(start):
        return pl.ds(pl.multiple_of(start, 128), CHUNK)

    def load(c, a):
        ref = (q_ref, k_ref, v_ref, g_ref)[a]
        return pltpu.make_async_copy(ref.at[0, :, columns(c * CHUNK)], loaded.at[c, a], load_s.at[c, a])

    @pl.loop(0, chunks)
    def _(c):
        for n in (5, 11):
            halo_in[c, n] = jnp.zeros(halo_in.shape[2:], jnp.bfloat16)
            back_in[c, n] = jnp.zeros(back_in.shape[2:], jnp.bfloat16)

    for a in range(4):
        load(0, a).start()

    barrier = pltpu.get_barrier_semaphore()
    for o in range(1, group):
        pl.semaphore_signal(barrier, inc=1, device_id=(t, z * group + mates[o]), device_id_type=MESH)
    for side in sides:
        pl.semaphore_signal(barrier, inc=1, device_id=(t, side), device_id_type=MESH)
    for o in range(group):
        pl.semaphore_signal(barrier, inc=1, device_id=(after, z * group + mates[o]), device_id_type=MESH)

    @pl.loop(1, chunks)
    def _(c):
        for a in range(4):
            load(c, a).start()

    order = packing_ref[0]
    unpack_ref[...] = one_hot(order, 0, (128, 128))
    pack_ref[...] = one_hot(upright(order), 1, (128, 128))
    pl.semaphore_wait(barrier, 2 * group + 3)

    def at_rows(ref, c, start, count):
        if not isinstance(start, int):
            start = pl.multiple_of(start, 16)
        return ref.at[c, :, pl.ds(start, count), :]

    def a2a(c, o, landing):
        return pltpu.make_async_remote_copy(
            src_ref=at_rows(packed, c, mates[o] * rows, rows),
            dst_ref=at_rows(win, c, landing * rows, rows),
            send_sem=a2a_s.at[c, o - 1],
            recv_sem=a2a_r.at[c, o - 1],
            device_id=(t, z * group + mates[o]),
            device_id_type=MESH,
        )

    last_plane, first_plane = z == planes - 1, z == 0
    right_a, right_b, left_a, left_b = sides
    rightward = (((0, 5, 0, right_a),), ((0, 4, 0, right_a), (4, 2, 1, right_b)))
    leftward = (((6, 5, 2, left_a),), ((6, 4, 2, left_a), (10, 2, 3, left_b)))
    returned_left = (((0, 5, 0, left_a),), ((0, 4, 0, left_a), (4, 2, 1, left_b)))
    returned_right = (((6, 5, 2, right_a),), ((6, 4, 2, right_a), (10, 2, 3, right_b)))

    def each(copies, turn, act):
        for n in range(2):
            @pl.when(turn if n == 1 else jnp.logical_not(turn))
            def _():
                for copy in copies[n]:
                    act(*copy)

    def outward(c, act):
        def one(first, count, n, target):
            act(pltpu.make_async_remote_copy(
                src_ref=halo.at[c, pl.ds(first, count)],
                dst_ref=halo_in.at[c, pl.ds(first, count)],
                send_sem=halo_s.at[c, n],
                recv_sem=halo_r.at[c, n],
                device_id=(t, target),
                device_id_type=MESH,
            ))
        return one

    def homeward(c, act):
        def one(first, count, n, target):
            act(pltpu.make_async_remote_copy(
                src_ref=back_out.at[c, pl.ds(first, count)],
                dst_ref=back_in.at[c, pl.ds(first, count)],
                send_sem=back_s.at[c, n],
                recv_sem=back_r.at[c, n],
                device_id=(t, target),
                device_id_type=MESH,
            ))
        return one

    def start(copy):
        copy.start()

    def landed(copy):
        copy.wait_recv()

    def gone(copy):
        copy.wait_send()

    def outward_sends(c, act):
        each(rightward, last_plane, outward(c, act))
        each(leftward, first_plane, outward(c, act))

    def outward_arrivals(c):
        each(returned_left, first_plane, outward(c, landed))
        each(returned_right, last_plane, outward(c, landed))

    def homeward_sends(c, act):
        each(returned_left, first_plane, homeward(c, act))
        each(returned_right, last_plane, homeward(c, act))

    def homeward_arrivals(c):
        each(rightward, last_plane, homeward(c, landed))
        each(leftward, first_plane, homeward(c, landed))

    def final(c, o, landing):
        return pltpu.make_async_remote_copy(
            src_ref=at_rows(fin_out, c, mates[o] * rows, rows),
            dst_ref=at_rows(fin_in, c, landing * rows, rows),
            send_sem=fin_s.at[c, o],
            recv_sem=fin_r.at[c, o],
            device_id=(before, z * group + mates[o]),
            device_id_type=MESH,
        )

    unpack_copy = pltpu.make_async_remote_copy(
        src_ref=unpack_ref, dst_ref=unpack_in, send_sem=un_s, recv_sem=un_r,
        device_id=(before, me), device_id_type=MESH,
    )
    unpack_copy.start()

    def hand_out(c):
        for a in range(4):
            load(c, a).wait()
            packed[c, a] = dot_nn(pack_ref[...], loaded[c, a]).astype(jnp.bfloat16)
        for o in range(1, group):
            a2a(c, o, j).start()
        own = pl.ds(pl.multiple_of(j * rows, 16), rows)
        for a in range(4):
            win[c, a, own, :] = packed[c, a, own, :]
            win[c, a, 224:256, :] = jnp.zeros((32, CHUNK), jnp.bfloat16)

    @pl.loop(0, 2)
    def _(c):
        hand_out(c)

    slots, kept, foreign = boundary_plan(ids_ref, blocks, planes, z, j)
    pick_ref[...] = one_hot(slots, 0, (96, 128))
    place_ref[...] = one_hot(upright(slots), 1, (128, 96))
    id_row = jnp.concatenate([kept, foreign], axis=1)
    id_col = jnp.concatenate([upright(kept), upright(foreign)], axis=0)
    id_col = id_col[0:224]
    bias[...] = jnp.where((id_col == id_row) & (id_row >= 0), 0.0, NEG)
    valid[...] = jnp.where(id_col >= 0, 1.0, 0.0)
    scale = HEAD_DIM ** (-0.5)

    def spread(c):
        for o in range(1, group):
            a2a(c, o, sources[o]).wait_recv()
        picked = [
            dot_nn(pick_ref[...], win[c, a, 0:128, :]).reshape(GROUPS, 8, CHUNK) for a in range(4)
        ]
        for a in (0, 2):
            pair = jnp.concatenate(picked[a : a + 2], axis=1)
            halo[c, :, a * 8 : a * 8 + 16, :] = pair.astype(jnp.bfloat16)
        outward_sends(c, start)

    def attend(c):
        outward_arrivals(c)
        for a in (0, 2):
            pair = halo_in[c, :, a * 8 : a * 8 + 16, :].astype(jnp.float32)
            for n in range(2):
                cells = pair[:, n * 8 : n * 8 + 8].reshape(GROUPS * 8, CHUNK)
                win[c, a + n, 128:224, :] = cells.astype(jnp.bfloat16)
        foreign = []
        for h in range(CHUNK // HEAD_DIM):
            head = slice(h * HEAD_DIM, (h + 1) * HEAD_DIM)
            q, g = [win[c, a, 0:224, head] for a in (0, 3)]
            k, v = [win[c, a, :, head] for a in (1, 2)]
            s = dot_nt(q, k) * (scale * LOG2_E) + bias[...]
            e = jnp.exp2(s - jnp.max(s, axis=1, keepdims=True))
            p = e * (valid[...] / jnp.sum(e, axis=1, keepdims=True))
            low = p.astype(jnp.bfloat16)
            dp = dot_nt(g, v)
            delta = jnp.sum(low.astype(jnp.float32) * dp, axis=1, keepdims=True)
            ds = (p * (dp - delta) * scale).astype(jnp.bfloat16)
            for a, grad in enumerate((dot_nn(ds, k), dot_tn(ds, q), dot_tn(low, g))):
                fin_out[c, a, :, head] = grad[0:128].astype(jnp.bfloat16)
                foreign.append(grad[128:224].reshape(GROUPS, 8, HEAD_DIM))
                if len(foreign) % 2 == 0:
                    pair = jnp.concatenate(foreign[-2:], axis=1)
                    last = len(foreign) * 8
                    back_out[c, :, last - 16 : last, :] = pair.astype(jnp.bfloat16)
        homeward_sends(c, start)

    def hand_on(c):
        homeward_arrivals(c)
        foreign = []
        for n in range(0, 3 * CHUNK // HEAD_DIM, 2):
            pair = back_in[c, :, n * 8 : n * 8 + 16, :].astype(jnp.float32)
            for i in range(2):
                foreign.append(pair[:, i * 8 : i * 8 + 8].reshape(GROUPS * 8, HEAD_DIM))
        for a in range(3):
            returned = dot_nn(place_ref[...], jnp.concatenate(foreign[a::3], axis=1).astype(jnp.bfloat16))
            fin_out[c, a] = (fin_out[c, a].astype(jnp.float32) + returned).astype(jnp.bfloat16)
        for o in range(group):
            final(c, o, j).start()

    def written(c, a):
        return pltpu.make_async_copy(
            placed.at[c, a], out_ref.at[0, :, columns(a * width + c * CHUNK)], put_s.at[c, a]
        )

    def finish(c):
        @pl.when(c == 0)
        def _():
            unpack_copy.wait_recv()

        for o in range(group):
            final(c, o, sources[o]).wait_recv()
        for a in range(3):
            placed[c, a] = dot_nn(unpack_in[...], fin_in[c, a]).astype(jnp.bfloat16)
            written(c, a).start()

    stages = (spread, attend, hand_on, finish, hand_out)
    lead = (2, 3, 5, 7, 0)

    @pl.loop(2, chunks + max(lead))
    def _(step):
        for late, stage in zip(lead, stages):

            @pl.when((step >= late) & (step < chunks + late))
            def _():
                stage(step - late)

    unpack_copy.wait_send()

    @pl.loop(0, chunks)
    def _(c):
        for o in range(1, group):
            a2a(c, o, j).wait_send()
        outward_sends(c, gone)
        homeward_sends(c, gone)
        for o in range(group):
            final(c, o, j).wait_send()
        for a in range(3):
            written(c, a).wait()


def hand_over(from_ref, to_ref, held, in_s, out_s):
    def part(n, inward):
        rows = pl.ds(n * 16, 16)
        if inward:
            return pltpu.make_async_copy(from_ref.at[:, rows], held.at[:, rows], in_s.at[n])
        return pltpu.make_async_copy(held.at[:, rows], to_ref.at[:, rows], out_s.at[n])

    for n in range(8):
        part(n, True).start()
    for n in range(8):
        part(n, True).wait()
        part(n, False).start()
    for n in range(8):
        part(n, False).wait()


def fused_body(sections, queries, key_cells, value_cells, grad_cells, packing, segment_ids):
    cell_count, width = queries.shape[1:]
    devices = lax.axis_size("dp")
    group = devices // 4
    planes = devices // group
    chunks = width // CHUNK
    vmem = pl.BlockSpec(memory_space=pltpu.VMEM)
    far = pl.BlockSpec(memory_space=pl.ANY)
    bf16 = jnp.bfloat16
    sem = pltpu.SemaphoreType.DMA
    result = pl.pallas_call(
        functools.partial(kernel, group, planes, sections, chunks, width),
        out_shape=jax.ShapeDtypeStruct((1, cell_count, 3 * width), bf16),
        in_specs=[far] * 4 + [vmem] * 2,
        out_specs=far,
        scratch_shapes=[
            pltpu.VMEM((chunks, 4, 128, CHUNK), bf16),
            pltpu.VMEM((chunks, 4, 128, CHUNK), bf16),
            pltpu.VMEM((chunks, 4, 256, CHUNK), bf16),
            pltpu.VMEM((chunks, GROUPS, 32, CHUNK), bf16),
            pltpu.VMEM((chunks, GROUPS, 32, CHUNK), bf16),
            pltpu.VMEM((chunks, GROUPS, 24 * CHUNK // HEAD_DIM, HEAD_DIM), bf16),
            pltpu.VMEM((chunks, GROUPS, 24 * CHUNK // HEAD_DIM, HEAD_DIM), bf16),
            pltpu.VMEM((chunks, 3, 128, CHUNK), bf16),
            pltpu.VMEM((chunks, 3, 128, CHUNK), bf16),
            pltpu.VMEM((128, 128), bf16),
            pltpu.VMEM((chunks, 3, 128, CHUNK), bf16),
            pltpu.VMEM((224, 256), jnp.float32),
            pltpu.VMEM((224, 1), jnp.float32),
            pltpu.VMEM((128, 128), bf16),
            pltpu.VMEM((128, 128), bf16),
            pltpu.VMEM((96, 128), bf16),
            pltpu.VMEM((128, 96), bf16),
            pltpu.VMEM((segment_ids.shape[1] // 128 + 8, 128), jnp.int32),
            sem((chunks, 4)),
            sem((chunks, group - 1)), sem((chunks, group - 1)),
            sem((chunks, 4)), sem((chunks, 4)),
            sem((chunks, 4)), sem((chunks, 4)),
            sem((chunks, group)), sem((chunks, group)),
            sem, sem, sem((chunks, 3)),
        ],
        compiler_params=pltpu.CompilerParams(
            collective_id=0, has_side_effects=True, vmem_limit_bytes=60 * 1024 * 1024
        ),
    )(queries, key_cells, value_cells, grad_cells, packing, segment_ids)
    return pl.pallas_call(
        hand_over,
        out_shape=jax.ShapeDtypeStruct(result.shape, bf16),
        in_specs=[far],
        out_specs=far,
        scratch_shapes=[pltpu.VMEM(result.shape, bf16), sem((8,)), sem((8,))],
        compiler_params=pltpu.CompilerParams(vmem_limit_bytes=60 * 1024 * 1024),
    )(result)


def solution(mesh):
    sections, devices = mesh.shape["section"], mesh.shape["dp"]

    def body_of(queries, *rest):
        fits = queries.shape[1] == 128 and queries.shape[2] % CHUNK == 0 and devices == 16
        if fits:
            return fused_body(sections, queries, *rest)
        return body(queries, *rest)

    return jax.shard_map(
        body_of,
        mesh=mesh,
        in_specs=(
            P("section", "dp", None),
            P("section", "dp", None),
            P("section", "dp", None),
            P("section", "dp", None),
            P("section", "dp", None),
            P("section", None),
        ),
        out_specs=P("section", "dp", None),
        check_vma=False,
    )
```

```python
import functools
import jax
import jax.numpy as jnp
from jax import lax
from jax.sharding import PartitionSpec as P
from jax.experimental import pallas as pl
from jax.experimental.pallas import tpu as pltpu

HEADS = 20
HEAD_DIM = 128
CHUNK = 256
MESH = pl.DeviceIdType.MESH
NEG = -1e30
LOG2_E = 1.4426950408889634
GROUPS = 12
INNER, TURN = 40, 32


def with_halo(value, sides, width):
    for axis, dim in sides:
        size, length = (lax.axis_size(axis), value.shape[dim])
        up = [(i, (i + 1) % size) for i in range(size - 1)]
        down = [(j, i) for i, j in up]
        last = lax.slice_in_dim(value, length - width, length, axis=dim)
        initial = lax.slice_in_dim(value, 0, width, axis=dim)
        before = lax.ppermute(last, axis, up)
        after = lax.ppermute(initial, axis, down)
        value = jnp.concatenate([before, value, after], axis=dim)
    return value


def passed_along(value, axis, steps):
    count = lax.axis_size(axis)
    initial, last = (max(0, -steps), min(count, count - steps))
    return lax.ppermute(value, axis, [(source, source + steps) for source in range(initial, last)])


def from_behind(block, axis, distance):
    devices = range(lax.axis_size(axis))
    route = [((i - distance) % len(devices), i) for i in devices]
    return lax.ppermute(block, axis, route)


def heads_of(matrix):
    return matrix.reshape(matrix.shape[0], HEADS, HEAD_DIM)


def masked_scores(query_rows, key_rows, query_ids, key_ids):
    scores = jnp.einsum(
        "ihd,jhd->hij", heads_of(query_rows), heads_of(key_rows), preferred_element_type=jnp.float32
    )
    scores = scores * HEAD_DIM ** (-0.5)
    allowed = (query_ids[:, None] == key_ids[None, :])[None]
    return jnp.where(allowed, scores, -jnp.inf)


def body(queries, key_cells, value_cells, grad_cells, packing, segment_ids):
    cell_count = queries.shape[1]
    width = queries.shape[2]
    groups = lax.axis_size("dp")
    per_peer = cell_count // groups
    reach = cell_count // 4
    place = lax.axis_index("dp")
    scale = HEAD_DIM ** (-0.5)
    order = packing[0, 0]

    def pack(matrix):
        return matrix[0][order].reshape(groups, per_peer, width)

    arrived = (
        lax.all_to_all(pack(queries), "dp", split_axis=0, concat_axis=0, tiled=True),
        lax.all_to_all(pack(key_cells), "dp", split_axis=0, concat_axis=0, tiled=True),
        lax.all_to_all(pack(value_cells), "dp", split_axis=0, concat_axis=0, tiled=True),
        lax.all_to_all(pack(grad_cells), "dp", split_axis=0, concat_axis=0, tiled=True),
    )
    own_q, own_k, own_v, own_g = [piece.reshape(cell_count, width) for piece in arrived]
    rim_ids = jnp.full((reach,), -1, jnp.int32)
    padded_ids = jnp.concatenate([rim_ids, segment_ids[0], rim_ids])
    window_ids = lax.dynamic_slice_in_dim(padded_ids, place * cell_count, cell_count + 2 * reach)
    own_ids = window_ids[reach : reach + cell_count]
    key_value = jnp.concatenate([own_k, own_v], axis=1)
    key_value_window = with_halo(key_value, (("dp", 0),), reach)
    key_window = key_value_window[:, :width]
    value_window = key_value_window[:, width:]
    scores = masked_scores(own_q, key_window, own_ids, window_ids)
    top = jnp.max(scores, axis=2)
    log_total = top + jnp.log(jnp.sum(jnp.exp(scores - top[:, :, None]), axis=2))
    probs = jnp.exp(scores - log_total[:, :, None])
    probs_low = probs.astype(jnp.bfloat16)
    grad_heads = heads_of(own_g)
    attended = jnp.einsum(
        "hij,jhd->ihd", probs_low, heads_of(value_window), preferred_element_type=jnp.float32
    )
    delta = jnp.sum(grad_heads.astype(jnp.float32) * attended, axis=2).T
    dprobs = jnp.einsum(
        "ihd,jhd->hij", grad_heads, heads_of(value_window), preferred_element_type=jnp.float32
    )
    dscores = (probs * (dprobs - delta[:, :, None]) * scale).astype(jnp.bfloat16)
    grad_query = jnp.einsum(
        "hij,jhd->ihd", dscores, heads_of(key_window), preferred_element_type=jnp.float32
    )
    grad_query = grad_query.reshape(cell_count, width).astype(jnp.bfloat16)
    window = cell_count + 2 * reach
    grad_key = jnp.einsum(
        "hij,ihd->jhd", dscores, heads_of(own_q), preferred_element_type=jnp.float32
    )
    grad_value = jnp.einsum(
        "hij,ihd->jhd", probs_low, grad_heads, preferred_element_type=jnp.float32
    )
    partial_value = jnp.concatenate(
        [grad_key.reshape(window, width), grad_value.reshape(window, width)], axis=1
    )
    from_after = passed_along(partial_value[:reach].astype(jnp.bfloat16), "dp", -1).astype(
        jnp.float32
    )
    from_before = passed_along(
        partial_value[reach + cell_count :].astype(jnp.bfloat16), "dp", 1
    ).astype(jnp.float32)
    summed = partial_value[reach : reach + cell_count]
    summed = summed.at[cell_count - reach :].add(from_after)
    summed = summed.at[:reach].add(from_before)
    packed_grads = jnp.concatenate([grad_query, summed.astype(jnp.bfloat16)], axis=1)
    returned = lax.all_to_all(
        packed_grads.reshape(groups, per_peer, 3 * width),
        "dp",
        split_axis=0,
        concat_axis=0,
        tiled=True,
    )
    returned = returned.reshape(cell_count, 3 * width)
    inverse = (
        jnp.zeros((cell_count,), jnp.int32).at[order].set(jnp.arange(cell_count, dtype=jnp.int32))
    )
    loaded_order = returned[inverse]
    handed = from_behind(loaded_order, "section", -1)
    return handed[None]


def dot_nt(a, b):
    return lax.dot_general(a, b, (((1,), (1,)), ((), ())), preferred_element_type=jnp.float32)


def dot_tn(a, b):
    return lax.dot_general(a, b, (((0,), (0,)), ((), ())), preferred_element_type=jnp.float32)


def dot_nn(a, b):
    return jnp.dot(a, b, preferred_element_type=jnp.float32)


def one_hot(index, dim, shape):
    return jnp.where(lax.broadcasted_iota(jnp.int32, shape, dim) == index, 1.0, 0.0).astype(jnp.bfloat16)


def small(x):
    return x.astype(jnp.float32).astype(jnp.bfloat16)


def upright(row):
    eye = one_hot(lax.broadcasted_iota(jnp.int32, (1, 128), 1), 0, (128, 128))
    column = dot_nt(eye, small(jnp.broadcast_to(row, (16, 128))))
    return column[:, 0:1].astype(jnp.int32)


def directions(tails, heads, turn):
    subset = lax.broadcasted_iota(jnp.int32, (4, 128), 1)
    number = lax.broadcasted_iota(jnp.int32, (4, 128), 0)
    chosen = jnp.where(number == 0, subset, jnp.where(number == 1, subset // 2, subset // 4))
    chosen = jnp.where(number == 3, subset // 8, chosen) % 2
    right, left = chosen * tails, (1 - chosen) * heads

    def total(x, rows):
        return sum(x[i : i + 1] for i in rows)

    inner = (total(right, range(4)) <= INNER) & (total(left, range(4)) <= INNER)
    turned = (total(right, range(3)) <= TURN) & (total(left, range(3)) <= TURN)
    turned = turned & (right[3:4] <= 16) & (left[3:4] <= 16)
    fits = jnp.where(turn, turned.astype(jnp.int32), inner.astype(jnp.int32))
    best = jnp.where((fits == 1) & (subset[0:1] < 16), subset[0:1], 16).astype(jnp.float32)
    best = jnp.min(best, axis=1, keepdims=True).astype(jnp.int32)
    picked = subset == best

    def at_best(x):
        return jnp.sum(jnp.where(picked, x, 0).astype(jnp.float32), axis=1, keepdims=True).astype(jnp.int32)

    go, right, left = at_best(chosen), at_best(right), at_best(left)

    def first_slots(x):
        starts = [jnp.zeros_like(x[0:1])]
        for i in range(3):
            starts.append(starts[i] + x[i : i + 1])
        starts[3] = jnp.where(turn, TURN, starts[3])
        return jnp.concatenate(starts, axis=0)

    return go, first_slots(right), first_slots(left)


def boundary_plan(ids_ref, blocks, planes, z, j):
    reach = 128 // 4
    count = ids_ref.shape[1] // 128
    blocks[...] = jnp.full(blocks.shape, -1, jnp.int32)
    for b in range(count):
        blocks[b + 1 : b + 2, :] = ids_ref[:, b * 128 : (b + 1) * 128]
    here, ahead, behind = [
        jnp.concatenate([blocks[pl.ds(4 * j + k + d, 1), :] for k in range(4)], axis=0) for d in (1, 2, 0)
    ]
    span = 128 // planes
    first_plane, last_plane = z == 0, z == planes - 1
    place = lax.broadcasted_iota(jnp.int32, (4, 128), 1)
    inside = place < reach

    def turned(x, plane):
        return pltpu.roll(x, lax.rem(2 * 128 - plane * span, 128), 1)

    own = turned(here, z)
    prior = turned(jnp.where(first_plane, behind, here), z - 1)
    later = turned(jnp.where(last_plane, ahead, here), z + 1)

    def matching(x, value, straddles):
        hits = jnp.sum(jnp.where(inside & (x == value), 1.0, 0.0), axis=1, keepdims=True)
        return jnp.where(straddles, hits, 0.0).astype(jnp.int32)

    first, last = own[:, 0:1], own[:, reach - 1 : reach]
    before, after = prior[:, reach - 1 : reach], later[:, 0:1]
    tail_r, head_r = [matching(x, last, last == after) for x in (own, later)]
    tail_l, head_l = [matching(x, first, first == before) for x in (prior, own)]
    go_r, right_r, left_r = directions(tail_r, head_r, last_plane)

    def shifted(x, by):
        rows = [x[(i + by) % 4 : (i + by) % 4 + 1] for i in range(4)]
        return jnp.where(first_plane, jnp.concatenate(rows, axis=0), x)

    go_l, right_l, left_l = [
        shifted(x, 3) for x in directions(shifted(tail_l, 1), shifted(head_l, 1), first_plane)
    ]
    sent_r, sent_l = jnp.where(go_r == 1, tail_r, 0), jnp.where(go_l == 0, head_l, 0)
    got_l, got_r = jnp.where(go_l == 1, tail_l, 0), jnp.where(go_r == 0, head_r, 0)
    begin = reach - sent_r
    slots = jnp.where(
        inside & (place >= begin),
        right_r + place - begin,
        jnp.where(place < sent_l, 48 + left_l + place, -1),
    )
    kept = jnp.where(slots >= 0, -1, own)
    lane = lax.broadcasted_iota(jnp.int32, (1, 128), 1)
    route = one_hot(lane // 32 * 8 + lane % 8, 0, (128, 128))
    block = lane // 8 % 4

    def arrival(x):
        moved = dot_nn(small(jnp.concatenate([x] * 4, axis=0)), route)
        total = jnp.zeros((1, 128), jnp.float32)
        for k in range(4):
            total = total + jnp.where(block == k, moved[k : k + 1], 0.0)
        return total.astype(jnp.int32)

    left_hit = (place >= right_l) & (place < right_l + got_l)
    right_hit = (place >= 48 + left_r) & (place < 48 + left_r + got_r)
    foreign = jnp.where(left_hit, first, jnp.where(right_hit, last, -1))
    foreign = jnp.max(foreign.astype(jnp.float32), axis=0, keepdims=True).astype(jnp.int32)
    return arrival(slots), arrival(kept), foreign


def kernel(
    group, planes, sections, chunks, width,
    q_ref, k_ref, v_ref, g_ref, packing_ref, ids_ref,
    out_ref,
    loaded, packed, win, halo, halo_in, back_out, back_in, fin_out, fin_in, unpack_in, placed, bias, valid,
    pack_ref, unpack_ref, pick_ref, place_ref, blocks, load_s,
    a2a_s, a2a_r, halo_s, halo_r, back_s, back_r, fin_s, fin_r, un_s, un_r, put_s,
):
    t = lax.axis_index("section")
    me = lax.axis_index("dp")
    z, j = lax.div(me, group), lax.rem(me, group)
    rows = 128 // group
    before = lax.rem(t + sections - 1, sections)
    after = lax.rem(t + 1, sections)
    zr, zl = lax.rem(z + 1, planes), lax.rem(z + planes - 1, planes)
    jr = lax.rem(j + jnp.where(z == planes - 1, 1, 0), group)
    jl = lax.rem(j + group - jnp.where(z == 0, 1, 0), group)
    sides = (zr * group + j, zr * group + jr, zl * group + j, zl * group + jl)
    mates = [lax.rem(j + o, group) for o in range(group)]
    sources = [lax.rem(j + group - o, group) for o in range(group)]

    def columns(start):
        return pl.ds(pl.multiple_of(start, 128), CHUNK)

    def load(c, a):
        ref = (q_ref, k_ref, v_ref, g_ref)[a]
        return pltpu.make_async_copy(ref.at[0, :, columns(c * CHUNK)], loaded.at[c, a], load_s.at[c, a])

    @pl.loop(0, chunks)
    def _(c):
        for n in (5, 11):
            halo_in[c, n] = jnp.zeros(halo_in.shape[2:], jnp.bfloat16)
            back_in[c, n] = jnp.zeros(back_in.shape[2:], jnp.bfloat16)

    for a in range(4):
        load(0, a).start()

    barrier = pltpu.get_barrier_semaphore()
    for o in range(1, group):
        pl.semaphore_signal(barrier, inc=1, device_id=(t, z * group + mates[o]), device_id_type=MESH)
    for side in sides:
        pl.semaphore_signal(barrier, inc=1, device_id=(t, side), device_id_type=MESH)
    for o in range(group):
        pl.semaphore_signal(barrier, inc=1, device_id=(after, z * group + mates[o]), device_id_type=MESH)

    @pl.loop(1, chunks)
    def _(c):
        for a in range(4):
            load(c, a).start()

    order = packing_ref[0]
    unpack_ref[...] = one_hot(order, 0, (128, 128))
    pack_ref[...] = one_hot(upright(order), 1, (128, 128))
    pl.semaphore_wait(barrier, 2 * group + 3)

    def at_rows(ref, c, start, count):
        if not isinstance(start, int):
            start = pl.multiple_of(start, 16)
        return ref.at[c, :, pl.ds(start, count), :]

    def a2a(c, o, landing):
        return pltpu.make_async_remote_copy(
            src_ref=at_rows(packed, c, mates[o] * rows, rows),
            dst_ref=at_rows(win, c, landing * rows, rows),
            send_sem=a2a_s.at[c, o - 1],
            recv_sem=a2a_r.at[c, o - 1],
            device_id=(t, z * group + mates[o]),
            device_id_type=MESH,
        )

    last_plane, first_plane = z == planes - 1, z == 0
    right_a, right_b, left_a, left_b = sides
    rightward = (((0, 5, 0, right_a),), ((0, 4, 0, right_a), (4, 2, 1, right_b)))
    leftward = (((6, 5, 2, left_a),), ((6, 4, 2, left_a), (10, 2, 3, left_b)))
    returned_left = (((0, 5, 0, left_a),), ((0, 4, 0, left_a), (4, 2, 1, left_b)))
    returned_right = (((6, 5, 2, right_a),), ((6, 4, 2, right_a), (10, 2, 3, right_b)))

    def each(copies, turn, act):
        for n in range(2):
            @pl.when(turn if n == 1 else jnp.logical_not(turn))
            def _():
                for copy in copies[n]:
                    act(*copy)

    def outward(c, act):
        def one(first, count, n, target):
            act(pltpu.make_async_remote_copy(
                src_ref=halo.at[c, pl.ds(first, count)],
                dst_ref=halo_in.at[c, pl.ds(first, count)],
                send_sem=halo_s.at[c, n],
                recv_sem=halo_r.at[c, n],
                device_id=(t, target),
                device_id_type=MESH,
            ))
        return one

    def homeward(c, act):
        def one(first, count, n, target):
            act(pltpu.make_async_remote_copy(
                src_ref=back_out.at[c, pl.ds(first, count)],
                dst_ref=back_in.at[c, pl.ds(first, count)],
                send_sem=back_s.at[c, n],
                recv_sem=back_r.at[c, n],
                device_id=(t, target),
                device_id_type=MESH,
            ))
        return one

    def start(copy):
        copy.start()

    def landed(copy):
        copy.wait_recv()

    def gone(copy):
        copy.wait_send()

    def outward_sends(c, act):
        each(rightward, last_plane, outward(c, act))
        each(leftward, first_plane, outward(c, act))

    def outward_arrivals(c):
        each(returned_left, first_plane, outward(c, landed))
        each(returned_right, last_plane, outward(c, landed))

    def homeward_sends(c, act):
        each(returned_left, first_plane, homeward(c, act))
        each(returned_right, last_plane, homeward(c, act))

    def homeward_arrivals(c):
        each(rightward, last_plane, homeward(c, landed))
        each(leftward, first_plane, homeward(c, landed))

    def final(c, o, landing):
        return pltpu.make_async_remote_copy(
            src_ref=at_rows(fin_out, c, mates[o] * rows, rows),
            dst_ref=at_rows(fin_in, c, landing * rows, rows),
            send_sem=fin_s.at[c, o],
            recv_sem=fin_r.at[c, o],
            device_id=(before, z * group + mates[o]),
            device_id_type=MESH,
        )

    unpack_copy = pltpu.make_async_remote_copy(
        src_ref=unpack_ref, dst_ref=unpack_in, send_sem=un_s, recv_sem=un_r,
        device_id=(before, me), device_id_type=MESH,
    )
    unpack_copy.start()

    def hand_out(c):
        for a in range(4):
            load(c, a).wait()
            packed[c, a] = dot_nn(pack_ref[...], loaded[c, a]).astype(jnp.bfloat16)
        for o in range(1, group):
            a2a(c, o, j).start()
        own = pl.ds(pl.multiple_of(j * rows, 16), rows)
        for a in range(4):
            win[c, a, own, :] = packed[c, a, own, :]
            win[c, a, 224:256, :] = jnp.zeros((32, CHUNK), jnp.bfloat16)

    @pl.loop(0, 2)
    def _(c):
        hand_out(c)

    slots, kept, foreign = boundary_plan(ids_ref, blocks, planes, z, j)
    pick_ref[...] = one_hot(slots, 0, (96, 128))
    place_ref[...] = one_hot(upright(slots), 1, (128, 96))
    id_row = jnp.concatenate([kept, foreign], axis=1)
    id_col = jnp.concatenate([upright(kept), upright(foreign)], axis=0)
    id_col = id_col[0:224]
    bias[...] = jnp.where((id_col == id_row) & (id_row >= 0), 0.0, NEG)
    valid[...] = jnp.where(id_col >= 0, 1.0, 0.0)
    scale = HEAD_DIM ** (-0.5)

    def spread(c):
        for o in range(1, group):
            a2a(c, o, sources[o]).wait_recv()
        picked = [
            dot_nn(pick_ref[...], win[c, a, 0:128, :]).reshape(GROUPS, 8, CHUNK) for a in range(4)
        ]
        for a in (0, 2):
            pair = jnp.concatenate(picked[a : a + 2], axis=1)
            halo[c, :, a * 8 : a * 8 + 16, :] = pair.astype(jnp.bfloat16)
        outward_sends(c, start)

    def attend(c):
        outward_arrivals(c)
        for a in (0, 2):
            pair = halo_in[c, :, a * 8 : a * 8 + 16, :].astype(jnp.float32)
            for n in range(2):
                cells = pair[:, n * 8 : n * 8 + 8].reshape(GROUPS * 8, CHUNK)
                win[c, a + n, 128:224, :] = cells.astype(jnp.bfloat16)
        foreign = []
        for h in range(CHUNK // HEAD_DIM):
            head = slice(h * HEAD_DIM, (h + 1) * HEAD_DIM)
            q, g = [win[c, a, 0:224, head] for a in (0, 3)]
            k, v = [win[c, a, :, head] for a in (1, 2)]
            s = dot_nt(q, k) * (scale * LOG2_E) + bias[...]
            e = jnp.exp2(s - jnp.max(s, axis=1, keepdims=True))
            p = e * (valid[...] / jnp.sum(e, axis=1, keepdims=True))
            low = p.astype(jnp.bfloat16)
            dp = dot_nt(g, v)
            delta = jnp.sum(low.astype(jnp.float32) * dp, axis=1, keepdims=True)
            ds = (p * (dp - delta) * scale).astype(jnp.bfloat16)
            for a, grad in enumerate((dot_nn(ds, k), dot_tn(ds, q), dot_tn(low, g))):
                fin_out[c, a, :, head] = grad[0:128].astype(jnp.bfloat16)
                foreign.append(grad[128:224].reshape(GROUPS, 8, HEAD_DIM))
                if len(foreign) % 2 == 0:
                    pair = jnp.concatenate(foreign[-2:], axis=1)
                    last = len(foreign) * 8
                    back_out[c, :, last - 16 : last, :] = pair.astype(jnp.bfloat16)
        homeward_sends(c, start)

    def hand_on(c):
        homeward_arrivals(c)
        foreign = []
        for n in range(0, 3 * CHUNK // HEAD_DIM, 2):
            pair = back_in[c, :, n * 8 : n * 8 + 16, :].astype(jnp.float32)
            for i in range(2):
                foreign.append(pair[:, i * 8 : i * 8 + 8].reshape(GROUPS * 8, HEAD_DIM))
        for a in range(3):
            returned = dot_nn(place_ref[...], jnp.concatenate(foreign[a::3], axis=1).astype(jnp.bfloat16))
            fin_out[c, a] = (fin_out[c, a].astype(jnp.float32) + returned).astype(jnp.bfloat16)
        for o in range(group):
            final(c, o, j).start()

    def written(c, a):
        return pltpu.make_async_copy(
            placed.at[c, a], out_ref.at[0, :, columns(a * width + c * CHUNK)], put_s.at[c, a]
        )

    def finish(c):
        @pl.when(c == 0)
        def _():
            unpack_copy.wait_recv()

        for o in range(group):
            final(c, o, sources[o]).wait_recv()
        for a in range(3):
            placed[c, a] = dot_nn(unpack_in[...], fin_in[c, a]).astype(jnp.bfloat16)
            written(c, a).start()

    stages = (spread, attend, hand_on, finish, hand_out)
    lead = (2, 5, 8, 10, 0)

    @pl.loop(2, chunks + max(lead))
    def _(step):
        for late, stage in zip(lead, stages):

            @pl.when((step >= late) & (step < chunks + late))
            def _():
                stage(step - late)

    unpack_copy.wait_send()

    @pl.loop(0, chunks)
    def _(c):
        for o in range(1, group):
            a2a(c, o, j).wait_send()
        outward_sends(c, gone)
        homeward_sends(c, gone)
        for o in range(group):
            final(c, o, j).wait_send()
        for a in range(3):
            written(c, a).wait()


def hand_over(from_ref, to_ref, held, in_s, out_s):
    def part(n, inward):
        rows = pl.ds(n * 16, 16)
        if inward:
            return pltpu.make_async_copy(from_ref.at[:, rows], held.at[:, rows], in_s.at[n])
        return pltpu.make_async_copy(held.at[:, rows], to_ref.at[:, rows], out_s.at[n])

    for n in range(8):
        part(n, True).start()
    for n in range(8):
        part(n, True).wait()
        part(n, False).start()
    for n in range(8):
        part(n, False).wait()


def fused_body(sections, queries, key_cells, value_cells, grad_cells, packing, segment_ids):
    cell_count, width = queries.shape[1:]
    devices = lax.axis_size("dp")
    group = devices // 4
    planes = devices // group
    chunks = width // CHUNK
    vmem = pl.BlockSpec(memory_space=pltpu.VMEM)
    far = pl.BlockSpec(memory_space=pl.ANY)
    bf16 = jnp.bfloat16
    sem = pltpu.SemaphoreType.DMA
    result = pl.pallas_call(
        functools.partial(kernel, group, planes, sections, chunks, width),
        out_shape=jax.ShapeDtypeStruct((1, cell_count, 3 * width), bf16),
        in_specs=[far] * 4 + [vmem] * 2,
        out_specs=far,
        scratch_shapes=[
            pltpu.VMEM((chunks, 4, 128, CHUNK), bf16),
            pltpu.VMEM((chunks, 4, 128, CHUNK), bf16),
            pltpu.VMEM((chunks, 4, 256, CHUNK), bf16),
            pltpu.VMEM((chunks, GROUPS, 32, CHUNK), bf16),
            pltpu.VMEM((chunks, GROUPS, 32, CHUNK), bf16),
            pltpu.VMEM((chunks, GROUPS, 24 * CHUNK // HEAD_DIM, HEAD_DIM), bf16),
            pltpu.VMEM((chunks, GROUPS, 24 * CHUNK // HEAD_DIM, HEAD_DIM), bf16),
            pltpu.VMEM((chunks, 3, 128, CHUNK), bf16),
            pltpu.VMEM((chunks, 3, 128, CHUNK), bf16),
            pltpu.VMEM((128, 128), bf16),
            pltpu.VMEM((chunks, 3, 128, CHUNK), bf16),
            pltpu.VMEM((224, 256), jnp.float32),
            pltpu.VMEM((224, 1), jnp.float32),
            pltpu.VMEM((128, 128), bf16),
            pltpu.VMEM((128, 128), bf16),
            pltpu.VMEM((96, 128), bf16),
            pltpu.VMEM((128, 96), bf16),
            pltpu.VMEM((segment_ids.shape[1] // 128 + 8, 128), jnp.int32),
            sem((chunks, 4)),
            sem((chunks, group - 1)), sem((chunks, group - 1)),
            sem((chunks, 4)), sem((chunks, 4)),
            sem((chunks, 4)), sem((chunks, 4)),
            sem((chunks, group)), sem((chunks, group)),
            sem, sem, sem((chunks, 3)),
        ],
        compiler_params=pltpu.CompilerParams(
            collective_id=0, has_side_effects=True, vmem_limit_bytes=60 * 1024 * 1024
        ),
    )(queries, key_cells, value_cells, grad_cells, packing, segment_ids)
    return pl.pallas_call(
        hand_over,
        out_shape=jax.ShapeDtypeStruct(result.shape, bf16),
        in_specs=[far],
        out_specs=far,
        scratch_shapes=[pltpu.VMEM(result.shape, bf16), sem((8,)), sem((8,))],
        compiler_params=pltpu.CompilerParams(vmem_limit_bytes=60 * 1024 * 1024),
    )(result)


def solution(mesh):
    sections, devices = mesh.shape["section"], mesh.shape["dp"]

    def body_of(queries, *rest):
        fits = queries.shape[1] == 128 and queries.shape[2] % CHUNK == 0 and devices == 16
        if fits:
            return fused_body(sections, queries, *rest)
        return body(queries, *rest)

    return jax.shard_map(
        body_of,
        mesh=mesh,
        in_specs=(
            P("section", "dp", None),
            P("section", "dp", None),
            P("section", "dp", None),
            P("section", "dp", None),
            P("section", "dp", None),
            P("section", None),
        ),
        out_specs=P("section", "dp", None),
        check_vma=False,
    )
```

```python
import functools
import jax
import jax.numpy as jnp
from jax import lax
from jax.sharding import PartitionSpec as P
from jax.experimental import pallas as pl
from jax.experimental.pallas import tpu as pltpu

HEADS = 20
HEAD_DIM = 128
CHUNK = 256
MESH = pl.DeviceIdType.MESH
NEG = -1e30
LOG2_E = 1.4426950408889634
GROUPS = 12
INNER, TURN = 40, 32


def with_halo(value, sides, width):
    for axis, dim in sides:
        size, length = (lax.axis_size(axis), value.shape[dim])
        up = [(i, (i + 1) % size) for i in range(size - 1)]
        down = [(j, i) for i, j in up]
        last = lax.slice_in_dim(value, length - width, length, axis=dim)
        initial = lax.slice_in_dim(value, 0, width, axis=dim)
        before = lax.ppermute(last, axis, up)
        after = lax.ppermute(initial, axis, down)
        value = jnp.concatenate([before, value, after], axis=dim)
    return value


def passed_along(value, axis, steps):
    count = lax.axis_size(axis)
    initial, last = (max(0, -steps), min(count, count - steps))
    return lax.ppermute(value, axis, [(source, source + steps) for source in range(initial, last)])


def from_behind(block, axis, distance):
    devices = range(lax.axis_size(axis))
    route = [((i - distance) % len(devices), i) for i in devices]
    return lax.ppermute(block, axis, route)


def heads_of(matrix):
    return matrix.reshape(matrix.shape[0], HEADS, HEAD_DIM)


def masked_scores(query_rows, key_rows, query_ids, key_ids):
    scores = jnp.einsum(
        "ihd,jhd->hij", heads_of(query_rows), heads_of(key_rows), preferred_element_type=jnp.float32
    )
    scores = scores * HEAD_DIM ** (-0.5)
    allowed = (query_ids[:, None] == key_ids[None, :])[None]
    return jnp.where(allowed, scores, -jnp.inf)


def body(queries, key_cells, value_cells, grad_cells, packing, segment_ids):
    cell_count = queries.shape[1]
    width = queries.shape[2]
    groups = lax.axis_size("dp")
    per_peer = cell_count // groups
    reach = cell_count // 4
    place = lax.axis_index("dp")
    scale = HEAD_DIM ** (-0.5)
    order = packing[0, 0]

    def pack(matrix):
        return matrix[0][order].reshape(groups, per_peer, width)

    arrived = (
        lax.all_to_all(pack(queries), "dp", split_axis=0, concat_axis=0, tiled=True),
        lax.all_to_all(pack(key_cells), "dp", split_axis=0, concat_axis=0, tiled=True),
        lax.all_to_all(pack(value_cells), "dp", split_axis=0, concat_axis=0, tiled=True),
        lax.all_to_all(pack(grad_cells), "dp", split_axis=0, concat_axis=0, tiled=True),
    )
    own_q, own_k, own_v, own_g = [piece.reshape(cell_count, width) for piece in arrived]
    rim_ids = jnp.full((reach,), -1, jnp.int32)
    padded_ids = jnp.concatenate([rim_ids, segment_ids[0], rim_ids])
    window_ids = lax.dynamic_slice_in_dim(padded_ids, place * cell_count, cell_count + 2 * reach)
    own_ids = window_ids[reach : reach + cell_count]
    key_value = jnp.concatenate([own_k, own_v], axis=1)
    key_value_window = with_halo(key_value, (("dp", 0),), reach)
    key_window = key_value_window[:, :width]
    value_window = key_value_window[:, width:]
    scores = masked_scores(own_q, key_window, own_ids, window_ids)
    top = jnp.max(scores, axis=2)
    log_total = top + jnp.log(jnp.sum(jnp.exp(scores - top[:, :, None]), axis=2))
    probs = jnp.exp(scores - log_total[:, :, None])
    probs_low = probs.astype(jnp.bfloat16)
    grad_heads = heads_of(own_g)
    attended = jnp.einsum(
        "hij,jhd->ihd", probs_low, heads_of(value_window), preferred_element_type=jnp.float32
    )
    delta = jnp.sum(grad_heads.astype(jnp.float32) * attended, axis=2).T
    dprobs = jnp.einsum(
        "ihd,jhd->hij", grad_heads, heads_of(value_window), preferred_element_type=jnp.float32
    )
    dscores = (probs * (dprobs - delta[:, :, None]) * scale).astype(jnp.bfloat16)
    grad_query = jnp.einsum(
        "hij,jhd->ihd", dscores, heads_of(key_window), preferred_element_type=jnp.float32
    )
    grad_query = grad_query.reshape(cell_count, width).astype(jnp.bfloat16)
    window = cell_count + 2 * reach
    grad_key = jnp.einsum(
        "hij,ihd->jhd", dscores, heads_of(own_q), preferred_element_type=jnp.float32
    )
    grad_value = jnp.einsum(
        "hij,ihd->jhd", probs_low, grad_heads, preferred_element_type=jnp.float32
    )
    partial_value = jnp.concatenate(
        [grad_key.reshape(window, width), grad_value.reshape(window, width)], axis=1
    )
    from_after = passed_along(partial_value[:reach].astype(jnp.bfloat16), "dp", -1).astype(
        jnp.float32
    )
    from_before = passed_along(
        partial_value[reach + cell_count :].astype(jnp.bfloat16), "dp", 1
    ).astype(jnp.float32)
    summed = partial_value[reach : reach + cell_count]
    summed = summed.at[cell_count - reach :].add(from_after)
    summed = summed.at[:reach].add(from_before)
    packed_grads = jnp.concatenate([grad_query, summed.astype(jnp.bfloat16)], axis=1)
    returned = lax.all_to_all(
        packed_grads.reshape(groups, per_peer, 3 * width),
        "dp",
        split_axis=0,
        concat_axis=0,
        tiled=True,
    )
    returned = returned.reshape(cell_count, 3 * width)
    inverse = (
        jnp.zeros((cell_count,), jnp.int32).at[order].set(jnp.arange(cell_count, dtype=jnp.int32))
    )
    loaded_order = returned[inverse]
    handed = from_behind(loaded_order, "section", -1)
    return handed[None]


def dot_nt(a, b):
    return lax.dot_general(a, b, (((1,), (1,)), ((), ())), preferred_element_type=jnp.float32)


def dot_tn(a, b):
    return lax.dot_general(a, b, (((0,), (0,)), ((), ())), preferred_element_type=jnp.float32)


def dot_nn(a, b):
    return jnp.dot(a, b, preferred_element_type=jnp.float32)


def one_hot(index, dim, shape):
    return jnp.where(lax.broadcasted_iota(jnp.int32, shape, dim) == index, 1.0, 0.0).astype(jnp.bfloat16)


def small(x):
    return x.astype(jnp.float32).astype(jnp.bfloat16)


def upright(row):
    eye = one_hot(lax.broadcasted_iota(jnp.int32, (1, 128), 1), 0, (128, 128))
    column = dot_nt(eye, small(jnp.broadcast_to(row, (16, 128))))
    return column[:, 0:1].astype(jnp.int32)


def directions(tails, heads, turn):
    subset = lax.broadcasted_iota(jnp.int32, (4, 128), 1)
    number = lax.broadcasted_iota(jnp.int32, (4, 128), 0)
    chosen = jnp.where(number == 0, subset, jnp.where(number == 1, subset // 2, subset // 4))
    chosen = jnp.where(number == 3, subset // 8, chosen) % 2
    right, left = chosen * tails, (1 - chosen) * heads

    def total(x, rows):
        return sum(x[i : i + 1] for i in rows)

    inner = (total(right, range(4)) <= INNER) & (total(left, range(4)) <= INNER)
    turned = (total(right, range(3)) <= TURN) & (total(left, range(3)) <= TURN)
    turned = turned & (right[3:4] <= 16) & (left[3:4] <= 16)
    fits = jnp.where(turn, turned.astype(jnp.int32), inner.astype(jnp.int32))
    best = jnp.where((fits == 1) & (subset[0:1] < 16), subset[0:1], 16).astype(jnp.float32)
    best = jnp.min(best, axis=1, keepdims=True).astype(jnp.int32)
    picked = subset == best

    def at_best(x):
        return jnp.sum(jnp.where(picked, x, 0).astype(jnp.float32), axis=1, keepdims=True).astype(jnp.int32)

    go, right, left = at_best(chosen), at_best(right), at_best(left)

    def first_slots(x):
        starts = [jnp.zeros_like(x[0:1])]
        for i in range(3):
            starts.append(starts[i] + x[i : i + 1])
        starts[3] = jnp.where(turn, TURN, starts[3])
        return jnp.concatenate(starts, axis=0)

    return go, first_slots(right), first_slots(left)


def boundary_plan(ids_ref, blocks, planes, z, j):
    reach = 128 // 4
    count = ids_ref.shape[1] // 128
    blocks[...] = jnp.full(blocks.shape, -1, jnp.int32)
    for b in range(count):
        blocks[b + 1 : b + 2, :] = ids_ref[:, b * 128 : (b + 1) * 128]
    here, ahead, behind = [
        jnp.concatenate([blocks[pl.ds(4 * j + k + d, 1), :] for k in range(4)], axis=0) for d in (1, 2, 0)
    ]
    span = 128 // planes
    first_plane, last_plane = z == 0, z == planes - 1
    place = lax.broadcasted_iota(jnp.int32, (4, 128), 1)
    inside = place < reach

    def turned(x, plane):
        return pltpu.roll(x, lax.rem(2 * 128 - plane * span, 128), 1)

    own = turned(here, z)
    prior = turned(jnp.where(first_plane, behind, here), z - 1)
    later = turned(jnp.where(last_plane, ahead, here), z + 1)

    def matching(x, value, straddles):
        hits = jnp.sum(jnp.where(inside & (x == value), 1.0, 0.0), axis=1, keepdims=True)
        return jnp.where(straddles, hits, 0.0).astype(jnp.int32)

    first, last = own[:, 0:1], own[:, reach - 1 : reach]
    before, after = prior[:, reach - 1 : reach], later[:, 0:1]
    tail_r, head_r = [matching(x, last, last == after) for x in (own, later)]
    tail_l, head_l = [matching(x, first, first == before) for x in (prior, own)]
    go_r, right_r, left_r = directions(tail_r, head_r, last_plane)

    def shifted(x, by):
        rows = [x[(i + by) % 4 : (i + by) % 4 + 1] for i in range(4)]
        return jnp.where(first_plane, jnp.concatenate(rows, axis=0), x)

    go_l, right_l, left_l = [
        shifted(x, 3) for x in directions(shifted(tail_l, 1), shifted(head_l, 1), first_plane)
    ]
    sent_r, sent_l = jnp.where(go_r == 1, tail_r, 0), jnp.where(go_l == 0, head_l, 0)
    got_l, got_r = jnp.where(go_l == 1, tail_l, 0), jnp.where(go_r == 0, head_r, 0)
    begin = reach - sent_r
    slots = jnp.where(
        inside & (place >= begin),
        right_r + place - begin,
        jnp.where(place < sent_l, 48 + left_l + place, -1),
    )
    kept = jnp.where(slots >= 0, -1, own)
    lane = lax.broadcasted_iota(jnp.int32, (1, 128), 1)
    route = one_hot(lane // 32 * 8 + lane % 8, 0, (128, 128))
    block = lane // 8 % 4

    def arrival(x):
        moved = dot_nn(small(jnp.concatenate([x] * 4, axis=0)), route)
        total = jnp.zeros((1, 128), jnp.float32)
        for k in range(4):
            total = total + jnp.where(block == k, moved[k : k + 1], 0.0)
        return total.astype(jnp.int32)

    left_hit = (place >= right_l) & (place < right_l + got_l)
    right_hit = (place >= 48 + left_r) & (place < 48 + left_r + got_r)
    foreign = jnp.where(left_hit, first, jnp.where(right_hit, last, -1))
    foreign = jnp.max(foreign.astype(jnp.float32), axis=0, keepdims=True).astype(jnp.int32)
    return arrival(slots), arrival(kept), foreign


def kernel(
    group, planes, sections, chunks, width,
    q_ref, k_ref, v_ref, g_ref, packing_ref, ids_ref,
    out_ref,
    loaded, packed, win, halo, halo_in, back_out, back_in, fin_out, fin_in, unpack_in, placed, bias, valid,
    pack_ref, unpack_ref, pick_ref, place_ref, blocks, load_s,
    a2a_s, a2a_r, halo_s, halo_r, back_s, back_r, fin_s, fin_r, un_s, un_r, put_s,
):
    t = lax.axis_index("section")
    me = lax.axis_index("dp")
    z, j = lax.div(me, group), lax.rem(me, group)
    rows = 128 // group
    before = lax.rem(t + sections - 1, sections)
    after = lax.rem(t + 1, sections)
    zr, zl = lax.rem(z + 1, planes), lax.rem(z + planes - 1, planes)
    jr = lax.rem(j + jnp.where(z == planes - 1, 1, 0), group)
    jl = lax.rem(j + group - jnp.where(z == 0, 1, 0), group)
    sides = (zr * group + j, zr * group + jr, zl * group + j, zl * group + jl)
    mates = [lax.rem(j + o, group) for o in range(group)]
    sources = [lax.rem(j + group - o, group) for o in range(group)]

    def columns(start):
        return pl.ds(pl.multiple_of(start, 128), CHUNK)

    def load(c, a):
        ref = (q_ref, k_ref, v_ref, g_ref)[a]
        return pltpu.make_async_copy(ref.at[0, :, columns(c * CHUNK)], loaded.at[c, a], load_s.at[c, a])

    @pl.loop(0, chunks)
    def _(c):
        for n in (5, 11):
            halo_in[c, n] = jnp.zeros(halo_in.shape[2:], jnp.bfloat16)
            back_in[c, n] = jnp.zeros(back_in.shape[2:], jnp.bfloat16)

    for a in range(4):
        load(0, a).start()

    barrier = pltpu.get_barrier_semaphore()
    for o in range(1, group):
        pl.semaphore_signal(barrier, inc=1, device_id=(t, z * group + mates[o]), device_id_type=MESH)
    for side in sides:
        pl.semaphore_signal(barrier, inc=1, device_id=(t, side), device_id_type=MESH)
    for o in range(group):
        pl.semaphore_signal(barrier, inc=1, device_id=(after, z * group + mates[o]), device_id_type=MESH)

    @pl.loop(1, chunks)
    def _(c):
        for a in range(4):
            load(c, a).start()

    order = packing_ref[0]
    unpack_ref[...] = one_hot(order, 0, (128, 128))
    pack_ref[...] = one_hot(upright(order), 1, (128, 128))
    pl.semaphore_wait(barrier, 2 * group + 3)

    def at_rows(ref, c, start, count):
        if not isinstance(start, int):
            start = pl.multiple_of(start, 16)
        return ref.at[c, :, pl.ds(start, count), :]

    def a2a(c, o, landing):
        return pltpu.make_async_remote_copy(
            src_ref=at_rows(packed, c, mates[o] * rows, rows),
            dst_ref=at_rows(win, c, landing * rows, rows),
            send_sem=a2a_s.at[c, o - 1],
            recv_sem=a2a_r.at[c, o - 1],
            device_id=(t, z * group + mates[o]),
            device_id_type=MESH,
        )

    last_plane, first_plane = z == planes - 1, z == 0
    right_a, right_b, left_a, left_b = sides
    rightward = (((0, 5, 0, right_a),), ((0, 4, 0, right_a), (4, 2, 1, right_b)))
    leftward = (((6, 5, 2, left_a),), ((6, 4, 2, left_a), (10, 2, 3, left_b)))
    returned_left = (((0, 5, 0, left_a),), ((0, 4, 0, left_a), (4, 2, 1, left_b)))
    returned_right = (((6, 5, 2, right_a),), ((6, 4, 2, right_a), (10, 2, 3, right_b)))

    def each(copies, turn, act):
        for n in range(2):
            @pl.when(turn if n == 1 else jnp.logical_not(turn))
            def _():
                for copy in copies[n]:
                    act(*copy)

    def outward(c, act):
        def one(first, count, n, target):
            act(pltpu.make_async_remote_copy(
                src_ref=halo.at[c, pl.ds(first, count)],
                dst_ref=halo_in.at[c, pl.ds(first, count)],
                send_sem=halo_s.at[c, n],
                recv_sem=halo_r.at[c, n],
                device_id=(t, target),
                device_id_type=MESH,
            ))
        return one

    def homeward(c, act):
        def one(first, count, n, target):
            act(pltpu.make_async_remote_copy(
                src_ref=back_out.at[c, pl.ds(first, count)],
                dst_ref=back_in.at[c, pl.ds(first, count)],
                send_sem=back_s.at[c, n],
                recv_sem=back_r.at[c, n],
                device_id=(t, target),
                device_id_type=MESH,
            ))
        return one

    def start(copy):
        copy.start()

    def landed(copy):
        copy.wait_recv()

    def gone(copy):
        copy.wait_send()

    def outward_sends(c, act):
        each(rightward, last_plane, outward(c, act))
        each(leftward, first_plane, outward(c, act))

    def outward_arrivals(c):
        each(returned_left, first_plane, outward(c, landed))
        each(returned_right, last_plane, outward(c, landed))

    def homeward_sends(c, act):
        each(returned_left, first_plane, homeward(c, act))
        each(returned_right, last_plane, homeward(c, act))

    def homeward_arrivals(c):
        each(rightward, last_plane, homeward(c, landed))
        each(leftward, first_plane, homeward(c, landed))

    def final(c, o, landing):
        return pltpu.make_async_remote_copy(
            src_ref=at_rows(fin_out, c, mates[o] * rows, rows),
            dst_ref=at_rows(fin_in, c, landing * rows, rows),
            send_sem=fin_s.at[c, o],
            recv_sem=fin_r.at[c, o],
            device_id=(before, z * group + mates[o]),
            device_id_type=MESH,
        )

    unpack_copy = pltpu.make_async_remote_copy(
        src_ref=unpack_ref, dst_ref=unpack_in, send_sem=un_s, recv_sem=un_r,
        device_id=(before, me), device_id_type=MESH,
    )
    unpack_copy.start()

    def hand_out(c):
        for a in range(4):
            load(c, a).wait()
            packed[c, a] = dot_nn(pack_ref[...], loaded[c, a]).astype(jnp.bfloat16)
        for o in range(1, group):
            a2a(c, o, j).start()
        own = pl.ds(pl.multiple_of(j * rows, 16), rows)
        for a in range(4):
            win[c, a, own, :] = packed[c, a, own, :]
            win[c, a, 224:256, :] = jnp.zeros((32, CHUNK), jnp.bfloat16)

    @pl.loop(0, 2)
    def _(c):
        hand_out(c)

    slots, kept, foreign = boundary_plan(ids_ref, blocks, planes, z, j)
    pick_ref[...] = one_hot(slots, 0, (96, 128))
    place_ref[...] = one_hot(upright(slots), 1, (128, 96))
    id_row = jnp.concatenate([kept, foreign], axis=1)
    id_col = jnp.concatenate([upright(kept), upright(foreign)], axis=0)
    id_col = id_col[0:224]
    bias[...] = jnp.where((id_col == id_row) & (id_row >= 0), 0.0, NEG)
    valid[...] = jnp.where(id_col >= 0, 1.0, 0.0)
    scale = HEAD_DIM ** (-0.5)

    def spread(c):
        for o in range(1, group):
            a2a(c, o, sources[o]).wait_recv()
        picked = [
            dot_nn(pick_ref[...], win[c, a, 0:128, :]).reshape(GROUPS, 8, CHUNK) for a in range(4)
        ]
        for a in (0, 2):
            pair = jnp.concatenate(picked[a : a + 2], axis=1)
            halo[c, :, a * 8 : a * 8 + 16, :] = pair.astype(jnp.bfloat16)
        outward_sends(c, start)

    def attend(c):
        outward_arrivals(c)
        for a in (0, 2):
            pair = halo_in[c, :, a * 8 : a * 8 + 16, :].astype(jnp.float32)
            for n in range(2):
                cells = pair[:, n * 8 : n * 8 + 8].reshape(GROUPS * 8, CHUNK)
                win[c, a + n, 128:224, :] = cells.astype(jnp.bfloat16)
        foreign = []
        for h in range(CHUNK // HEAD_DIM):
            head = slice(h * HEAD_DIM, (h + 1) * HEAD_DIM)
            q, g = [win[c, a, 0:224, head] for a in (0, 3)]
            k, v = [win[c, a, :, head] for a in (1, 2)]
            s = dot_nt(q, k) * (scale * LOG2_E) + bias[...]
            e = jnp.exp2(s - jnp.max(s, axis=1, keepdims=True))
            p = e * (valid[...] / jnp.sum(e, axis=1, keepdims=True))
            low = p.astype(jnp.bfloat16)
            dp = dot_nt(g, v)
            delta = jnp.sum(low.astype(jnp.float32) * dp, axis=1, keepdims=True)
            ds = (p * (dp - delta) * scale).astype(jnp.bfloat16)
            for a, grad in enumerate((dot_nn(ds, k), dot_tn(ds, q), dot_tn(low, g))):
                fin_out[c, a, :, head] = grad[0:128].astype(jnp.bfloat16)
                foreign.append(grad[128:224].reshape(GROUPS, 8, HEAD_DIM))
                if len(foreign) % 2 == 0:
                    pair = jnp.concatenate(foreign[-2:], axis=1)
                    last = len(foreign) * 8
                    back_out[c, :, last - 16 : last, :] = pair.astype(jnp.bfloat16)
        homeward_sends(c, start)

    def hand_on(c):
        homeward_arrivals(c)
        foreign = []
        for n in range(0, 3 * CHUNK // HEAD_DIM, 2):
            pair = back_in[c, :, n * 8 : n * 8 + 16, :].astype(jnp.float32)
            for i in range(2):
                foreign.append(pair[:, i * 8 : i * 8 + 8].reshape(GROUPS * 8, HEAD_DIM))
        for a in range(3):
            returned = dot_nn(place_ref[...], jnp.concatenate(foreign[a::3], axis=1).astype(jnp.bfloat16))
            fin_out[c, a] = (fin_out[c, a].astype(jnp.float32) + returned).astype(jnp.bfloat16)
        for o in range(group):
            final(c, o, j).start()

    def written(c, a):
        return pltpu.make_async_copy(
            placed.at[c, a], out_ref.at[0, :, columns(a * width + c * CHUNK)], put_s.at[c, a]
        )

    def finish(c):
        @pl.when(c == 0)
        def _():
            unpack_copy.wait_recv()

        for o in range(group):
            final(c, o, sources[o]).wait_recv()
        for a in range(3):
            placed[c, a] = dot_nn(unpack_in[...], fin_in[c, a]).astype(jnp.bfloat16)
            written(c, a).start()

    stages = (spread, attend, hand_on, finish, hand_out)
    lead = (2, 4, 6, 8, 0)

    @pl.loop(2, chunks + max(lead))
    def _(step):
        for late, stage in zip(lead, stages):

            @pl.when((step >= late) & (step < chunks + late))
            def _():
                stage(step - late)

    unpack_copy.wait_send()

    @pl.loop(0, chunks)
    def _(c):
        for o in range(1, group):
            a2a(c, o, j).wait_send()
        outward_sends(c, gone)
        homeward_sends(c, gone)
        for o in range(group):
            final(c, o, j).wait_send()
        for a in range(3):
            written(c, a).wait()


def hand_over(from_ref, to_ref, held, in_s, out_s):
    def part(n, inward):
        rows = pl.ds(n * 16, 16)
        if inward:
            return pltpu.make_async_copy(from_ref.at[:, rows], held.at[:, rows], in_s.at[n])
        return pltpu.make_async_copy(held.at[:, rows], to_ref.at[:, rows], out_s.at[n])

    for n in range(8):
        part(n, True).start()
    for n in range(8):
        part(n, True).wait()
        part(n, False).start()
    for n in range(8):
        part(n, False).wait()


def fused_body(sections, queries, key_cells, value_cells, grad_cells, packing, segment_ids):
    cell_count, width = queries.shape[1:]
    devices = lax.axis_size("dp")
    group = devices // 4
    planes = devices // group
    chunks = width // CHUNK
    vmem = pl.BlockSpec(memory_space=pltpu.VMEM)
    far = pl.BlockSpec(memory_space=pl.ANY)
    bf16 = jnp.bfloat16
    sem = pltpu.SemaphoreType.DMA
    result = pl.pallas_call(
        functools.partial(kernel, group, planes, sections, chunks, width),
        out_shape=jax.ShapeDtypeStruct((1, cell_count, 3 * width), bf16),
        in_specs=[far] * 4 + [vmem] * 2,
        out_specs=far,
        scratch_shapes=[
            pltpu.VMEM((chunks, 4, 128, CHUNK), bf16),
            pltpu.VMEM((chunks, 4, 128, CHUNK), bf16),
            pltpu.VMEM((chunks, 4, 256, CHUNK), bf16),
            pltpu.VMEM((chunks, GROUPS, 32, CHUNK), bf16),
            pltpu.VMEM((chunks, GROUPS, 32, CHUNK), bf16),
            pltpu.VMEM((chunks, GROUPS, 24 * CHUNK // HEAD_DIM, HEAD_DIM), bf16),
            pltpu.VMEM((chunks, GROUPS, 24 * CHUNK // HEAD_DIM, HEAD_DIM), bf16),
            pltpu.VMEM((chunks, 3, 128, CHUNK), bf16),
            pltpu.VMEM((chunks, 3, 128, CHUNK), bf16),
            pltpu.VMEM((128, 128), bf16),
            pltpu.VMEM((chunks, 3, 128, CHUNK), bf16),
            pltpu.VMEM((224, 256), jnp.float32),
            pltpu.VMEM((224, 1), jnp.float32),
            pltpu.VMEM((128, 128), bf16),
            pltpu.VMEM((128, 128), bf16),
            pltpu.VMEM((96, 128), bf16),
            pltpu.VMEM((128, 96), bf16),
            pltpu.VMEM((segment_ids.shape[1] // 128 + 8, 128), jnp.int32),
            sem((chunks, 4)),
            sem((chunks, group - 1)), sem((chunks, group - 1)),
            sem((chunks, 4)), sem((chunks, 4)),
            sem((chunks, 4)), sem((chunks, 4)),
            sem((chunks, group)), sem((chunks, group)),
            sem, sem, sem((chunks, 3)),
        ],
        compiler_params=pltpu.CompilerParams(
            collective_id=0, has_side_effects=True, vmem_limit_bytes=60 * 1024 * 1024
        ),
    )(queries, key_cells, value_cells, grad_cells, packing, segment_ids)
    return pl.pallas_call(
        hand_over,
        out_shape=jax.ShapeDtypeStruct(result.shape, bf16),
        in_specs=[far],
        out_specs=far,
        scratch_shapes=[pltpu.VMEM(result.shape, bf16), sem((8,)), sem((8,))],
        compiler_params=pltpu.CompilerParams(vmem_limit_bytes=60 * 1024 * 1024),
    )(result)


def solution(mesh):
    sections, devices = mesh.shape["section"], mesh.shape["dp"]

    def body_of(queries, *rest):
        fits = queries.shape[1] == 128 and queries.shape[2] % CHUNK == 0 and devices == 16
        if fits:
            return fused_body(sections, queries, *rest)
        return body(queries, *rest)

    return jax.shard_map(
        body_of,
        mesh=mesh,
        in_specs=(
            P("section", "dp", None),
            P("section", "dp", None),
            P("section", "dp", None),
            P("section", "dp", None),
            P("section", "dp", None),
            P("section", None),
        ),
        out_specs=P("section", "dp", None),
        check_vma=False,
    )
```
